32 devices in a mesh: sp: 8 (over z, y), tp: 4 (over x, core).
Axes of the slice: x: 2, y: 2, z: 4, core: 2. Of those that a mesh axis runs over, the one named last changes fastest.
Arguments:
- inputs: bfloat16 [25088, 1024], P(('sp', 'tp')), may hold values from -100 to 100, as said below
- grad_out: bfloat16 [25088, 512], P(('sp', 'tp')), may hold values from -6 to 6
- window_valid: int32 [512], P('sp'), may hold values 0 or 1
- window_edge: int32 [512], P('sp'), may hold values from 0 to 3
- merge_gain: bfloat16 [1024], replicated, may hold values from 0.5 to 1.5
- merge_bias: bfloat16 [1024], replicated, may hold values from -1.75 to 1.75
- merge_weight: bfloat16 [1024, 512], P(None, 'tp'), may hold values from -0.1875 to 0.1875
- attn_gain: bfloat16 [512], replicated, may hold values from 0.5 to 1.5
- attn_bias: bfloat16 [512], replicated, may hold values from -1.75 to 1.75
- query_key_value_weight: bfloat16 [512, 3, 512], P(None, None, 'tp'), may hold values from -0.25 to 0.25
- qv_bias: bfloat16 [2, 512], P(None, 'tp'), may hold values from -1.75 to 1.75
- rel_table: bfloat16 [169, 16], P(None, 'tp'), may hold values from -6 to 6
- proj_weight: bfloat16 [512, 512], P('tp'), may hold values from -0.75 to 0.75
- proj_bias: bfloat16 [512], replicated, may hold values from -1.75 to 1.75
- mlp_gain: bfloat16 [512], replicated, may hold values from 0.5 to 1.5
- mlp_bias: bfloat16 [512], replicated, may hold values from -1.75 to 1.75
- up_weight: bfloat16 [512, 2048], P(None, 'tp'), may hold values from -0.25 to 0.25
- up_bias: bfloat16 [2048], P('tp'), may hold values from -1.75 to 1.75
- down_weight: bfloat16 [2048, 512], P('tp'), may hold values from -0.125 to 0.125
- down_bias: bfloat16 [512], replicated, may hold values from -1.75 to 1.75
Outputs:
- block_out: bfloat16 [25088, 512], P(('sp', 'tp'))
- grad_inputs: float32 [25088, 1024], P(('sp', 'tp'))
- grad_merge_gain: float32 [1024], replicated
- grad_merge_bias: float32 [1024], replicated
- grad_merge_weight: float32 [1024, 512], P(None, 'tp')
- grad_attn_gain: float32 [512], replicated
- grad_attn_bias: float32 [512], replicated
- grad_qkv_weight: float32 [512, 3, 512], P(None, None, 'tp')
- grad_qv_bias: float32 [2, 512], P(None, 'tp')
- grad_rel_table: float32 [169, 16], P(None, 'tp')
- grad_proj_weight: float32 [512, 512], P('tp')
- grad_proj_bias: float32 [512], replicated
- grad_mlp_gain: float32 [512], replicated
- grad_mlp_bias: float32 [512], replicated
- grad_up_weight: float32 [512, 2048], P(None, 'tp')
- grad_up_bias: float32 [2048], P('tp')
- grad_down_weight: float32 [2048, 512], P('tp')
- grad_down_bias: float32 [512], replicated
The draws below stay inside these ranges and needn't reach their ends.
Inputs may be any that keep to these rules, and one draw needn't show every extreme that they name: `inputs`: section-2 features; each feature has its own scale and each token its own. `window_edge`: bit 0 set: the window's last three columns come from the page's other side under the shift; bit 1: the same for its last three rows. `window_valid`: 0 marks a window of a padded page area.
All inputs are finite; a program needn't handle non-finite values. No bound on the sum of `window_valid` on one device may be relied on, other than what follows from the above.
Results may differ from the reference program's by a relative error of at most 0.02.
Values may be sent and summed in bfloat16 or wider, within the bound.
A program may use at most 128 MiB of HBM per device.

```python
import math
import jax
import jax.numpy as jnp
from jax import lax

D = 512
DIN = 1024
HEADS = 16
HD = 32
FF = 2048
SIDE = 7
REL = 169
WINDOWS = 512
TOKENS = 25088
N_SP = 8


def draw_inputs(key, part):
    key = jax.random.fold_in(key, 11)
    key_main, key_rows, key_cols = jax.random.split(key, 3)
    col_scale = jnp.exp(jax.random.uniform(key_cols, (1, DIN), jnp.float32, math.log(0.3), math.log(3.0)))
    row_scale = jnp.exp(jax.random.uniform(key_rows, (TOKENS, 1), jnp.float32, math.log(0.5), math.log(5.0)))
    values = jax.random.normal(key_main, (TOKENS, DIN), jnp.float32) * col_scale * row_scale
    return jnp.clip(values, -100.0, 100.0).astype(jnp.bfloat16)


def touch_ends(array, own_key, least, largest):
    dims = array.shape
    spot = [jax.random.randint(jax.random.fold_in(own_key, axis), (), 0, dims[axis]) for axis in range(len(dims))]
    array = array.at[tuple(spot)].set(least)
    longest = dims.index(max(dims))
    spot[longest] = (spot[longest] + 1) % dims[longest]
    return array.at[tuple(spot)].set(largest)


def level_of(rng, dims, cuts, smallest, high):
    loudness, own = 1.0, jax.random.fold_in(rng, 6)
    for dim, shards_of in cuts:
        draws = jnp.exp(jax.random.uniform(jax.random.fold_in(own, dim), (shards_of,), jnp.float32, smallest / len(cuts), high / len(cuts)))
        loudness = loudness * jnp.repeat(draws, dims[dim] // shards_of).reshape([-1 if axis == dim else 1 for axis in range(len(dims))])
    return loudness


def bell_draw(key, shape, deviation, bound, cuts=(), kind=jnp.bfloat16):
    values = deviation * jax.random.normal(key, shape, jnp.float32)
    if cuts:
        values = values * level_of(key, shape, cuts, -0.22, 0.18)
    return jnp.clip(values, -bound, bound).astype(kind)


def setup_inputs(seed: int = 0) -> dict:
    splits = jax.random.split(jax.random.key(seed), 21)
    inputs = draw_inputs(jax.random.fold_in(splits[20], 71), 0)
    grad_out = bell_draw(splits[1], (TOKENS, D), 1.0, 6.0, ((0, 32),))
    window_valid = touch_ends((jax.random.randint(splits[2], (WINDOWS,), 0, 4) < 3).astype(jnp.int32), jax.random.fold_in(splits[2], 1), 0, 1)
    window_edge = touch_ends(jax.random.randint(splits[3], (WINDOWS,), 0, 4), jax.random.fold_in(splits[3], 1), 0, 3).astype(jnp.int32)
    merge_gain = jnp.clip(1.0 + 0.1 * jax.random.normal(splits[4], (DIN,), jnp.float32), 0.5, 1.5).astype(jnp.bfloat16)
    merge_bias = bell_draw(splits[5], (DIN,), 0.3, 1.75)
    merge_weight = bell_draw(splits[6], (DIN, D), DIN ** -0.5, 0.1875, ((1, 4),))
    attn_gain = jnp.clip(1.0 + 0.1 * jax.random.normal(splits[7], (D,), jnp.float32), 0.5, 1.5).astype(jnp.bfloat16)
    attn_bias = bell_draw(splits[8], (D,), 0.3, 1.75)
    query_key_value_weight = bell_draw(splits[9], (D, 3, D), D ** -0.5, 0.25, ((2, 4),))
    qv_bias = bell_draw(splits[10], (2, D), 0.3, 1.75, ((1, 4),))
    rel_table = bell_draw(splits[11], (REL, HEADS), 1.0, 6.0, ((1, 4),))
    proj_weight = bell_draw(splits[12], (D, D), (D // 8) ** -0.5, 0.75, ((0, 4),))
    proj_bias = bell_draw(splits[13], (D,), 0.3, 1.75)
    mlp_gain = jnp.clip(1.0 + 0.1 * jax.random.normal(splits[14], (D,), jnp.float32), 0.5, 1.5).astype(jnp.bfloat16)
    mlp_bias = bell_draw(splits[15], (D,), 0.3, 1.75)
    up_weight = bell_draw(splits[16], (D, FF), D ** -0.5, 0.25, ((1, 4),))
    up_bias = bell_draw(splits[17], (FF,), 0.3, 1.75, ((0, 4),))
    down_weight = bell_draw(splits[18], (FF, D), FF ** -0.5, 0.125, ((0, 4),))
    down_bias = bell_draw(splits[19], (D,), 0.3, 1.75)
    return dict(inputs=inputs, grad_out=grad_out, window_valid=window_valid, window_edge=window_edge, merge_gain=merge_gain, merge_bias=merge_bias, merge_weight=merge_weight, attn_gain=attn_gain, attn_bias=attn_bias, query_key_value_weight=query_key_value_weight, qv_bias=qv_bias, rel_table=rel_table, proj_weight=proj_weight, proj_bias=proj_bias, mlp_gain=mlp_gain, mlp_bias=mlp_bias, up_weight=up_weight, up_bias=up_bias, down_weight=down_weight, down_bias=down_bias)


EPSILON = 1e-05
NEG_FILL = -1000000000.0
FULL_PRECISION = lax.Precision.HIGHEST

@jax.custom_vjp
def low(v):
    return lax.optimization_barrier(v.astype(jnp.bfloat16)).astype(jnp.float32)

@jax.custom_vjp
def low_back(v):
    return v

def low_keep(v):
    return (low(v), None)

def low_pass(kept, grad):
    return (grad,)

def back_keep(v):
    return (v, None)

def back_low(kept, grad):
    return (low(grad),)
low.defvjp(low_keep, low_pass)
low_back.defvjp(back_keep, back_low)

def layer_norm(values, gain_vec, shift_term):
    row_mean = lax.optimization_barrier(jnp.mean(values, -1, keepdims=True))
    centred = values - row_mean
    variance = lax.optimization_barrier(jnp.mean(centred * centred, -1, keepdims=True))
    return centred * lax.rsqrt(variance + EPSILON) * gain_vec + shift_term

def product(left_side, right_side):
    return jnp.dot(left_side, right_side, precision=FULL_PRECISION)

def window_layout(edge_ids):
    position = jnp.arange(SIDE * SIDE, dtype=jnp.int32)
    row_of = position // SIDE
    col_of = position % SIDE
    rel_index = (row_of[:, None] - row_of[None, :] + SIDE - 1) * (2 * SIDE - 1) + (col_of[:, None] - col_of[None, :] + SIDE - 1)
    shift_size = SIDE // 2
    col_high = (col_of >= SIDE - shift_size).astype(jnp.int32)
    row_high = (row_of >= SIDE - shift_size).astype(jnp.int32)
    region = (edge_ids % 2)[:, None] * col_high[None, :] + 2 * (edge_ids // 2)[:, None] * row_high[None, :]
    allowed = region[:, :, None] == region[:, None, :]
    return (rel_index, allowed)

def reference(inputs, grad_out, window_valid, window_edge, merge_gain, merge_bias, merge_weight, attn_gain, attn_bias, query_key_value_weight, qv_bias, rel_table, proj_weight, proj_bias, mlp_gain, mlp_bias, up_weight, up_bias, down_weight, down_bias):
    rel_index, allowed = window_layout(window_edge)
    valid_rows = jnp.repeat(window_valid.astype(jnp.float32), SIDE * SIDE)[:, None]
    groups = N_SP
    factor = HD ** (-0.5)
    allowed_groups = allowed.reshape((groups, -1) + allowed.shape[1:])

    def forward(inputs, merge_gain, merge_bias, merge_weight, attn_gain, attn_bias, query_key_value_weight, qv_bias, rel_table, proj_weight, proj_bias, mlp_gain, mlp_bias, up_weight, up_bias, down_weight, down_bias):
        merged = low(layer_norm(inputs, merge_gain, merge_bias))
        section_out = low_back(low(product(merged, merge_weight)))
        attention_input = low(layer_norm(section_out, attn_gain, attn_bias))
        projected_rows = jnp.einsum('tv,vfq->tfq', attention_input, query_key_value_weight, precision=FULL_PRECISION)
        queries = low_back(low(projected_rows[:, 0] + qv_bias[0]))
        key_rows = low_back(low(projected_rows[:, 1]))
        value_rows = low_back(low(projected_rows[:, 2] + qv_bias[1]))
        bias_heads = jnp.transpose(rel_table[rel_index], (2, 0, 1))
        win_shape = (groups, -1, SIDE * SIDE, HEADS, HD)

        def attend(pieces):
            query_win, key_win, value_win, allowed_win = pieces
            logits = jnp.einsum('wihd,wjhd->whij', query_win, key_win, precision=FULL_PRECISION) * factor + bias_heads[None]
            logits = low_back(jnp.where(allowed_win[:, None], logits, NEG_FILL))
            row_top = lax.optimization_barrier(jnp.max(logits, -1, keepdims=True))
            exp_terms = jnp.exp(logits - row_top)
            attn_probs = low(exp_terms / lax.optimization_barrier(jnp.sum(exp_terms, -1, keepdims=True)))
            return jnp.einsum('whij,wjhd->wihd', attn_probs, value_win, precision=FULL_PRECISION)
        attended = lax.map(jax.checkpoint(attend), (queries.reshape(win_shape), key_rows.reshape(win_shape), value_rows.reshape(win_shape), allowed_groups))
        attended = low_back(low(attended.reshape(queries.shape)))
        attn_out = low_back(product(attended, proj_weight))
        residual = section_out + attn_out + proj_bias
        mlp_in = low(layer_norm(residual, mlp_gain, mlp_bias))
        pre_act = low_back(product(mlp_in, up_weight) + up_bias)
        hidden = low(jax.nn.gelu(pre_act, approximate=False))
        mlp_out = low_back(product(hidden, down_weight))
        return (residual + mlp_out + down_bias) * valid_rows
    floats = tuple((argument.astype(jnp.float32) for argument in (inputs, merge_gain, merge_bias, merge_weight, attn_gain, attn_bias, query_key_value_weight, qv_bias, rel_table, proj_weight, proj_bias, mlp_gain, mlp_bias, up_weight, up_bias, down_weight, down_bias)))
    output, pullback = jax.vjp(forward, *floats)
    gradients = pullback(grad_out.astype(jnp.float32))
    return (output.astype(jnp.bfloat16), gradients[0], gradients[1], gradients[2], gradients[3], gradients[4], gradients[5], gradients[6], gradients[7], gradients[8], gradients[9], gradients[10], gradients[11], gradients[12], gradients[13], gradients[14], gradients[15], gradients[16])
```

```python
from functools import partial

import jax
import jax.numpy as jnp
from jax import lax
from jax.sharding import PartitionSpec as P

SIDE = 7


EPSILON = 1e-05
NEG_FILL = -1000000000.0
FULL_PRECISION = lax.Precision.HIGHEST


def norm_forward(values, gain_vec, shift_term):
    row_mean = jnp.mean(values, -1, keepdims=True)
    centred = values - row_mean
    variance = jnp.mean(centred * centred, -1, keepdims=True)
    inv_std = lax.rsqrt(variance + EPSILON)
    normed = centred * inv_std
    return (normed * gain_vec + shift_term, normed, inv_std)


def norm_backward(upstream, normed, inv_std, gain_vec):
    scaled = upstream * gain_vec
    result = (
        scaled
        - jnp.mean(scaled, -1, keepdims=True)
        - normed * jnp.mean(scaled * normed, -1, keepdims=True)
    )
    return (result * inv_std, jnp.sum(upstream * normed, 0), jnp.sum(upstream, 0))


def contract_rows(left_side, right_side):
    return lax.dot_general(
        left_side, right_side, (((0,), (0,)), ((), ())), preferred_element_type=jnp.float32
    )


def contract_cols(left_side, right_side):
    return lax.dot_general(
        left_side, right_side, (((1,), (1,)), ((), ())), preferred_element_type=jnp.float32
    )


def window_tables(edge_ids):
    position = jnp.arange(SIDE * SIDE, dtype=jnp.int32)
    row_of = position // SIDE
    col_of = position % SIDE
    rel_index = (row_of[:, None] - row_of[None, :] + SIDE - 1) * (2 * SIDE - 1) + (
        col_of[:, None] - col_of[None, :] + SIDE - 1
    )
    onehot = (
        rel_index[:, :, None] == jnp.arange((2 * SIDE - 1) ** 2, dtype=jnp.int32)[None, None, :]
    ).astype(jnp.float32)
    shift_size = SIDE // 2
    col_high = (col_of >= SIDE - shift_size).astype(jnp.int32)
    row_high = (row_of >= SIDE - shift_size).astype(jnp.int32)
    region = (edge_ids % 2)[:, None] * col_high[None, :] + 2 * (edge_ids // 2)[:, None] * row_high[
        None, :
    ]
    allowed = region[:, :, None] == region[:, None, :]
    return (onehot, allowed)


def window_split(values, windows, head_count):
    return values.reshape(windows, SIDE * SIDE, head_count, -1)


def window_logits(queries, key_rows, bias_heads, allowed):
    windows, head_count = (allowed.shape[0], bias_heads.shape[0])
    query_win = window_split(queries, windows, head_count)
    key_win = window_split(key_rows, windows, head_count)
    factor = query_win.shape[-1] ** (-0.5)
    logits = (
        jnp.einsum("wihd,wjhd->whij", query_win, key_win, preferred_element_type=jnp.float32)
        * factor
        + bias_heads[None]
    )
    return jnp.where(allowed[:, None], logits, NEG_FILL)


def attend_forward(queries, key_rows, value_rows, bias_heads, allowed):
    windows, head_count = (allowed.shape[0], bias_heads.shape[0])
    logits = window_logits(queries, key_rows, bias_heads, allowed)
    row_top = jnp.max(logits, -1, keepdims=True)
    exp_terms = jnp.exp(logits - row_top)
    row_total = jnp.sum(exp_terms, -1, keepdims=True)
    attn_probs = (exp_terms / row_total).astype(jnp.bfloat16)
    attended = jnp.einsum(
        "whij,wjhd->wihd",
        attn_probs,
        window_split(value_rows, windows, head_count),
        preferred_element_type=jnp.float32,
    )
    return (attended.reshape(queries.shape).astype(jnp.bfloat16), row_top + jnp.log(row_total))


def attend_backward(d_attended, queries, key_rows, value_rows, bias_heads, allowed, log_total):
    windows, head_count = (allowed.shape[0], bias_heads.shape[0])
    logits = window_logits(queries, key_rows, bias_heads, allowed)
    attn_probs = jnp.exp(logits - log_total)
    d_win = window_split(d_attended, windows, head_count)
    query_win = window_split(queries, windows, head_count)
    key_win = window_split(key_rows, windows, head_count)
    value_win = window_split(value_rows, windows, head_count)
    d_probs = jnp.einsum("wihd,wjhd->whij", d_win, value_win, preferred_element_type=jnp.float32)
    d_values = jnp.einsum(
        "whij,wihd->wjhd",
        attn_probs.astype(jnp.bfloat16),
        d_win,
        preferred_element_type=jnp.float32,
    )
    d_logits = (attn_probs * (d_probs - jnp.sum(d_probs * attn_probs, -1, keepdims=True))).astype(
        jnp.bfloat16
    )
    factor = query_win.shape[-1] ** (-0.5)
    d_queries = (
        jnp.einsum("whij,wjhd->wihd", d_logits, key_win, preferred_element_type=jnp.float32)
        * factor
    )
    d_keys = (
        jnp.einsum("whij,wihd->wjhd", d_logits, query_win, preferred_element_type=jnp.float32)
        * factor
    )
    d_bias = jnp.sum(d_logits.astype(jnp.float32), 0)
    flat_shape = queries.shape
    return (
        d_queries.reshape(flat_shape).astype(jnp.bfloat16),
        d_keys.reshape(flat_shape).astype(jnp.bfloat16),
        d_values.reshape(flat_shape).astype(jnp.bfloat16),
        d_bias,
    )


def on_device(
    inputs,
    grad_out,
    window_valid,
    window_edge,
    merge_gain,
    merge_bias,
    merge_weight,
    attn_gain,
    attn_bias,
    query_key_value_weight,
    qv_bias,
    rel_table,
    proj_weight,
    proj_bias,
    mlp_gain,
    mlp_bias,
    up_weight,
    up_bias,
    down_weight,
    down_bias,
):
    row_count = inputs.shape[0]
    windows = row_count // (SIDE * SIDE)
    tp_index = lax.axis_index("tp")
    valid_mine = lax.dynamic_slice_in_dim(window_valid, tp_index * windows, windows, 0)
    keep_rows = jnp.repeat(valid_mine.astype(jnp.float32), SIDE * SIDE)[:, None]
    gather_last = lambda block: lax.all_gather(block, "tp", axis=block.ndim - 1, tiled=True)
    gather_first = lambda block: lax.all_gather(block, "tp", axis=0, tiled=True)
    merge_all = gather_last(merge_weight)
    qkv_all = gather_last(query_key_value_weight)
    qv_all = gather_last(qv_bias)
    table_all = gather_last(rel_table)
    proj_all = gather_first(proj_weight)
    up_all = gather_last(up_weight)
    up_bias_all = gather_first(up_bias)
    down_all = gather_first(down_weight)
    edge_mine = lax.dynamic_slice_in_dim(window_edge, tp_index * windows, windows, 0)
    merge_gain_f = merge_gain.astype(jnp.float32)
    merged, merge_hat, merge_inv = norm_forward(
        inputs.astype(jnp.float32), merge_gain_f, merge_bias.astype(jnp.float32)
    )
    merged = merged.astype(jnp.bfloat16)
    section_out = jnp.dot(merged, merge_all, preferred_element_type=jnp.float32).astype(
        jnp.bfloat16
    )
    section_float = section_out.astype(jnp.float32)
    attn_gain_f = attn_gain.astype(jnp.float32)
    attn_normed, attn_hat, attn_inv = norm_forward(
        section_float, attn_gain_f, attn_bias.astype(jnp.float32)
    )
    attention_input = attn_normed.astype(jnp.bfloat16)
    projected_rows = jnp.einsum(
        "tv,vfq->tfq", attention_input, qkv_all, preferred_element_type=jnp.float32
    )
    queries = (projected_rows[:, 0] + qv_all[0].astype(jnp.float32)).astype(jnp.bfloat16)
    key_rows = projected_rows[:, 1].astype(jnp.bfloat16)
    value_rows = (projected_rows[:, 2] + qv_all[1].astype(jnp.float32)).astype(jnp.bfloat16)
    onehot, allowed = window_tables(edge_mine)
    bias_heads = jnp.einsum(
        "ijr,rh->hij", onehot, table_all.astype(jnp.float32), precision=FULL_PRECISION
    )
    attended, log_total = attend_forward(queries, key_rows, value_rows, bias_heads, allowed)
    attn_out = jnp.dot(attended, proj_all, preferred_element_type=jnp.float32)
    residual = section_float + attn_out + proj_bias.astype(jnp.float32)
    mlp_gain_f = mlp_gain.astype(jnp.float32)
    mlp_normed, mlp_hat, mlp_inv = norm_forward(residual, mlp_gain_f, mlp_bias.astype(jnp.float32))
    mlp_in = mlp_normed.astype(jnp.bfloat16)
    pre_act = jnp.dot(mlp_in, up_all, preferred_element_type=jnp.float32) + up_bias_all.astype(
        jnp.float32
    )
    hidden_float, gelu_pullback = jax.vjp(partial(jax.nn.gelu, approximate=False), pre_act)
    hidden = hidden_float.astype(jnp.bfloat16)
    mlp_out = jnp.dot(hidden, down_all, preferred_element_type=jnp.float32)
    block_out = ((residual + mlp_out + down_bias.astype(jnp.float32)) * keep_rows).astype(
        jnp.bfloat16
    )
    scatter_last = lambda grad: lax.psum(
        lax.psum_scatter(
            grad.astype(jnp.bfloat16), "tp", scatter_dimension=grad.ndim - 1, tiled=True
        ),
        "sp",
    ).astype(jnp.float32)
    scatter_first = lambda grad: lax.psum(
        lax.psum_scatter(grad.astype(jnp.bfloat16), "tp", scatter_dimension=0, tiled=True),
        "sp",
    ).astype(jnp.float32)
    d_out = grad_out.astype(jnp.float32) * keep_rows
    d_down_bias = jnp.sum(d_out, 0)
    d_mlp = d_out.astype(jnp.bfloat16)
    d_hidden = contract_cols(d_mlp, down_all)
    d_down_weight = scatter_first(contract_rows(hidden, d_mlp))
    d_pre = gelu_pullback(d_hidden)[0].astype(jnp.bfloat16)
    d_up_bias = jnp.sum(d_pre.astype(jnp.float32), 0)
    d_up_weight = scatter_last(contract_rows(mlp_in, d_pre))
    d_mlp_in = contract_cols(d_pre, up_all)
    d_mlp_norm, d_mlp_gain, d_mlp_bias = norm_backward(d_mlp_in, mlp_hat, mlp_inv, mlp_gain_f)
    d_residual = d_out + d_mlp_norm
    d_proj_bias = jnp.sum(d_residual, 0)
    d_attn = d_residual.astype(jnp.bfloat16)
    d_attended = contract_cols(d_attn, proj_all).astype(jnp.bfloat16)
    d_proj_weight = scatter_first(contract_rows(attended, d_attn))
    d_queries, d_keys, d_values, d_bias = attend_backward(
        d_attended, queries, key_rows, value_rows, bias_heads, allowed, log_total
    )
    d_rel_table = jnp.einsum("ijr,hij->rh", onehot, d_bias, precision=FULL_PRECISION)
    d_qv_bias = jnp.stack(
        [jnp.sum(d_queries.astype(jnp.float32), 0), jnp.sum(d_values.astype(jnp.float32), 0)]
    )
    projected_gradient = jnp.stack([d_queries, d_keys, d_values], axis=1)
    d_qkv_weight = scatter_last(
        jnp.einsum(
            "pi,pyt->iyt", attention_input, projected_gradient, preferred_element_type=jnp.float32
        )
    )
    d_attn_in = jnp.einsum(
        "qut,xut->qx", projected_gradient, qkv_all, preferred_element_type=jnp.float32
    )
    d_attn_norm, d_attn_gain, d_attn_bias = norm_backward(
        d_attn_in, attn_hat, attn_inv, attn_gain_f
    )
    d_section = (d_residual + d_attn_norm).astype(jnp.bfloat16)
    d_merge_weight = scatter_last(contract_rows(merged, d_section))
    d_merged = contract_cols(d_section, merge_all)
    d_inputs, d_merge_gain, d_merge_bias = norm_backward(
        d_merged, merge_hat, merge_inv, merge_gain_f
    )
    sums = lax.psum(
        (
            d_merge_gain,
            d_merge_bias,
            d_attn_gain,
            d_attn_bias,
            d_proj_bias,
            d_mlp_gain,
            d_mlp_bias,
            d_down_bias,
            d_qv_bias,
            d_rel_table,
            d_up_bias,
        ),
        ("sp", "tp"),
    )
    mine_last = lambda whole: lax.dynamic_slice_in_dim(
        whole,
        tp_index * (whole.shape[-1] // lax.axis_size("tp")),
        whole.shape[-1] // lax.axis_size("tp"),
        whole.ndim - 1,
    )
    return (
        block_out,
        d_inputs,
        sums[0],
        sums[1],
        d_merge_weight,
        sums[2],
        sums[3],
        d_qkv_weight,
        mine_last(sums[8]),
        mine_last(sums[9]),
        d_proj_weight,
        sums[4],
        sums[5],
        sums[6],
        d_up_weight,
        mine_last(sums[10]),
        d_down_weight,
        sums[7],
    )


def solution(mesh):
    placed = (
        P(("sp", "tp"), None),
        P(("sp", "tp"), None),
        P("sp"),
        P("sp"),
        P(),
        P(),
        P(None, "tp"),
        P(),
        P(),
        P(None, None, "tp"),
        P(None, "tp"),
        P(None, "tp"),
        P("tp", None),
        P(),
        P(),
        P(),
        P(None, "tp"),
        P("tp"),
        P("tp", None),
        P(),
    )
    return jax.shard_map(
        on_device,
        mesh=mesh,
        in_specs=placed,
        out_specs=(
            P(("sp", "tp"), None),
            P(("sp", "tp"), None),
            P(),
            P(),
            P(None, "tp"),
            P(),
            P(),
            P(None, None, "tp"),
            P(None, "tp"),
            P(None, "tp"),
            P("tp", None),
            P(),
            P(),
            P(),
            P(None, "tp"),
            P("tp"),
            P("tp", None),
            P(),
        ),
        check_vma=False,
    )
```

```python
import functools
import math

import jax
import jax.numpy as jnp
from jax import lax
from jax.experimental import pallas as pl
from jax.experimental.pallas import tpu as pltpu
from jax.sharding import PartitionSpec as P

SIDE = 7
TOK = SIDE * SIDE
REL_SIDE = 2 * SIDE - 1
REL = REL_SIDE * REL_SIDE
SPAN = 64
GROUP = 4
HD = 32
LANES = 128
EPSILON = 1e-05
NEG_FILL = -1000000000.0
MIB = 1 << 20
F32 = jnp.float32
BF16 = jnp.bfloat16


def dot(left, right):
    return jnp.dot(left, right, preferred_element_type=F32)


def dot_cols(left, right):
    return lax.dot_general(left, right, (((1,), (1,)), ((), ())), preferred_element_type=F32)


def dot_rows(left, right):
    return lax.dot_general(left, right, (((0,), (0,)), ((), ())), preferred_element_type=F32)


def rows_at(index, size):
    return pl.ds(pl.multiple_of(index * size, size), size)


def each(count, body, unroll=1):
    def step(index, carry):
        body(index)
        return carry

    lax.fori_loop(0, count, step, 0, unroll=unroll)


def fold(values):
    total = values[0:8]
    for start in range(8, values.shape[0], 8):
        total = total + values[start : start + 8]
    return total


def iota(shape, dim):
    return lax.broadcasted_iota(jnp.int32, shape, dim)


def norm_rows(values):
    mean = jnp.mean(values, -1, keepdims=True)
    centred = values - mean
    inv = lax.rsqrt(jnp.mean(centred * centred, -1, keepdims=True) + EPSILON)
    return centred * inv, mean, inv


def norm_back(upstream, normed, inv, gain):
    scaled = upstream * gain
    return inv * (
        scaled
        - jnp.mean(scaled, -1, keepdims=True)
        - normed * jnp.mean(scaled * normed, -1, keepdims=True)
    )


def gelu_both(values):
    size = jnp.abs(values) * 0.7071067811865476
    bell = jnp.exp(-size * size)
    t = 1.0 / (1.0 + 0.3275911 * size)
    poly = t * (
        0.254829592
        + t * (-0.284496736 + t * (1.421413741 + t * (-1.453152027 + t * 1.061405429)))
    )
    tail = 0.5 * poly * bell
    phi = jnp.where(values >= 0, 1.0 - tail, tail)
    return values * phi, phi + values * bell * 0.3989422804014327


def window_row_col(index):
    row = (index * 37) >> 8
    return row, index - SIDE * row


def region_ids(index, edge, outside):
    row, col = window_row_col(index)
    high = SIDE - SIDE // 2
    region = (edge & 1) * (col >= high).astype(jnp.int32) + 2 * (edge >> 1) * (
        row >= high
    ).astype(jnp.int32)
    return jnp.where((index >= 0) & (index < TOK), region, outside)


def head_masks():
    lane = iota((1, LANES), 1)
    return [((lane >> 5) == head).astype(F32).astype(BF16) for head in range(GROUP)]


def spread_heads(block, masks):
    return jnp.concatenate([block * mask for mask in masks], axis=0)


def pick_heads(product):
    lane = iota((SPAN, LANES), 1)
    result = product[3 * SPAN : 4 * SPAN]
    for head in (2, 1, 0):
        result = jnp.where(
            lane < (head + 1) * HD, product[head * SPAN : (head + 1) * SPAN], result
        )
    return result


def same_head(rows, columns):
    return (
        (iota((rows, columns), 0) // (rows // GROUP))
        == (iota((rows, columns), 1) // (columns // GROUP))
    ).astype(F32).astype(BF16)


def offset_select(half):
    place = iota((LANES, LANES), 0)
    lane = iota((LANES, LANES), 1)
    token = lane - half * SPAN
    row, col = window_row_col(token & (SPAN - 1))
    wanted = (SIDE - 1) * (REL_SIDE + 1) - (REL_SIDE * row + col)
    hit = (place == wanted) & (token >= 0) & (token < TOK)
    return hit.astype(F32).astype(BF16)


def build_bias(table, spread_ref, bias_ref):
    heads = table.shape[0]

    def one(index):
        row = index // SIDE
        shift = index + (SIDE - 1) * row
        rolled = pltpu.roll(table, (2 * LANES - shift) % (2 * LANES), 1)
        spread_ref[rows_at(index, heads), :] = rolled[:, :LANES]

    spread_ref[...] = jnp.zeros_like(spread_ref)
    for index in range(TOK):
        one(index)
    low, high = offset_select(0), offset_select(1)
    for pair in range(heads // 2):
        first = spread_ref[pl.ds(2 * pair, SPAN, stride=heads), :].astype(BF16)
        second = spread_ref[pl.ds(2 * pair + 1, SPAN, stride=heads), :].astype(BF16)
        bias_ref[:, pair * LANES : (pair + 1) * LANES] = dot(first, low) + dot(second, high)


def split_bf16(values):
    high = values.astype(BF16)
    return high, (values - high.astype(F32)).astype(BF16)


def reduce_bias(bias_ref, spread_ref, heads):
    low, high = offset_select(0), offset_select(1)
    for pair in range(heads // 2):
        parts = split_bf16(bias_ref[:, pair * LANES : (pair + 1) * LANES])
        spread_ref[pl.ds(2 * pair, SPAN, stride=heads), :] = sum(
            dot_cols(part, low) for part in parts
        )
        spread_ref[pl.ds(2 * pair + 1, SPAN, stride=heads), :] = sum(
            dot_cols(part, high) for part in parts
        )
    total = jnp.zeros((heads, 2 * LANES), F32)
    blank = jnp.zeros((heads, LANES), F32)
    for index in range(TOK):
        shift = index + (SIDE - 1) * (index // SIDE)
        row = jnp.concatenate([spread_ref[index * heads : (index + 1) * heads, :], blank], axis=1)
        total = total + (pltpu.roll(row, shift, 1) if shift else row)
    return total


def shift_both(ref, forward):
    rows, columns = ref.shape
    down, right = (1, 1) if forward else (rows - 1, columns - 1)
    ref[...] = pltpu.roll(pltpu.roll(ref[...], down, 0), right, 1)


def attention_forward(window, edge, qkv, bias_ref, probs_ref, att_ref):
    base = pl.ds(pl.multiple_of(window * (TOK - 1), 16), SPAN)
    masks = head_masks()
    ones = same_head(GROUP * SPAN, GROUP * SPAN)
    row_index = iota((SPAN, 1), 0) - window
    row_in = (row_index >= 0) & (row_index < TOK)
    row_region = region_ids(row_index, edge, 8)
    lane_region = region_ids((iota((1, GROUP * SPAN), 1) & (SPAN - 1)) - window, edge, 16)
    allowed = row_region == lane_region
    first_half = iota((SPAN, LANES), 1) < SPAN
    keep = row_in.astype(F32)
    groups = att_ref.shape[1] // LANES
    for group in range(groups):
        lanes = pl.ds(group * LANES, LANES)
        wide = pl.ds(group * GROUP * SPAN, GROUP * SPAN)
        query, key, value = (qkv[part, base, lanes] for part in range(3))
        logits = dot_cols(query, spread_heads(key, masks)) * (HD**-0.5) + bias_ref[:, wide]
        logits = jnp.where(allowed, logits, NEG_FILL)
        tops = []
        for half in range(GROUP * SPAN // LANES):
            piece = logits[:, half * LANES : (half + 1) * LANES]
            top_low = jnp.max(jnp.where(first_half, piece, 2 * NEG_FILL), -1, keepdims=True)
            top_high = jnp.max(jnp.where(first_half, 2 * NEG_FILL, piece), -1, keepdims=True)
            tops.append(jnp.where(first_half, top_low, top_high))
        terms = jnp.exp(logits - jnp.concatenate(tops, axis=1))
        totals = dot(terms.astype(BF16), ones)
        probs = (terms * (keep / totals)).astype(BF16)
        probs_ref[window, :, wide] = probs
        attended = dot(probs, spread_heads(value, masks))
        att_ref[base, lanes] = jnp.where(
            row_in, attended, att_ref[base, lanes].astype(F32)
        ).astype(BF16)


def attention_backward(window, qkv, d_att, probs_ref, d_bias_ref, d_qkv):
    base = pl.ds(pl.multiple_of(window * (TOK - 1), 16), SPAN)
    masks = head_masks()
    ones = same_head(GROUP * SPAN, GROUP * SPAN)
    row_index = iota((SPAN, 1), 0) - window
    row_in = (row_index >= 0) & (row_index < TOK)
    groups = d_att.shape[1] // LANES
    factor = HD**-0.5

    def put(part, lanes, values):
        d_qkv[part, base, lanes] = jnp.where(
            row_in, values, d_qkv[part, base, lanes].astype(F32)
        ).astype(BF16)

    for group in range(groups):
        lanes = pl.ds(group * LANES, LANES)
        wide = pl.ds(group * GROUP * SPAN, GROUP * SPAN)
        query, key, value = (qkv[part, base, lanes] for part in range(3))
        upstream = d_att[base, lanes]
        probs = probs_ref[window, :, wide]
        probs_wide = probs.astype(F32)
        d_probs = dot_cols(upstream, spread_heads(value, masks))
        weighted = d_probs * probs_wide
        delta = dot(weighted.astype(BF16), ones)
        d_logits = (weighted - probs_wide * delta).astype(BF16)
        d_bias_ref[:, wide] += d_logits.astype(F32)
        put(0, lanes, dot(d_logits, spread_heads(key, masks)) * factor)
        put(1, lanes, pick_heads(dot_rows(d_logits, query)) * factor)
        put(2, lanes, pick_heads(dot_rows(probs, upstream)))


def sum_rows(values):
    return jnp.sum(values, 0, keepdims=True)


class Local:
    def __init__(self, refs, first_window):
        self.__dict__.update(refs)
        self.first_window = first_window
        self.rows, self.wide = self.x.shape
        self.width = self.section.shape[1]
        self.units = self.hidden.shape[1]
        self.windows = self.rows // TOK
        self.heads = self.width // HD
        self.chunk = 16
        self.steps = self.rows // self.chunk
        self.tile = self.units // self.gu.shape[0]

    def gain(self, row, lanes):
        return self.gains[row : row + 1, :lanes]

    def stat(self, at, index):
        return self.stats[at, index : index + 1]

    def keep_stats(self, at, index, mean, inv):
        self.stats[at, index : index + 1] = mean
        self.stats[at, index + 1 : index + 2] = inv

    def prepare(self):
        def keep_rows(window):
            base = pl.ds(pl.multiple_of(window * (TOK - 1), 16), SPAN)
            index = iota((SPAN, 1), 0) - window
            inside = (index >= 0) & (index < TOK)
            valid = self.valid[self.first_window + window].astype(F32)
            self.stats[base, 6:7] = jnp.where(inside, valid, self.stats[base, 6:7])

        each(self.windows, keep_rows)

    def table_bias(self):
        build_bias(self.table(), self.spread, self.bias)

    def merge_norm(self):
        gain, shift = self.gain(0, self.wide), self.gain(1, self.wide)

        def step(index):
            at = rows_at(index, self.chunk)
            normed, mean, inv = norm_rows(self.x[at, :].astype(F32))
            self.merged[at, :] = (normed * gain + shift).astype(BF16)
            self.keep_stats(at, 0, mean, inv)

        each(self.steps, step, 7)

    def merge(self):
        self.section[...] = dot(self.merged[...], self.wm[...]).astype(BF16)

    def attn_norm(self):
        gain, shift = self.gain(2, self.width), self.gain(3, self.width)

        def step(index):
            at = rows_at(index, self.chunk)
            normed, mean, inv = norm_rows(self.section[at, :].astype(F32))
            self.attn_in[at, :] = (normed * gain + shift).astype(BF16)
            self.keep_stats(at, 2, mean, inv)

        each(self.steps, step, 7)

    def project(self):
        for part in range(3):
            product = dot(self.attn_in[...], self.wqkv[part])
            if part != 1:
                product = product + self.qkv_bias(part)
            self.qkv[part] = product.astype(BF16)

    def attend(self, first, last):
        def step(index):
            window = first + index
            edge = self.edge[self.first_window + window]
            attention_forward(window, edge, self.qkv, self.bias, self.probs, self.att)
            shift_both(self.bias, True)

        each(last - first, step)

    def attn_out(self):
        self.resid[...] = dot(self.att[...], self.wp[...])

    def mlp_norm(self):
        gain, shift = self.gain(4, self.width), self.gain(5, self.width)
        proj_bias = self.gain(6, self.width)

        def step(index):
            at = rows_at(index, self.chunk)
            total = self.section[at, :].astype(F32) + self.resid[at, :] + proj_bias
            self.resid[at, :] = total
            normed, mean, inv = norm_rows(total)
            self.mlp_in[at, :] = (normed * gain + shift).astype(BF16)
            self.keep_stats(at, 4, mean, inv)

        each(self.steps, step, 7)

    def up(self):
        def part(index):
            columns = rows_at(index, self.tile)
            self.pre[...] = dot(self.mlp_in[...], self.wu[:, columns])
            shift = self.up_bias(index)

            def activate(step):
                at = rows_at(step, self.chunk)
                value, rate = gelu_both(self.pre[at, :] + shift)
                self.hidden[at, columns] = value.astype(BF16)
                self.slope[at, columns] = rate.astype(BF16)

            each(self.steps, activate, 7)

        each(self.units // self.tile, part)

    def down(self):
        self.pre[...] = dot(self.hidden[...], self.wd[...])

    def finish(self):
        down_bias = self.gain(7, self.width)

        def step(index, total):
            at = rows_at(index, self.chunk)
            mask = self.stat(at, 6)
            block = (self.resid[at, :] + self.pre[at, :] + down_bias) * mask
            self.out[at, :] = block.astype(BF16)
            grad = self.grad_out[at, :].astype(F32) * mask
            self.d_mlp[at, :] = grad.astype(BF16)
            return total + fold(grad)

        total = lax.fori_loop(
            0, self.steps, step, jnp.zeros((8, self.width), F32), unroll=7
        )
        self.put_sum(7, total)

    def down_back(self, index):
        columns = rows_at(index, self.tile)
        self.pre[...] = dot_cols(self.d_mlp[...], self.wd[columns, :])
        put_blocks(self.gd, index, dot_rows(self.hidden[:, columns], self.d_mlp[...]))

        def activate(step, total):
            at = rows_at(step, self.chunk)
            grad = (self.pre[at, :] * self.slope[at, columns].astype(F32)).astype(BF16)
            self.hidden[at, columns] = grad
            return total + fold(grad.astype(F32))

        total = lax.fori_loop(0, self.steps, activate, jnp.zeros((8, self.tile), F32), unroll=7)
        self.put_up_sum(index, total)
        put_blocks(self.gu, index, dot_rows(self.mlp_in[...], self.hidden[:, columns]))

    def up_back(self):
        self.pre[...] = dot_cols(self.hidden[...], self.wu[...])

    def mlp_back(self):
        gain = self.gain(4, self.width)

        def step(index, totals):
            at = rows_at(index, self.chunk)
            inv = self.stat(at, 5)
            normed = (self.resid[at, :] - self.stat(at, 4)) * inv
            upstream = self.pre[at, :]
            d_resid = self.d_mlp[at, :].astype(F32) + norm_back(upstream, normed, inv, gain)
            self.resid[at, :] = d_resid
            self.d_mlp[at, :] = d_resid.astype(BF16)
            return (
                totals[0] + fold(upstream * normed),
                totals[1] + fold(upstream),
                totals[2] + fold(d_resid),
            )

        blank = jnp.zeros((8, self.width), F32)
        totals = lax.fori_loop(0, self.steps, step, (blank, blank, blank), unroll=7)
        for row, total in zip((5, 6, 4), totals):
            self.put_sum(row, total)

    def proj_back(self):
        size = self.width // self.gp.shape[0]
        product = dot_rows(self.att[...], self.d_mlp[...])
        for index in range(self.gp.shape[0]):
            put_blocks(self.gp, index, product[index * size : (index + 1) * size])
        self.att[...] = dot_cols(self.d_mlp[...], self.wp[...]).astype(BF16)
        self.d_bias[...] = jnp.zeros_like(self.d_bias)

    def attend_back(self, first, last):
        def step(index):
            shift_both(self.d_bias, False)
            attention_backward(
                last - 1 - index, self.qkv, self.att, self.probs, self.d_bias, self.qkv
            )

        each(last - first, step)

    def bias_back(self):
        self.put_table(reduce_bias(self.d_bias, self.spread, self.heads))
        ones = jnp.full((8, self.rows), 1.0, BF16)
        self.put_sum(8, dot(ones, self.qkv[0]), True)
        self.put_sum(9, dot(ones, self.qkv[2]), True)

    def qkv_back(self):
        for part in range(3):
            put_columns(self.gqkv, part, dot_rows(self.attn_in[...], self.qkv[part]))
        self.pre[...] = (
            dot_cols(self.qkv[0], self.wqkv[0])
            + dot_cols(self.qkv[1], self.wqkv[1])
            + dot_cols(self.qkv[2], self.wqkv[2])
        )

    def attn_back(self):
        gain = self.gain(2, self.width)

        def step(index, totals):
            at = rows_at(index, self.chunk)
            inv = self.stat(at, 3)
            normed = (self.section[at, :].astype(F32) - self.stat(at, 2)) * inv
            upstream = self.pre[at, :]
            d_section = self.resid[at, :] + norm_back(upstream, normed, inv, gain)
            self.d_mlp[at, :] = d_section.astype(BF16)
            return totals[0] + fold(upstream * normed), totals[1] + fold(upstream)

        blank = jnp.zeros((8, self.width), F32)
        totals = lax.fori_loop(0, self.steps, step, (blank, blank), unroll=7)
        self.put_sum(2, totals[0])
        self.put_sum(3, totals[1])

    def merge_weight_back(self):
        put_columns(self.gm, 0, dot_rows(self.merged[...], self.d_mlp[...]))

    def merge_in_back(self):
        self.d_in[...] = dot_cols(self.d_mlp[...], self.wm[...])

    def merge_back(self):
        gain = self.gain(0, self.wide)

        def step(index, totals):
            at = rows_at(index, self.chunk)
            inv = self.stat(at, 1)
            normed = (self.x[at, :].astype(F32) - self.stat(at, 0)) * inv
            upstream = self.d_in[at, :]
            self.d_in[at, :] = norm_back(upstream, normed, inv, gain)
            return totals[0] + fold(upstream * normed), totals[1] + fold(upstream)

        blank = jnp.zeros((8, self.wide), F32)
        totals = lax.fori_loop(0, self.steps, step, (blank, blank), unroll=7)
        self.put_sum(0, totals[0])
        self.put_sum(1, totals[1])

    def put_sum(self, row, values, summed=False):
        values = values[0:1] if summed else sum_rows(values)
        for block in range(values.shape[1] // LANES):
            place = SUM_ROWS[row] + block
            self.sums[place : place + 1, :] = values[:, block * LANES : (block + 1) * LANES]

    def put_up_sum(self, index, total):
        values = sum_rows(total)
        blocks = self.tile // LANES
        for block in range(blocks):
            place = SUM_ROWS[10] + index * blocks + block
            self.sums[pl.ds(place, 1), :] = values[:, block * LANES : (block + 1) * LANES]

    def put_table(self, values):
        for half in range(2):
            place = SUM_ROWS[11] + half * self.heads
            self.sums[place : place + self.heads, :] = values[:, half * LANES : (half + 1) * LANES]


SUM_ROWS = (0, 8, 16, 20, 24, 28, 32, 36, 40, 44, 48, 64)
SUM_SIZE = 128


def put_blocks(ref, shard, values):
    rows = values.shape[0]
    for block in range(values.shape[1] // LANES):
        at = pl.ds(block * rows, rows)
        ref[shard, at, :] = values[:, block * LANES : (block + 1) * LANES].astype(BF16)


def put_columns(ref, part, values):
    rows = values.shape[0]
    for shard in range(ref.shape[0]):
        piece = values[:, shard * LANES : (shard + 1) * LANES]
        ref[shard, part * rows : (part + 1) * rows, :] = piece.astype(BF16)


def local_scratch(rows, wide, width, units):
    heads = width // HD
    windows = rows // TOK
    return dict(
        merged=pltpu.VMEM((rows, wide), BF16),
        section=pltpu.VMEM((rows, width), BF16),
        attn_in=pltpu.VMEM((rows, width), BF16),
        qkv=pltpu.VMEM((3, rows, width), BF16),
        probs=pltpu.VMEM((windows, SPAN, heads * SPAN), BF16),
        att=pltpu.VMEM((rows, width), BF16),
        resid=pltpu.VMEM((rows, width), F32),
        mlp_in=pltpu.VMEM((rows, width), BF16),
        hidden=pltpu.VMEM((rows, units), BF16),
        slope=pltpu.VMEM((rows, units), BF16),
        pre=pltpu.VMEM((rows, width), F32),
        d_mlp=pltpu.VMEM((rows, width), BF16),
        stats=pltpu.VMEM((rows, 8), F32),
        bias=pltpu.VMEM((SPAN, heads * SPAN), F32),
        d_bias=pltpu.VMEM((SPAN, heads * SPAN), F32),
        spread=pltpu.VMEM((SPAN * heads, LANES), F32),
    )


MESH_ID = pl.DeviceIdType.MESH


class Links:
    def __init__(self, send_sems, recv_sems, plan):
        self.send_sems, self.recv_sems, self.plan = send_sems, recv_sems, plan
        self.sent = []
        self.sp, self.tp = lax.axis_index("sp"), lax.axis_index("tp")

    def place(self, way):
        kind, distance = way
        if kind == "tp":
            return self.sp, self.tp ^ distance
        return self.sp ^ distance, self.tp

    def copy(self, name, way, source, target):
        slot = self.plan.setdefault(name, len(self.plan))
        return pltpu.make_async_remote_copy(
            src_ref=source,
            dst_ref=target,
            send_sem=self.send_sems.at[slot],
            recv_sem=self.recv_sems.at[slot],
            device_id=self.place(way),
            device_id_type=MESH_ID,
        )

    def send(self, name, way, source, target):
        copy = self.copy(name, way, source, target)
        copy.start()
        self.sent.append(copy)

    def receive(self, name, way, target):
        self.copy(name, way, target, target).wait_recv()

    def keep(self, name, source, target):
        slot = self.plan.setdefault(name, len(self.plan))
        copy = pltpu.make_async_copy(source, target, self.recv_sems.at[slot])
        copy.start()
        return copy

    def greet(self, ways):
        barrier = pltpu.get_barrier_semaphore()
        for way in ways:
            pl.semaphore_signal(
                barrier, inc=1, device_id=self.place(way), device_id_type=MESH_ID
            )
        pl.semaphore_wait(barrier, len(ways))

    def drain(self):
        for copy in self.sent:
            copy.wait_send()


CORE, ACROSS, BESIDE = ("tp", 1), ("tp", 2), ("sp", 1)


def far_ways(sp_size):
    return [("sp", 2 * step) for step in range(1, sp_size // 2)]


class Gather:
    def __init__(self, links, name, own, whole, view, split):
        self.links, self.name, self.own, self.whole = links, name, own, whole
        self.view, self.split = view, split
        self.half = links.sp & 1

    def part(self, shard, half=None):
        return self.view(self.whole, shard, half)

    def label(self, step):
        return (self.name, step)

    def start(self):
        links = self.links
        mine = links.tp
        self.local = links.keep(self.label("own"), self.own, self.part(mine))
        half = self.half if self.split else None
        links.send(
            self.label("x"), ACROSS, self.view(self.own, None, half), self.part(mine, half)
        )
        links.send(self.label("c"), CORE, self.own, self.part(mine))

    def forward(self):
        links = self.links
        other = links.tp ^ 2
        half = self.half if self.split else None
        block = self.part(other, half)
        links.receive(self.label("x"), ACROSS, block)
        if self.split:
            links.send(self.label("y"), BESIDE, block, block)
        links.send(self.label("xc"), CORE, block, block)

    def forward_beside(self):
        if self.split:
            links = self.links
            block = self.part(links.tp ^ 2, 1 - self.half)
            links.receive(self.label("y"), BESIDE, block)
            links.send(self.label("yc"), CORE, block, block)

    def finish(self):
        links = self.links
        self.local.wait()
        links.receive(self.label("c"), CORE, self.part(links.tp ^ 1))
        half = self.half if self.split else None
        links.receive(self.label("xc"), CORE, self.part(links.tp ^ 3, half))
        if self.split:
            links.receive(self.label("yc"), CORE, self.part(links.tp ^ 3, 1 - self.half))


def column_view(size, halves):
    def view(ref, shard, half):
        rank = len(ref.shape)
        rows = ref.shape[rank - 2]
        at = slice(None) if half is None else pl.ds(
            pl.multiple_of(half * (rows // 2), 16), rows // 2
        )
        lanes = slice(None) if shard is None else pl.ds(pl.multiple_of(shard * size, LANES), size)
        return ref.at[(slice(None),) * (rank - 2) + (at, lanes)]

    return view


def row_view(size):
    def view(ref, shard, half):
        start = 0 if shard is None else shard * size
        if half is None:
            return ref.at[pl.ds(start, size), :]
        start = start + half * (size // 2)
        return ref.at[pl.ds(pl.multiple_of(start, 16), size // 2), :]

    return view


def lead_view(ref, shard, half):
    return ref if shard is None else ref.at[shard]


def add_rows(target, start, rows, terms, chunk=128):
    chunk = math.gcd(rows, chunk)

    def step(index):
        offset = index * chunk

        def at(first):
            return pl.ds(pl.multiple_of(first + offset, 16), chunk)

        total = None
        for ref, first in terms:
            value = ref[at(first), :].astype(F32)
            total = value if total is None else total + value
        target[at(start), :] = total.astype(target.dtype)

    each(rows // chunk, step)


class Reduce:
    def __init__(self, links, name, grads, core_in, across_in, beside_in, far_in, result, group):
        self.links, self.name, self.grads = links, name, grads
        self.core_in, self.across_in, self.beside_in = core_in, across_in, beside_in
        self.far_in, self.result, self.group = far_in, result, group
        self.rows = grads.shape[1]
        self.half_rows = self.rows // 2
        self.piece = self.half_rows // group
        self.half = links.sp & 1
        self.seat = links.sp >> 1
        self.steps = [
            self.core_send, self.core_add, self.across_add, self.beside_add, self.far_add,
            self.far_done, self.beside_done,
        ]

    def run(self):
        self.steps.pop(0)()

    def label(self, *step):
        return (self.name,) + step

    def core_send(self):
        links = self.links
        for across in range(2):
            links.send(
                self.label("c", across), CORE, self.grads.at[(links.tp & 1) ^ 1 | 2 * across],
                self.core_in.at[across],
            )

    def core_add(self):
        links = self.links
        for across in range(2):
            links.receive(self.label("c", across), CORE, self.core_in.at[across])
        other = links.tp ^ 2
        block = self.grads.at[other]
        add_rows(block, 0, self.rows, [(block, 0), (self.core_in.at[other >> 1], 0)])
        links.send(self.label("x"), ACROSS, block, self.across_in)

    def across_add(self):
        links = self.links
        links.receive(self.label("x"), ACROSS, self.across_in)
        block = self.grads.at[links.tp]
        terms = [(block, 0), (self.core_in.at[links.tp >> 1], 0), (self.across_in, 0)]
        add_rows(block, 0, self.rows, terms)
        links.send(
            self.label("y"), BESIDE, self.rows_of(block, 1 - self.half), self.beside_in
        )

    def rows_of(self, ref, half, piece=None):
        if piece is None:
            return ref.at[pl.ds(pl.multiple_of(half * self.half_rows, 16), self.half_rows), :]
        start = half * self.half_rows + piece * self.piece
        return ref.at[pl.ds(pl.multiple_of(start, 16), self.piece), :]

    def beside_add(self):
        links = self.links
        links.receive(self.label("y"), BESIDE, self.beside_in)
        block = self.grads.at[links.tp]
        mine = self.half * self.half_rows
        add_rows(block, mine, self.half_rows, [(block, mine), (self.beside_in, 0)])
        for step in range(1, self.group):
            links.send(
                self.label("z", step), ("sp", 2 * step),
                self.rows_of(block, self.half, self.seat ^ step), self.far_in.at[step - 1],
            )

    def far_add(self):
        links = self.links
        block = self.grads.at[links.tp]
        mine = self.half * self.half_rows + self.seat * self.piece
        terms = [(block, mine)]
        for step in range(1, self.group):
            links.receive(self.label("z", step), ("sp", 2 * step), self.far_in.at[step - 1])
            terms.append((self.far_in.at[step - 1], 0))
        add_rows(self.result, mine, self.piece, terms)
        done = self.rows_of(self.result, self.half, self.seat)
        for step in range(1, self.group):
            links.send(self.label("a", step), ("sp", 2 * step), done, done)

    def far_done(self):
        links = self.links
        for step in range(1, self.group):
            links.receive(
                self.label("a", step), ("sp", 2 * step),
                self.rows_of(self.result, self.half, self.seat ^ step),
            )
        done = self.rows_of(self.result, self.half)
        links.send(self.label("b"), BESIDE, done, done)

    def beside_done(self):
        self.links.receive(
            self.label("b"), BESIDE, self.rows_of(self.result, 1 - self.half)
        )


class Total:
    def __init__(self, links, name, stages, inboxes, far_in, result, group):
        self.links, self.name, self.stages, self.inboxes = links, name, stages, inboxes
        self.far_in, self.result, self.group = far_in, result, group
        self.piece = result.shape[0] // group
        self.seat = links.sp >> 1
        self.ways = (CORE, ACROSS, BESIDE)
        self.steps = [
            functools.partial(self.exchange, 0), functools.partial(self.add, 0),
            functools.partial(self.add, 1), functools.partial(self.add, 2), self.far_add,
            self.far_done,
        ]

    def run(self):
        self.steps.pop(0)()

    def label(self, *step):
        return (self.name,) + step

    def at(self, ref, piece):
        return ref.at[pl.ds(pl.multiple_of(piece * self.piece, 8), self.piece), :]

    def exchange(self, stage):
        self.links.send(
            self.label("e", stage), self.ways[stage], self.stages.at[stage],
            self.inboxes.at[stage],
        )

    def add(self, stage):
        self.links.receive(self.label("e", stage), self.ways[stage], self.inboxes.at[stage])
        self.stages[stage + 1] = self.stages[stage] + self.inboxes[stage]
        if stage < 2:
            self.exchange(stage + 1)
            return
        for step in range(1, self.group):
            self.links.send(
                self.label("z", step), ("sp", 2 * step),
                self.at(self.stages.at[3], self.seat ^ step), self.far_in.at[step - 1],
            )

    def far_add(self):
        total = self.at(self.stages.at[3], self.seat)[...]
        for step in range(1, self.group):
            self.links.receive(self.label("z", step), ("sp", 2 * step), self.far_in.at[step - 1])
            total = total + self.far_in[step - 1]
        done = self.at(self.result, self.seat)
        done[...] = total
        for step in range(1, self.group):
            self.links.send(self.label("a", step), ("sp", 2 * step), done, done)

    def far_done(self):
        for step in range(1, self.group):
            self.links.receive(
                self.label("a", step), ("sp", 2 * step), self.at(self.result, self.seat ^ step)
            )


GRADS = ("gd", "gu", "gp", "gqkv", "gm")
WEIGHTS = ("wm", "wqkv", "wp", "wu", "wd")
INPUTS = ("valid", "edge", "x", "grad_out", "gains", "pack") + tuple("own_" + n for n in WEIGHTS)
OUTPUTS = ("out", "d_in", "o_gm", "o_gqkv", "o_gp", "o_gu", "o_gd", "o_sums")


def whole_kernel(names, group, plan, *refs):
    refs = dict(zip(names, refs, strict=True))
    links = Links(refs.pop("send_sems"), refs.pop("recv_sems"), plan)
    links.greet([CORE, ACROSS, BESIDE] + far_ways(2 * group))

    own = {name: refs.pop("own_" + name) for name in WEIGHTS}
    views = dict(
        wm=column_view(own["wm"].shape[1], True),
        wqkv=column_view(own["wqkv"].shape[2], True),
        wp=row_view(own["wp"].shape[0]),
        wu=column_view(own["wu"].shape[1], True),
        wd=row_view(own["wd"].shape[0]),
    )
    gathers = {
        name: Gather(links, name, own[name], refs[name], views[name], name != "wm")
        for name in WEIGHTS
    }
    gathers["pack"] = Gather(links, "pack", refs.pop("pack"), refs["packs"], lead_view, False)
    for name in ("wm", "pack", "wqkv", "wp", "wu", "wd"):
        gathers[name].start()

    packs = refs.pop("packs")
    results = {name: refs.pop("r_" + name) for name in GRADS}
    outs = {name: refs.pop("o_" + name) for name in GRADS}
    reduces = {
        name: Reduce(
            links, name, refs[name], refs.pop("c_" + name), refs.pop("x_" + name),
            refs.pop("y_" + name), refs.pop("z_" + name), results[name], group,
        )
        for name in GRADS
    }
    stages, inboxes = refs.pop("sum_stages"), refs.pop("sum_inboxes")
    refs["sums"] = stages.at[0]
    total = Total(links, "sums", stages, inboxes, refs.pop("sum_far"), refs.pop("o_sums"), group)

    shards = packs.shape[0]

    def table():
        rows = refs["rel_rows"]
        return jnp.concatenate(
            [packs[shard, 0:rows, : 2 * LANES] for shard in range(shards)], axis=0
        )

    def qkv_bias(part):
        row = 4 if part == 0 else 5
        return jnp.concatenate(
            [packs[shard, row : row + 1, :LANES] for shard in range(shards)], axis=1
        )

    def up_bias(index):
        return packs[index, 6:7, :]

    refs.update(table=table, qkv_bias=qkv_bias, up_bias=up_bias, rel_rows=4)
    local = Local(refs, links.tp * (refs["x"].shape[0] // TOK))

    def output(name):
        fin, out = results[name], outs[name]
        if name == "gm":
            out[...] = fin[...].astype(F32)
        elif name == "gqkv":
            rows = out.shape[1]
            for part in range(3):
                out[part] = fin[part * rows : (part + 1) * rows, :].astype(F32)
        else:
            rows = out.shape[0]
            for block in range(out.shape[1] // LANES):
                lanes = slice(block * LANES, (block + 1) * LANES)
                out[:, lanes] = fin[block * rows : (block + 1) * rows, :].astype(F32)

    stages[0] = jnp.zeros_like(stages[0])
    local.prepare()
    local.merge_norm()
    gathers["wm"].forward()
    gathers["pack"].forward()
    gathers["wm"].finish()
    gathers["pack"].finish()
    local.merge()
    gathers["wqkv"].forward()
    gathers["wp"].forward()
    local.attn_norm()
    local.table_bias()
    gathers["wqkv"].forward_beside()
    gathers["wp"].forward_beside()
    gathers["wqkv"].finish()
    local.project()
    windows = local.windows
    quarter = windows // 4
    local.attend(0, quarter)
    gathers["wu"].forward()
    gathers["wp"].finish()
    local.attend(quarter, 2 * quarter)
    gathers["wu"].forward_beside()
    gathers["wd"].forward()
    local.attend(2 * quarter, 3 * quarter)
    gathers["wd"].forward_beside()
    local.attend(3 * quarter, windows)
    local.attn_out()
    local.mlp_norm()
    gathers["wu"].finish()
    local.up()
    gathers["wd"].finish()
    local.down()
    local.finish()

    each(refs["gd"].shape[0], local.down_back)
    reduces["gd"].run()
    reduces["gu"].run()
    local.up_back()
    reduces["gd"].run()
    reduces["gu"].run()
    local.mlp_back()
    local.proj_back()
    reduces["gp"].run()
    local.attend_back(3 * quarter, windows)
    reduces["gp"].run()
    reduces["gd"].run()
    local.attend_back(2 * quarter, 3 * quarter)
    reduces["gd"].run()
    reduces["gu"].run()
    local.attend_back(quarter, 2 * quarter)
    reduces["gd"].run()
    reduces["gu"].run()
    reduces["gp"].run()
    local.attend_back(0, quarter)
    reduces["gd"].run()
    reduces["gu"].run()
    reduces["gp"].run()
    local.bias_back()
    local.qkv_back()
    reduces["gqkv"].run()
    reduces["gd"].run()
    reduces["gu"].run()
    reduces["gp"].run()
    local.attn_back()
    reduces["gqkv"].run()
    reduces["gp"].run()
    output("gd")
    local.merge_weight_back()
    reduces["gm"].run()
    reduces["gu"].run()
    local.merge_in_back()
    reduces["gm"].run()
    reduces["gp"].run()
    local.merge_back()
    total.run()
    total.run()
    reduces["gqkv"].run()
    reduces["gm"].run()
    total.run()
    reduces["gqkv"].run()
    reduces["gm"].run()
    total.run()
    output("gu")
    output("gp")
    reduces["gqkv"].run()
    reduces["gm"].run()
    total.run()
    reduces["gqkv"].run()
    reduces["gm"].run()
    total.run()
    reduces["gqkv"].run()
    reduces["gm"].run()
    output("gqkv")
    output("gm")
    links.drain()


def whole_call(group, inputs):
    rows, wide = inputs["x"].shape
    shards = 4
    width = inputs["own_wu"].shape[0]
    units = shards * inputs["own_wu"].shape[1]
    depth = dict(gd=units, gu=units, gp=width, gqkv=3 * width, gm=wide)
    scratch = local_scratch(rows, wide, width, units)
    scratch.update(
        wm=pltpu.VMEM((wide, width), BF16),
        wqkv=pltpu.VMEM((3, width, width), BF16),
        wp=pltpu.VMEM((width, width), BF16),
        wu=pltpu.VMEM((width, units), BF16),
        wd=pltpu.VMEM((units, width), BF16),
        packs=pltpu.VMEM((shards,) + inputs["pack"].shape, F32),
    )
    for name in GRADS:
        size = depth[name]
        scratch[name] = pltpu.VMEM((shards, size, LANES), BF16)
        scratch["c_" + name] = pltpu.VMEM((2, size, LANES), BF16)
        scratch["x_" + name] = pltpu.VMEM((size, LANES), BF16)
        scratch["y_" + name] = pltpu.VMEM((size // 2, LANES), BF16)
        scratch["z_" + name] = pltpu.VMEM((group - 1, size // 2 // group, LANES), BF16)
        scratch["r_" + name] = pltpu.VMEM((size, LANES), BF16)
    scratch["sum_stages"] = pltpu.VMEM((4, SUM_SIZE, LANES), F32)
    scratch["sum_inboxes"] = pltpu.VMEM((3, SUM_SIZE, LANES), F32)
    scratch["sum_far"] = pltpu.VMEM((group - 1, SUM_SIZE // group, LANES), F32)
    count = 6 * 6 + len(GRADS) * (5 + 2 * group) + 4 + 2 * group
    scratch["send_sems"] = pltpu.SemaphoreType.DMA((count,))
    scratch["recv_sems"] = pltpu.SemaphoreType.DMA((count,))
    outs = dict(
        out=jax.ShapeDtypeStruct((rows, width), BF16),
        d_in=jax.ShapeDtypeStruct((rows, wide), F32),
        o_gm=jax.ShapeDtypeStruct(inputs["own_wm"].shape, F32),
        o_gqkv=jax.ShapeDtypeStruct(inputs["own_wqkv"].shape, F32),
        o_gp=jax.ShapeDtypeStruct(inputs["own_wp"].shape, F32),
        o_gu=jax.ShapeDtypeStruct(inputs["own_wu"].shape, F32),
        o_gd=jax.ShapeDtypeStruct(inputs["own_wd"].shape, F32),
        o_sums=jax.ShapeDtypeStruct((SUM_SIZE, LANES), F32),
    )
    names = INPUTS + OUTPUTS + tuple(scratch)
    vmem = pl.BlockSpec(memory_space=pltpu.VMEM)
    smem = pl.BlockSpec(memory_space=pltpu.SMEM)
    hbm = pl.BlockSpec(memory_space=pl.ANY)
    return pl.pallas_call(
        functools.partial(whole_kernel, names, group, {}),
        out_shape=[outs[name] for name in OUTPUTS],
        in_specs=[smem, smem, vmem, vmem, vmem, hbm] + [hbm] * len(WEIGHTS),
        out_specs=[vmem] * len(OUTPUTS),
        scratch_shapes=list(scratch.values()),
        compiler_params=pltpu.CompilerParams(
            vmem_limit_bytes=63 * MIB, collective_id=0, has_side_effects=True
        ),
    )(*[inputs[name] for name in INPUTS])


def pad_to(values, rows, lanes):
    return jnp.pad(values, ((0, rows - values.shape[0]), (0, lanes - values.shape[1])))


def on_device(
    inputs, grad_out, window_valid, window_edge, merge_gain, merge_bias, merge_weight, attn_gain,
    attn_bias, query_key_value_weight, qv_bias, rel_table, proj_weight, proj_bias, mlp_gain,
    mlp_bias, up_weight, up_bias, down_weight, down_bias,
):
    tp_index = lax.axis_index("tp")
    wide, width, tile = merge_gain.shape[0], down_bias.shape[0], up_bias.shape[0]
    gains = jnp.concatenate(
        [
            pad_to(vector.astype(F32)[None], 1, wide)
            for vector in (
                merge_gain, merge_bias, attn_gain, attn_bias, mlp_gain, mlp_bias, proj_bias,
                down_bias,
            )
        ],
        axis=0,
    )
    pack = jnp.concatenate(
        [
            pad_to(rel_table.T.astype(F32), 4, tile),
            pad_to(qv_bias.astype(F32), 2, tile),
            pad_to(up_bias.astype(F32)[None], 2, tile),
        ],
        axis=0,
    )
    out, d_in, gm, gqkv, gp, gu, gd, sums = whole_call(
        lax.axis_size("sp") // 2,
        dict(
            valid=window_valid, edge=window_edge, x=inputs, grad_out=grad_out, gains=gains,
            pack=pack, own_wm=merge_weight,
            own_wqkv=jnp.transpose(query_key_value_weight, (1, 0, 2)), own_wp=proj_weight,
            own_wu=up_weight, own_wd=down_weight,
        ),
    )

    def vector(row, size):
        return lax.slice_in_dim(sums, SUM_ROWS[row], SUM_ROWS[row] + size // LANES).reshape(-1)

    def mine(whole, size):
        return lax.dynamic_slice_in_dim(whole, tp_index * size, size, 0)

    heads = width // HD
    table = jnp.concatenate(
        [sums[SUM_ROWS[11] + half * heads :][:heads] for half in range(2)], axis=1
    )[:, :REL]
    qv = jnp.stack([mine(vector(row, width), qv_bias.shape[1]) for row in (8, 9)])
    return (
        out,
        d_in,
        vector(0, wide),
        vector(1, wide),
        gm,
        vector(2, width),
        vector(3, width),
        jnp.transpose(gqkv, (1, 0, 2)),
        qv,
        mine(table, rel_table.shape[1]).T,
        gp,
        vector(4, width),
        vector(5, width),
        vector(6, width),
        gu,
        mine(vector(10, 4 * tile), tile),
        gd,
        vector(7, width),
    )


def solution(mesh):
    placed = (
        P(("sp", "tp"), None),
        P(("sp", "tp"), None),
        P("sp"),
        P("sp"),
        P(),
        P(),
        P(None, "tp"),
        P(),
        P(),
        P(None, None, "tp"),
        P(None, "tp"),
        P(None, "tp"),
        P("tp", None),
        P(),
        P(),
        P(),
        P(None, "tp"),
        P("tp"),
        P("tp", None),
        P(),
    )
    return jax.shard_map(
        on_device,
        mesh=mesh,
        in_specs=placed,
        out_specs=(
            P(("sp", "tp"), None),
            P(("sp", "tp"), None),
            P(),
            P(),
            P(None, "tp"),
            P(),
            P(),
            P(None, None, "tp"),
            P(None, "tp"),
            P(None, "tp"),
            P("tp", None),
            P(),
            P(),
            P(),
            P(None, "tp"),
            P("tp"),
            P("tp", None),
            P(),
        ),
        check_vma=False,
    )
```

```python
import functools
import math

import jax
import jax.numpy as jnp
from jax import lax
from jax.experimental import pallas as pl
from jax.experimental.pallas import tpu as pltpu
from jax.sharding import PartitionSpec as P

SIDE = 7
TOK = SIDE * SIDE
REL_SIDE = 2 * SIDE - 1
REL = REL_SIDE * REL_SIDE
SPAN = 64
GROUP = 4
HD = 32
LANES = 128
EPSILON = 1e-05
NEG_FILL = -1000000000.0
MIB = 1 << 20
F32 = jnp.float32
BF16 = jnp.bfloat16


def dot(left, right):
    return jnp.dot(left, right, preferred_element_type=F32)


def dot_cols(left, right):
    return lax.dot_general(left, right, (((1,), (1,)), ((), ())), preferred_element_type=F32)


def dot_rows(left, right):
    return lax.dot_general(left, right, (((0,), (0,)), ((), ())), preferred_element_type=F32)


def rows_at(index, size):
    return pl.ds(pl.multiple_of(index * size, size), size)


def each(count, body, unroll=1):
    def step(index, carry):
        body(index)
        return carry

    lax.fori_loop(0, count, step, 0, unroll=unroll)


def fold(values):
    total = values[0:8]
    for start in range(8, values.shape[0], 8):
        total = total + values[start : start + 8]
    return total


def iota(shape, dim):
    return lax.broadcasted_iota(jnp.int32, shape, dim)


def norm_rows(values):
    mean = jnp.mean(values, -1, keepdims=True)
    centred = values - mean
    inv = lax.rsqrt(jnp.mean(centred * centred, -1, keepdims=True) + EPSILON)
    return centred * inv, mean, inv


def norm_back(upstream, normed, inv, gain):
    scaled = upstream * gain
    return inv * (
        scaled
        - jnp.mean(scaled, -1, keepdims=True)
        - normed * jnp.mean(scaled * normed, -1, keepdims=True)
    )


def gelu_both(values):
    size = jnp.abs(values) * 0.7071067811865476
    bell = jnp.exp(-size * size)
    t = 1.0 / (1.0 + 0.3275911 * size)
    poly = t * (
        0.254829592
        + t * (-0.284496736 + t * (1.421413741 + t * (-1.453152027 + t * 1.061405429)))
    )
    tail = 0.5 * poly * bell
    phi = jnp.where(values >= 0, 1.0 - tail, tail)
    return values * phi, phi + values * bell * 0.3989422804014327


def window_row_col(index):
    row = (index * 37) >> 8
    return row, index - SIDE * row


def region_ids(index, edge, outside):
    row, col = window_row_col(index)
    high = SIDE - SIDE // 2
    region = (edge & 1) * (col >= high).astype(jnp.int32) + 2 * (edge >> 1) * (
        row >= high
    ).astype(jnp.int32)
    return jnp.where((index >= 0) & (index < TOK), region, outside)


def head_masks():
    lane = iota((1, LANES), 1)
    return [((lane >> 5) == head).astype(F32).astype(BF16) for head in range(GROUP)]


def spread_heads(block, masks):
    return jnp.concatenate([block * mask for mask in masks], axis=0)


def pick_heads(product):
    lane = iota((SPAN, LANES), 1)
    result = product[3 * SPAN : 4 * SPAN]
    for head in (2, 1, 0):
        result = jnp.where(
            lane < (head + 1) * HD, product[head * SPAN : (head + 1) * SPAN], result
        )
    return result


def same_head(rows, columns):
    return (
        (iota((rows, columns), 0) // (rows // GROUP))
        == (iota((rows, columns), 1) // (columns // GROUP))
    ).astype(F32).astype(BF16)


def offset_select(half):
    place = iota((LANES, LANES), 0)
    lane = iota((LANES, LANES), 1)
    token = lane - half * SPAN
    row, col = window_row_col(token & (SPAN - 1))
    wanted = (SIDE - 1) * (REL_SIDE + 1) - (REL_SIDE * row + col)
    hit = (place == wanted) & (token >= 0) & (token < TOK)
    return hit.astype(F32).astype(BF16)


def build_bias(table, spread_ref, bias_ref):
    heads = table.shape[0]

    def one(index):
        row = index // SIDE
        shift = index + (SIDE - 1) * row
        rolled = pltpu.roll(table, (2 * LANES - shift) % (2 * LANES), 1)
        spread_ref[rows_at(index, heads), :] = rolled[:, :LANES]

    spread_ref[...] = jnp.zeros_like(spread_ref)
    for index in range(TOK):
        one(index)
    low, high = offset_select(0), offset_select(1)
    for pair in range(heads // 2):
        first = spread_ref[pl.ds(2 * pair, SPAN, stride=heads), :].astype(BF16)
        second = spread_ref[pl.ds(2 * pair + 1, SPAN, stride=heads), :].astype(BF16)
        bias_ref[:, pair * LANES : (pair + 1) * LANES] = dot(first, low) + dot(second, high)


def split_bf16(values):
    high = values.astype(BF16)
    return high, (values - high.astype(F32)).astype(BF16)


def reduce_bias(bias_ref, spread_ref, heads):
    low, high = offset_select(0), offset_select(1)
    for pair in range(heads // 2):
        parts = split_bf16(bias_ref[:, pair * LANES : (pair + 1) * LANES])
        spread_ref[pl.ds(2 * pair, SPAN, stride=heads), :] = sum(
            dot_cols(part, low) for part in parts
        )
        spread_ref[pl.ds(2 * pair + 1, SPAN, stride=heads), :] = sum(
            dot_cols(part, high) for part in parts
        )
    total = jnp.zeros((heads, 2 * LANES), F32)
    blank = jnp.zeros((heads, LANES), F32)
    for index in range(TOK):
        shift = index + (SIDE - 1) * (index // SIDE)
        row = jnp.concatenate([spread_ref[index * heads : (index + 1) * heads, :], blank], axis=1)
        total = total + (pltpu.roll(row, shift, 1) if shift else row)
    return total


def shift_both(ref, forward):
    rows, columns = ref.shape
    down, right = (1, 1) if forward else (rows - 1, columns - 1)
    ref[...] = pltpu.roll(pltpu.roll(ref[...], down, 0), right, 1)


def attention_forward(window, edge, qkv, bias_ref, probs_ref, att_ref):
    base = pl.ds(pl.multiple_of(window * (TOK - 1), 16), SPAN)
    masks = head_masks()
    ones = same_head(GROUP * SPAN, GROUP * SPAN)
    row_index = iota((SPAN, 1), 0) - window
    row_in = (row_index >= 0) & (row_index < TOK)
    row_region = region_ids(row_index, edge, 8)
    lane_region = region_ids((iota((1, GROUP * SPAN), 1) & (SPAN - 1)) - window, edge, 16)
    allowed = row_region == lane_region
    first_half = iota((SPAN, LANES), 1) < SPAN
    keep = row_in.astype(F32)
    groups = att_ref.shape[1] // LANES
    for group in range(groups):
        lanes = pl.ds(group * LANES, LANES)
        wide = pl.ds(group * GROUP * SPAN, GROUP * SPAN)
        query, key, value = (qkv[part, base, lanes] for part in range(3))
        logits = dot_cols(query, spread_heads(key, masks)) * (HD**-0.5) + bias_ref[:, wide]
        logits = jnp.where(allowed, logits, NEG_FILL)
        tops = []
        for half in range(GROUP * SPAN // LANES):
            piece = logits[:, half * LANES : (half + 1) * LANES]
            top_low = jnp.max(jnp.where(first_half, piece, 2 * NEG_FILL), -1, keepdims=True)
            top_high = jnp.max(jnp.where(first_half, 2 * NEG_FILL, piece), -1, keepdims=True)
            tops.append(jnp.where(first_half, top_low, top_high))
        terms = jnp.exp(logits - jnp.concatenate(tops, axis=1))
        totals = dot(terms.astype(BF16), ones)
        probs = (terms * (keep / totals)).astype(BF16)
        probs_ref[window, :, wide] = probs
        attended = dot(probs, spread_heads(value, masks))
        att_ref[base, lanes] = jnp.where(
            row_in, attended, att_ref[base, lanes].astype(F32)
        ).astype(BF16)


def attention_backward(window, qkv, d_att, probs_ref, d_bias_ref, d_qkv):
    base = pl.ds(pl.multiple_of(window * (TOK - 1), 16), SPAN)
    masks = head_masks()
    ones = same_head(GROUP * SPAN, GROUP * SPAN)
    row_index = iota((SPAN, 1), 0) - window
    row_in = (row_index >= 0) & (row_index < TOK)
    groups = d_att.shape[1] // LANES
    factor = HD**-0.5

    def put(part, lanes, values):
        d_qkv[part, base, lanes] = jnp.where(
            row_in, values, d_qkv[part, base, lanes].astype(F32)
        ).astype(BF16)

    for group in range(groups):
        lanes = pl.ds(group * LANES, LANES)
        wide = pl.ds(group * GROUP * SPAN, GROUP * SPAN)
        query, key, value = (qkv[part, base, lanes] for part in range(3))
        upstream = d_att[base, lanes]
        probs = probs_ref[window, :, wide]
        probs_wide = probs.astype(F32)
        d_probs = dot_cols(upstream, spread_heads(value, masks))
        weighted = d_probs * probs_wide
        delta = dot(weighted.astype(BF16), ones)
        d_logits = (weighted - probs_wide * delta).astype(BF16)
        d_bias_ref[:, wide] += d_logits.astype(F32)
        put(0, lanes, dot(d_logits, spread_heads(key, masks)) * factor)
        put(1, lanes, pick_heads(dot_rows(d_logits, query)) * factor)
        put(2, lanes, pick_heads(dot_rows(probs, upstream)))


def sum_rows(values):
    return jnp.sum(values, 0, keepdims=True)


class Local:
    def __init__(self, refs, first_window):
        self.__dict__.update(refs)
        self.first_window = first_window
        self.rows, self.wide = self.x.shape
        self.width = self.section.shape[1]
        self.units = self.hidden.shape[1]
        self.windows = self.rows // TOK
        self.heads = self.width // HD
        self.chunk = 16
        self.steps = self.rows // self.chunk
        self.tile = self.units // self.gu.shape[0]

    def gain(self, row, lanes):
        return self.gains[row : row + 1, :lanes]

    def stat(self, at, index):
        return self.stats[at, index : index + 1]

    def keep_stats(self, at, index, mean, inv):
        self.stats[at, index : index + 1] = mean
        self.stats[at, index + 1 : index + 2] = inv

    def spread_vectors(self):
        for row, ref in enumerate(self.vectors):
            values = ref[...].astype(F32)
            for block in range(values.shape[0]):
                lanes = slice(block * LANES, (block + 1) * LANES)
                self.gains[row : row + 1, lanes] = values[block : block + 1]

    def prepare(self):
        def keep_rows(window):
            base = pl.ds(pl.multiple_of(window * (TOK - 1), 16), SPAN)
            index = iota((SPAN, 1), 0) - window
            inside = (index >= 0) & (index < TOK)
            valid = self.valid[self.first_window + window].astype(F32)
            self.stats[base, 6:7] = jnp.where(inside, valid, self.stats[base, 6:7])

        each(self.windows, keep_rows)

    def table_bias(self):
        build_bias(self.table(), self.spread, self.bias)

    def merge_norm(self):
        gain, shift = self.gain(0, self.wide), self.gain(1, self.wide)

        def step(index):
            at = rows_at(index, self.chunk)
            normed, mean, inv = norm_rows(self.x[at, :].astype(F32))
            self.merged[at, :] = (normed * gain + shift).astype(BF16)
            self.keep_stats(at, 0, mean, inv)

        each(self.steps, step, 7)

    def merge(self):
        self.section[...] = dot(self.merged[...], self.wm[...]).astype(BF16)

    def attn_norm(self):
        gain, shift = self.gain(2, self.width), self.gain(3, self.width)

        def step(index):
            at = rows_at(index, self.chunk)
            normed, mean, inv = norm_rows(self.section[at, :].astype(F32))
            self.attn_in[at, :] = (normed * gain + shift).astype(BF16)
            self.keep_stats(at, 2, mean, inv)

        each(self.steps, step, 7)

    def project(self, part):
        product = dot(self.attn_in[...], self.wqkv[part])
        if part != 1:
            product = product + self.qkv_bias(part)
        self.qkv[part] = product.astype(BF16)

    def attend(self, first, last):
        def step(index):
            window = first + index
            edge = self.edge[self.first_window + window]
            attention_forward(window, edge, self.qkv, self.bias, self.probs, self.att)
            shift_both(self.bias, True)

        each(last - first, step)

    def attn_out(self):
        self.resid[...] = dot(self.att[...], self.wp[...])

    def mlp_norm(self):
        gain, shift = self.gain(4, self.width), self.gain(5, self.width)
        proj_bias = self.gain(6, self.width)

        def step(index):
            at = rows_at(index, self.chunk)
            total = self.section[at, :].astype(F32) + self.resid[at, :] + proj_bias
            self.resid[at, :] = total
            normed, mean, inv = norm_rows(total)
            self.mlp_in[at, :] = (normed * gain + shift).astype(BF16)
            self.keep_stats(at, 4, mean, inv)

        each(self.steps, step, 7)

    def up(self):
        def part(index):
            columns = rows_at(index, self.tile)
            self.pre[...] = dot(self.mlp_in[...], self.wu[:, columns])
            shift = self.up_bias(index)

            def activate(step):
                at = rows_at(step, self.chunk)
                value, rate = gelu_both(self.pre[at, :] + shift)
                self.hidden[at, columns] = value.astype(BF16)
                self.slope[at, columns] = rate.astype(BF16)

            each(self.steps, activate, 7)

        each(self.units // self.tile, part)

    def down(self):
        self.pre[...] = dot(self.hidden[...], self.wd[...])

    def grad_rows(self):
        def step(index, total):
            at = rows_at(index, self.chunk)
            grad = self.grad_out[at, :].astype(F32) * self.stat(at, 6)
            self.d_mlp[at, :] = grad.astype(BF16)
            return total + fold(grad)

        total = lax.fori_loop(
            0, self.steps, step, jnp.zeros((8, self.width), F32), unroll=7
        )
        self.put_sum(7, total)

    def finish(self):
        down_bias = self.gain(7, self.width)

        def step(index):
            at = rows_at(index, self.chunk)
            block = (self.resid[at, :] + self.pre[at, :] + down_bias) * self.stat(at, 6)
            self.out[at, :] = block.astype(BF16)

        each(self.steps, step, 7)

    def down_weight_back(self):
        def part(index):
            columns = rows_at(index, self.tile)
            put_blocks(self.gd, index, dot_rows(self.hidden[:, columns], self.d_mlp[...]))

        each(self.units // self.tile, part)

    def hidden_back(self, first, last):
        def part(step):
            index = first + step
            columns = rows_at(index, self.tile)
            self.pre[...] = dot_cols(self.d_mlp[...], self.wd[columns, :])

            def activate(step, total):
                at = rows_at(step, self.chunk)
                grad = (self.pre[at, :] * self.slope[at, columns].astype(F32)).astype(BF16)
                self.d_pre[at, columns] = grad
                return total + fold(grad.astype(F32))

            total = lax.fori_loop(
                0, self.steps, activate, jnp.zeros((8, self.tile), F32), unroll=7
            )
            self.put_up_sum(index, total)
            put_blocks(self.gu, index, dot_rows(self.mlp_in[...], self.d_pre[:, columns]))

        each(last - first, part)

    def up_back(self):
        self.pre[...] = dot_cols(self.d_pre[...], self.wu[...])

    def mlp_back(self):
        gain = self.gain(4, self.width)

        def step(index, totals):
            at = rows_at(index, self.chunk)
            inv = self.stat(at, 5)
            normed = (self.resid[at, :] - self.stat(at, 4)) * inv
            upstream = self.pre[at, :]
            d_resid = self.d_mlp[at, :].astype(F32) + norm_back(upstream, normed, inv, gain)
            self.d_resid[at, :] = d_resid
            self.d_mlp[at, :] = d_resid.astype(BF16)
            return (
                totals[0] + fold(upstream * normed),
                totals[1] + fold(upstream),
                totals[2] + fold(d_resid),
            )

        blank = jnp.zeros((8, self.width), F32)
        totals = lax.fori_loop(0, self.steps, step, (blank, blank, blank), unroll=7)
        for row, total in zip((5, 6, 4), totals):
            self.put_sum(row, total)

    def proj_back(self):
        size = self.width // self.gp.shape[0]
        product = dot_rows(self.att[...], self.d_mlp[...])
        for index in range(self.gp.shape[0]):
            put_blocks(self.gp, index, product[index * size : (index + 1) * size])
        self.att[...] = dot_cols(self.d_mlp[...], self.wp[...]).astype(BF16)
        self.d_bias[...] = jnp.zeros_like(self.d_bias)

    def attend_back(self, first, last):
        def step(index):
            shift_both(self.d_bias, False)
            attention_backward(
                last - 1 - index, self.qkv, self.att, self.probs, self.d_bias, self.qkv
            )

        each(last - first, step)

    def bias_back(self):
        self.put_table(reduce_bias(self.d_bias, self.spread, self.heads))
        ones = jnp.full((8, self.rows), 1.0, BF16)
        self.put_sum(8, dot(ones, self.qkv[0]), True)
        self.put_sum(9, dot(ones, self.qkv[2]), True)

    def qkv_weight_back(self):
        for part in range(3):
            put_columns(self.gqkv, part, dot_rows(self.attn_in[...], self.qkv[part]))

    def qkv_back(self):
        self.pre[...] = (
            dot_cols(self.qkv[0], self.wqkv[0])
            + dot_cols(self.qkv[1], self.wqkv[1])
            + dot_cols(self.qkv[2], self.wqkv[2])
        )

    def attn_back(self):
        gain = self.gain(2, self.width)

        def step(index, totals):
            at = rows_at(index, self.chunk)
            inv = self.stat(at, 3)
            normed = (self.section[at, :].astype(F32) - self.stat(at, 2)) * inv
            upstream = self.pre[at, :]
            d_section = self.d_resid[at, :] + norm_back(upstream, normed, inv, gain)
            self.d_mlp[at, :] = d_section.astype(BF16)
            return totals[0] + fold(upstream * normed), totals[1] + fold(upstream)

        blank = jnp.zeros((8, self.width), F32)
        totals = lax.fori_loop(0, self.steps, step, (blank, blank), unroll=7)
        self.put_sum(2, totals[0])
        self.put_sum(3, totals[1])

    def merge_weight_back(self):
        put_columns(self.gm, 0, dot_rows(self.merged[...], self.d_mlp[...]))

    def merge_in_back(self):
        self.d_in[...] = dot_cols(self.d_mlp[...], self.wm[...])

    def merge_back(self, first, last, totals=None):
        gain = self.gain(0, self.wide)

        def step(index, totals):
            at = rows_at(first + index, self.chunk)
            inv = self.stat(at, 1)
            normed = (self.x[at, :].astype(F32) - self.stat(at, 0)) * inv
            upstream = self.d_in[at, :]
            self.d_in[at, :] = norm_back(upstream, normed, inv, gain)
            return totals[0] + fold(upstream * normed), totals[1] + fold(upstream)

        blank = jnp.zeros((8, self.wide), F32)
        totals = lax.fori_loop(0, last - first, step, totals or (blank, blank), unroll=7)
        if last == self.steps:
            self.put_sum(0, totals[0])
            self.put_sum(1, totals[1])
        return totals

    def put_sum(self, row, values, summed=False):
        values = values[0:1] if summed else sum_rows(values)
        for block in range(values.shape[1] // LANES):
            place = SUM_ROWS[row] + block
            self.sums[place : place + 1, :] = values[:, block * LANES : (block + 1) * LANES]

    def put_up_sum(self, index, total):
        values = sum_rows(total)
        blocks = self.tile // LANES
        for block in range(blocks):
            place = SUM_ROWS[10] + index * blocks + block
            self.sums[pl.ds(place, 1), :] = values[:, block * LANES : (block + 1) * LANES]

    def put_table(self, values):
        for half in range(2):
            place = SUM_ROWS[11] + half * self.heads
            self.sums[place : place + self.heads, :] = values[:, half * LANES : (half + 1) * LANES]


SUM_ROWS = (0, 8, 16, 20, 24, 28, 32, 36, 40, 44, 48, 64)
SUM_SIZE = 128


def put_blocks(ref, shard, values):
    rows = values.shape[0]
    for block in range(values.shape[1] // LANES):
        at = pl.ds(block * rows, rows)
        ref[shard, at, :] = values[:, block * LANES : (block + 1) * LANES].astype(BF16)


def put_columns(ref, part, values):
    rows = values.shape[0]
    for shard in range(ref.shape[0]):
        piece = values[:, shard * LANES : (shard + 1) * LANES]
        ref[shard, part * rows : (part + 1) * rows, :] = piece.astype(BF16)


def local_scratch(rows, wide, width, units):
    heads = width // HD
    windows = rows // TOK
    return dict(
        merged=pltpu.VMEM((rows, wide), BF16),
        section=pltpu.VMEM((rows, width), BF16),
        attn_in=pltpu.VMEM((rows, width), BF16),
        qkv=pltpu.VMEM((3, rows, width), BF16),
        probs=pltpu.VMEM((windows, SPAN, heads * SPAN), BF16),
        att=pltpu.VMEM((rows, width), BF16),
        resid=pltpu.VMEM((rows, width), F32),
        mlp_in=pltpu.VMEM((rows, width), BF16),
        hidden=pltpu.VMEM((rows, units), BF16),
        slope=pltpu.VMEM((rows, units), BF16),
        pre=pltpu.VMEM((rows, width), F32),
        d_mlp=pltpu.VMEM((rows, width), BF16),
        d_pre=pltpu.VMEM((rows, units), BF16),
        d_resid=pltpu.VMEM((rows, width), F32),
        gains=pltpu.VMEM((8, wide), F32),
        stats=pltpu.VMEM((rows, 8), F32),
        bias=pltpu.VMEM((SPAN, heads * SPAN), F32),
        d_bias=pltpu.VMEM((SPAN, heads * SPAN), F32),
        spread=pltpu.VMEM((SPAN * heads, LANES), F32),
    )


MESH_ID = pl.DeviceIdType.MESH


class Links:
    def __init__(self, send_sems, recv_sems, plan):
        self.send_sems, self.recv_sems, self.plan = send_sems, recv_sems, plan
        self.sent = []
        self.sp, self.tp = lax.axis_index("sp"), lax.axis_index("tp")

    def place(self, way):
        kind, distance = way
        if kind == "tp":
            return self.sp, self.tp ^ distance
        return self.sp ^ distance, self.tp

    def copy(self, name, way, source, target):
        slot = self.plan.setdefault(name, len(self.plan))
        return pltpu.make_async_remote_copy(
            src_ref=source,
            dst_ref=target,
            send_sem=self.send_sems.at[slot],
            recv_sem=self.recv_sems.at[slot],
            device_id=self.place(way),
            device_id_type=MESH_ID,
        )

    def send(self, name, way, source, target):
        copy = self.copy(name, way, source, target)
        copy.start()
        self.sent.append(copy)

    def receive(self, name, way, target):
        self.copy(name, way, target, target).wait_recv()

    def keep(self, name, source, target):
        slot = self.plan.setdefault(name, len(self.plan))
        copy = pltpu.make_async_copy(source, target, self.recv_sems.at[slot])
        copy.start()
        return copy

    def greet(self, ways):
        barrier = pltpu.get_barrier_semaphore()
        for way in ways:
            pl.semaphore_signal(
                barrier, inc=1, device_id=self.place(way), device_id_type=MESH_ID
            )
        pl.semaphore_wait(barrier, len(ways))

    def drain(self):
        for copy in self.sent:
            copy.wait_send()


CORE, ACROSS, BESIDE = ("tp", 1), ("tp", 2), ("sp", 1)


def far_ways(sp_size):
    return [("sp", 2 * step) for step in range(1, sp_size // 2)]


class Gather:
    def __init__(self, links, name, own, whole, view, split):
        self.links, self.name, self.own, self.whole = links, name, own, whole
        self.view, self.split = view, split
        self.half = links.sp & 1

    def part(self, shard, half=None):
        return self.view(self.whole, shard, half)

    def label(self, step):
        return (self.name, step)

    def start(self):
        links = self.links
        mine = links.tp
        self.local = links.keep(self.label("own"), self.own, self.part(mine))
        half = self.half if self.split else None
        links.send(
            self.label("x"), ACROSS, self.view(self.own, None, half), self.part(mine, half)
        )
        links.send(self.label("c"), CORE, self.own, self.part(mine))

    def forward(self):
        links = self.links
        other = links.tp ^ 2
        half = self.half if self.split else None
        block = self.part(other, half)
        links.receive(self.label("x"), ACROSS, block)
        if self.split:
            links.send(self.label("y"), BESIDE, block, block)
        links.send(self.label("xc"), CORE, block, block)

    def forward_beside(self):
        if self.split:
            links = self.links
            block = self.part(links.tp ^ 2, 1 - self.half)
            links.receive(self.label("y"), BESIDE, block)
            links.send(self.label("yc"), CORE, block, block)

    def finish(self):
        links = self.links
        self.local.wait()
        links.receive(self.label("c"), CORE, self.part(links.tp ^ 1))
        half = self.half if self.split else None
        links.receive(self.label("xc"), CORE, self.part(links.tp ^ 3, half))
        if self.split:
            links.receive(self.label("yc"), CORE, self.part(links.tp ^ 3, 1 - self.half))


def column_view(size, halves):
    def view(ref, shard, half):
        rank = len(ref.shape)
        rows = ref.shape[rank - 2]
        at = slice(None) if half is None else pl.ds(
            pl.multiple_of(half * (rows // 2), 16), rows // 2
        )
        lanes = slice(None) if shard is None else pl.ds(pl.multiple_of(shard * size, LANES), size)
        return ref.at[(slice(None),) * (rank - 2) + (at, lanes)]

    return view


def row_view(size):
    def view(ref, shard, half):
        start = 0 if shard is None else shard * size
        if half is None:
            return ref.at[pl.ds(start, size), :]
        start = start + half * (size // 2)
        return ref.at[pl.ds(pl.multiple_of(start, 16), size // 2), :]

    return view


def lead_view(ref, shard, half):
    return ref if shard is None else ref.at[shard]


def add_rows(target, start, rows, terms, chunk=128):
    chunk = math.gcd(rows, chunk)

    def step(index):
        offset = index * chunk

        def at(first):
            return pl.ds(pl.multiple_of(first + offset, 16), chunk)

        total = None
        for ref, first in terms:
            value = ref[at(first), :].astype(F32)
            total = value if total is None else total + value
        target[at(start), :] = total.astype(target.dtype)

    each(rows // chunk, step)


class Reduce:
    def __init__(self, links, name, grads, core_in, first_in, second_in, far_in, result, group,
                 across_first):
        self.links, self.name, self.grads = links, name, grads
        self.core_in, self.first_in, self.second_in = core_in, first_in, second_in
        self.far_in, self.result, self.group = far_in, result, group
        self.rows = grads.shape[1]
        self.half_rows = self.rows // 2
        self.piece = self.half_rows // group
        self.half = links.sp & 1
        self.seat = links.sp >> 1
        self.across = links.tp >> 1
        if across_first:
            middle = [self.core_add_across, self.across_beside, self.beside_last]
        else:
            middle = [self.core_add_beside, self.beside_across, self.across_last]
        self.steps = [self.core_send] + middle + [self.far_add, self.far_done, self.beside_done]

    def run(self):
        self.steps.pop(0)()

    def label(self, *step):
        return (self.name,) + step

    def rows_of(self, ref, half, piece=None):
        if piece is None:
            return ref.at[pl.ds(pl.multiple_of(half * self.half_rows, 16), self.half_rows), :]
        start = half * self.half_rows + piece * self.piece
        return ref.at[pl.ds(pl.multiple_of(start, 16), self.piece), :]

    def core_send(self):
        links = self.links
        for across in range(2):
            links.send(
                self.label("c", across), CORE, self.grads.at[(links.tp & 1) ^ 1 | 2 * across],
                self.core_in.at[across],
            )

    def core_receive(self):
        for across in range(2):
            self.links.receive(self.label("c", across), CORE, self.core_in.at[across])

    def core_add_across(self):
        self.core_receive()
        other = self.links.tp ^ 2
        block = self.grads.at[other]
        add_rows(block, 0, self.rows, [(block, 0), (self.core_in.at[self.across ^ 1], 0)])
        self.links.send(self.label("x"), ACROSS, block, self.first_in)

    def across_beside(self):
        links = self.links
        links.receive(self.label("x"), ACROSS, self.first_in)
        block = self.grads.at[links.tp]
        terms = [(block, 0), (self.core_in.at[self.across], 0), (self.first_in, 0)]
        add_rows(block, 0, self.rows, terms)
        links.send(
            self.label("y"), BESIDE, self.rows_of(block, 1 - self.half), self.second_in
        )

    def beside_last(self):
        self.links.receive(self.label("y"), BESIDE, self.second_in)
        self.add_and_spread([(self.second_in, 0)])

    def core_add_beside(self):
        links = self.links
        self.core_receive()
        for across in range(2):
            block = self.grads.at[(links.tp & 1) | 2 * across]
            add_rows(block, 0, self.rows, [(block, 0), (self.core_in.at[across], 0)])
            links.send(
                self.label("y", across), BESIDE, self.rows_of(block, 1 - self.half),
                self.first_in.at[across],
            )

    def beside_across(self):
        links = self.links
        for across in range(2):
            links.receive(self.label("y", across), BESIDE, self.first_in.at[across])
        block = self.grads.at[links.tp ^ 2]
        mine = self.half * self.half_rows
        terms = [(block, mine), (self.first_in.at[self.across ^ 1], 0)]
        add_rows(block, mine, self.half_rows, terms)
        links.send(self.label("x"), ACROSS, self.rows_of(block, self.half), self.second_in)

    def across_last(self):
        self.links.receive(self.label("x"), ACROSS, self.second_in)
        self.add_and_spread([(self.first_in.at[self.across], 0), (self.second_in, 0)])

    def add_and_spread(self, terms):
        block = self.grads.at[self.links.tp]
        mine = self.half * self.half_rows
        add_rows(block, mine, self.half_rows, [(block, mine)] + terms)
        for step in range(1, self.group):
            self.links.send(
                self.label("z", step), ("sp", 2 * step),
                self.rows_of(block, self.half, self.seat ^ step), self.far_in.at[step - 1],
            )

    def far_add(self):
        links = self.links
        block = self.grads.at[links.tp]
        mine = self.half * self.half_rows + self.seat * self.piece
        terms = [(block, mine)]
        for step in range(1, self.group):
            links.receive(self.label("z", step), ("sp", 2 * step), self.far_in.at[step - 1])
            terms.append((self.far_in.at[step - 1], 0))
        add_rows(self.result, mine, self.piece, terms)
        done = self.rows_of(self.result, self.half, self.seat)
        for step in range(1, self.group):
            links.send(self.label("a", step), ("sp", 2 * step), done, done)

    def far_done(self):
        links = self.links
        for step in range(1, self.group):
            links.receive(
                self.label("a", step), ("sp", 2 * step),
                self.rows_of(self.result, self.half, self.seat ^ step),
            )
        done = self.rows_of(self.result, self.half)
        links.send(self.label("b"), BESIDE, done, done)

    def beside_done(self):
        self.links.receive(
            self.label("b"), BESIDE, self.rows_of(self.result, 1 - self.half)
        )


class Total:
    def __init__(self, links, name, stages, inboxes, far_in, result, group):
        self.links, self.name, self.stages, self.inboxes = links, name, stages, inboxes
        self.far_in, self.result, self.group = far_in, result, group
        self.piece = result.shape[0] // group
        self.seat = links.sp >> 1
        self.ways = (CORE, ACROSS, BESIDE)
        self.steps = [
            functools.partial(self.exchange, 0), functools.partial(self.add, 0),
            functools.partial(self.add, 1), functools.partial(self.add, 2), self.far_add,
            self.far_done,
        ]

    def run(self):
        self.steps.pop(0)()

    def label(self, *step):
        return (self.name,) + step

    def at(self, ref, piece):
        return ref.at[pl.ds(pl.multiple_of(piece * self.piece, 8), self.piece), :]

    def exchange(self, stage):
        self.links.send(
            self.label("e", stage), self.ways[stage], self.stages.at[stage],
            self.inboxes.at[stage],
        )

    def add(self, stage):
        self.links.receive(self.label("e", stage), self.ways[stage], self.inboxes.at[stage])
        self.stages[stage + 1] = self.stages[stage] + self.inboxes[stage]
        if stage < 2:
            self.exchange(stage + 1)
            return
        for step in range(1, self.group):
            self.links.send(
                self.label("z", step), ("sp", 2 * step),
                self.at(self.stages.at[3], self.seat ^ step), self.far_in.at[step - 1],
            )

    def far_add(self):
        total = self.at(self.stages.at[3], self.seat)[...]
        for step in range(1, self.group):
            self.links.receive(self.label("z", step), ("sp", 2 * step), self.far_in.at[step - 1])
            total = total + self.far_in[step - 1]
        done = self.at(self.result, self.seat)
        done[...] = total
        for step in range(1, self.group):
            self.links.send(self.label("a", step), ("sp", 2 * step), done, done)

    def far_done(self):
        for step in range(1, self.group):
            self.links.receive(
                self.label("a", step), ("sp", 2 * step), self.at(self.result, self.seat ^ step)
            )


UNITS = (
    ("gd", 0, 1024, True), ("gd", 1024, 1024, True),
    ("gu", 0, 1024, True), ("gu", 1024, 1024, True),
    ("gp", 0, 512, True),
    ("gqkv", 0, 1024, True), ("gqkv", 1024, 512, False),
    ("gm", 0, 512, True), ("gm", 512, 512, False),
)
GRADS = ("gd", "gu", "gp", "gqkv", "gm")
WEIGHTS = ("wm", "wqkv", "wp", "wu", "wd")
VECTORS = (
    "merge_gain", "merge_bias", "attn_gain", "attn_bias", "mlp_gain", "mlp_bias", "proj_bias",
    "down_bias",
)
INPUTS = (
    ("valid", "edge", "x", "grad_out", "rel", "qv", "ub") + VECTORS
    + tuple("own_" + name for name in WEIGHTS)
)
OUTPUTS = ("h_out", "h_d_in") + tuple("r_" + name for name in GRADS) + ("r_sums",)


def unit_name(name, first):
    return name + str(first)


def whole_kernel(names, group, plan, *refs):
    refs = dict(zip(names, refs, strict=True))
    links = Links(refs.pop("send_sems"), refs.pop("recv_sems"), plan)
    own_pack, packs = refs.pop("pack"), refs.pop("packs")
    rel, qv, ub = refs.pop("rel"), refs.pop("qv"), refs.pop("ub")
    heads_here = rel.shape[0]
    own_pack[...] = jnp.zeros_like(own_pack)
    own_pack[0:heads_here, 0:REL] = rel[...].astype(F32)
    own_pack[4:6, 0:LANES] = qv[...].astype(F32)
    for block in range(ub.shape[0]):
        lanes = slice(block * LANES, (block + 1) * LANES)
        own_pack[6:7, lanes] = ub[block : block + 1, :].astype(F32)

    own = {name: refs.pop("own_" + name) for name in WEIGHTS}
    whole = {name: refs[name] for name in WEIGHTS}
    for part, name in enumerate(("wq", "wk", "wv")):
        own[name], whole[name] = own["wqkv"].at[part], whole["wqkv"].at[part]
    columns = column_view(LANES, True)
    views = dict(
        wm=columns, wq=columns, wk=columns, wv=columns, wp=row_view(own["wp"].shape[0]),
        wu=column_view(own["wu"].shape[1], True), wd=row_view(own["wd"].shape[0]),
    )
    gathers = {"pack": Gather(links, "pack", own_pack, packs, lead_view, False)}
    for name in ("wm", "wq", "wk", "wv", "wp", "wu", "wd"):
        gathers[name] = Gather(links, name, own[name], whole[name], views[name], name != "wm")
    links.greet([CORE, ACROSS, BESIDE] + far_ways(2 * group))
    for gather in gathers.values():
        gather.start()

    results = {name: refs.pop("r_" + name) for name in GRADS}
    reduces = {}
    for name, first, rows, across_first in UNITS:
        unit = unit_name(name, first)
        part = pl.ds(first, rows)
        reduces.setdefault(name, []).append(
            Reduce(
                links, unit, refs[name].at[:, part, :], refs.pop("c_" + unit),
                refs.pop("f_" + unit), refs.pop("s_" + unit), refs.pop("z_" + unit),
                results[name].at[part, :], group, across_first,
            )
        )
    stages, inboxes = refs.pop("sum_stages"), refs.pop("sum_inboxes")
    refs["sums"] = stages.at[0]
    total = Total(links, "sums", stages, inboxes, refs.pop("sum_far"), refs.pop("r_sums"), group)
    shards = packs.shape[0]

    def table():
        return jnp.concatenate(
            [packs[shard, 0:heads_here, : 2 * LANES] for shard in range(shards)], axis=0
        )

    def qkv_bias(part):
        row = 4 if part == 0 else 5
        return jnp.concatenate(
            [packs[shard, row : row + 1, :LANES] for shard in range(shards)], axis=1
        )

    def up_bias(index):
        return packs[index, 6:7, :]

    refs["vectors"] = [refs.pop(name) for name in VECTORS]
    refs.update(table=table, qkv_bias=qkv_bias, up_bias=up_bias)
    h_out, h_d_in = refs.pop("h_out"), refs.pop("h_d_in")
    local = Local(refs, links.tp * (refs["x"].shape[0] // TOK))

    def forward(*names):
        for name in names:
            gathers[name].forward()

    def beside(*names):
        for name in names:
            gathers[name].forward_beside()

    def ready(*names):
        for name in names:
            gathers[name].finish()

    def run(*units):
        for name, index in units:
            reduces[name][index].run()

    gd0, gd1, gu0, gu1, gp0 = ("gd", 0), ("gd", 1), ("gu", 0), ("gu", 1), ("gp", 0)
    qkv0, qkv1, gm0, gm1 = ("gqkv", 0), ("gqkv", 1), ("gm", 0), ("gm", 1)
    windows, steps = local.windows, local.steps

    stages[0] = jnp.zeros_like(stages[0])
    local.spread_vectors()
    local.merge_norm()
    local.prepare()
    forward("pack")
    local.grad_rows()
    ready("pack")
    local.table_bias()
    forward("wm")
    ready("wm")
    local.merge()
    forward("wq")
    local.attn_norm()
    forward("wk", "wv")
    beside("wq")
    ready("wq")
    local.project(0)
    beside("wk")
    ready("wk")
    local.project(1)
    beside("wv")
    ready("wv")
    local.project(2)
    forward("wp")

    def attend(first, last):
        local.attend(first * windows // 8, last * windows // 8)

    attend(0, 2)
    beside("wp")
    forward("wu")
    attend(2, 4)
    ready("wp")
    forward("wd")
    attend(4, 6)
    beside("wu", "wd")
    attend(6, 8)
    local.attn_out()
    local.mlp_norm()
    ready("wu")
    local.up()
    ready("wd")

    def attend_back(index):
        local.attend_back((7 - index) * windows // 8, (8 - index) * windows // 8)

    tiles = local.units // local.tile
    local.down_weight_back()
    run(gd0, gd1)
    local.hidden_back(0, tiles // 2)
    run(gd0, gd1)
    local.hidden_back(tiles // 2, tiles)
    run(gu0, gu1)
    local.up_back()
    run(gu0, gu1)
    local.mlp_back()
    run(gd0)
    local.proj_back()
    run(gp0)
    attend_back(0)
    run(gp0, gd1)
    attend_back(1)
    run(gd0)
    attend_back(2)
    run(gu0, gd1)
    attend_back(3)
    run(gd0)
    attend_back(4)
    run(gu1, gu0)
    attend_back(5)
    run(gd1, gd0, gp0)
    attend_back(6)
    run(gu1, gu0)
    attend_back(7)
    run(gd1, gp0)
    local.qkv_weight_back()
    run(qkv0, qkv1, gu1, gu0)
    local.qkv_back()
    run(qkv0, qkv1, gp0)
    local.attn_back()
    run(gd0, gu1, gd1)
    local.merge_weight_back()
    run(gm0, gm1, qkv1, gp0)
    local.merge_in_back()
    run(gm0, gm1)
    local.bias_back()
    run(qkv0, qkv1)
    local.down()
    local.finish()
    done = [links.keep("out", local.out, h_out)]
    run(gm1, gm0)
    totals = local.merge_back(0, 4 * steps // 7)
    run(qkv0, qkv1, gm1, gm0)
    local.merge_back(4 * steps // 7, steps, totals)
    done.append(links.keep("d_in", local.d_in, h_d_in))
    total.run()
    run(qkv0, qkv1)
    total.run()
    run(gm0, gm1)
    total.run()
    run(qkv0, qkv1, gu0, gu1, gp0)
    total.run()
    run(gm0, gm1)
    total.run()
    run(qkv0, gm0, gm1)
    total.run()
    for copy in done:
        copy.wait()
    links.drain()


def finish_kernel(names, *refs):
    refs = dict(zip(names, refs, strict=True))
    tp = lax.axis_index("tp")
    pieces, number = [], 0
    for name in ("d_in", "out"):
        source, target, held = refs["h_" + name], refs["o_" + name], refs["v_" + name]
        size = held.shape[0] // PIECES
        for index in range(PIECES):
            at = pl.ds(index * size, size)
            sems = refs["sems"].at[number], refs["sems"].at[number + 1]
            number += 2
            pieces.append(
                (
                    pltpu.make_async_copy(source.at[at], held.at[at], sems[0]),
                    pltpu.make_async_copy(held.at[at], target.at[at], sems[1]),
                )
            )
    for incoming, _ in pieces:
        incoming.start()
    sums = refs["r_sums"]
    for row, name in enumerate(
        ("merge_gain", "merge_bias", "attn_gain", "attn_bias", "proj_bias", "mlp_gain",
         "mlp_bias", "down_bias")
    ):
        out = refs["o_" + name]
        out[...] = sums[SUM_ROWS[row] : SUM_ROWS[row] + out.shape[0], :]
    for index in range(2):
        refs["o_qv"][index : index + 1, :] = sums[pl.ds(SUM_ROWS[8 + index] + tp, 1), :]
    blocks = refs["o_ub"].shape[0]
    for index in range(blocks):
        refs["o_ub"][index : index + 1, :] = sums[
            pl.ds(SUM_ROWS[10] + tp * blocks + index, 1), :
        ]
    mine = refs["o_rel"].shape[0]
    heads = SHARDS * mine
    for index in range(mine):
        first = SUM_ROWS[11] + tp * mine + index
        low, high = sums[pl.ds(first, 1), :], sums[pl.ds(first + heads, 1), :]
        refs["o_rel"][index : index + 1, :LANES] = low
        refs["o_rel"][index : index + 1, LANES:] = high[:, : REL - LANES]
    for name in GRADS:
        result, out = refs["r_" + name], refs["o_" + name]
        if len(out.shape) == 3:
            rows = out.shape[1]
            for part in range(out.shape[0]):
                out[part] = result[part * rows : (part + 1) * rows, :].astype(F32)
        else:
            rows = out.shape[0]
            for block in range(out.shape[1] // LANES):
                lanes = slice(block * LANES, (block + 1) * LANES)
                out[:, lanes] = result[block * rows : (block + 1) * rows, :].astype(F32)
    for incoming, outgoing in pieces:
        incoming.wait()
        outgoing.start()
    for _, outgoing in pieces:
        outgoing.wait()


SHARDS = 4
PIECES = 7
VMEM_SPEC = pl.BlockSpec(memory_space=pltpu.VMEM)
SMEM_SPEC = pl.BlockSpec(memory_space=pltpu.SMEM)
HBM_SPEC = pl.BlockSpec(memory_space=pl.ANY)


def whole_call(group, inputs):
    rows, wide = inputs["x"].shape
    width = inputs["own_wu"].shape[0]
    units = SHARDS * inputs["own_wu"].shape[1]
    depth = dict(gd=units, gu=units, gp=width, gqkv=3 * width, gm=wide)
    scratch = local_scratch(rows, wide, width, units)
    scratch.update(
        wm=pltpu.VMEM((wide, width), BF16),
        wqkv=pltpu.VMEM((3, width, width), BF16),
        wp=pltpu.VMEM((width, width), BF16),
        wu=pltpu.VMEM((width, units), BF16),
        wd=pltpu.VMEM((units, width), BF16),
        pack=pltpu.VMEM((8, units // SHARDS), F32),
        packs=pltpu.VMEM((SHARDS, 8, units // SHARDS), F32),
        out=pltpu.VMEM((rows, width), BF16),
        d_in=pltpu.VMEM((rows, wide), F32),
    )
    for name in GRADS:
        scratch[name] = pltpu.VMEM((SHARDS, depth[name], LANES), BF16)
    for name, first, size, across_first in UNITS:
        unit = unit_name(name, first)
        half = size // 2
        scratch["c_" + unit] = pltpu.VMEM((2, size, LANES), BF16)
        first_shape = (size, LANES) if across_first else (2, half, LANES)
        scratch["f_" + unit] = pltpu.VMEM(first_shape, BF16)
        scratch["s_" + unit] = pltpu.VMEM((half, LANES), BF16)
        scratch["z_" + unit] = pltpu.VMEM((group - 1, half // group, LANES), BF16)
    scratch["sum_stages"] = pltpu.VMEM((4, SUM_SIZE, LANES), F32)
    scratch["sum_inboxes"] = pltpu.VMEM((3, SUM_SIZE, LANES), F32)
    scratch["sum_far"] = pltpu.VMEM((group - 1, SUM_SIZE // group, LANES), F32)
    count = 8 * 6 + len(UNITS) * (5 + 2 * group) + 6 + 2 * group
    scratch["send_sems"] = pltpu.SemaphoreType.DMA((count,))
    scratch["recv_sems"] = pltpu.SemaphoreType.DMA((count,))
    outs = dict(
        h_out=jax.ShapeDtypeStruct((rows, width), BF16),
        h_d_in=jax.ShapeDtypeStruct((rows, wide), F32),
        r_sums=jax.ShapeDtypeStruct((SUM_SIZE, LANES), F32),
    )
    for name in GRADS:
        outs["r_" + name] = jax.ShapeDtypeStruct((depth[name], LANES), BF16)
    names = INPUTS + OUTPUTS + tuple(scratch)
    in_vmem = 5 + len(VECTORS)
    return pl.pallas_call(
        functools.partial(whole_kernel, names, group, {}),
        out_shape=[outs[name] for name in OUTPUTS],
        in_specs=[SMEM_SPEC] * 2 + [VMEM_SPEC] * in_vmem + [HBM_SPEC] * len(WEIGHTS),
        out_specs=[HBM_SPEC] * 2 + [VMEM_SPEC] * (len(OUTPUTS) - 2),
        scratch_shapes=list(scratch.values()),
        compiler_params=pltpu.CompilerParams(
            vmem_limit_bytes=63 * MIB, collective_id=0, has_side_effects=True
        ),
    )(*[inputs[name] for name in INPUTS])


def finish_call(results, shapes):
    names = OUTPUTS + tuple("o_" + name for name in shapes) + ("v_out", "v_d_in", "sems")
    return pl.pallas_call(
        functools.partial(finish_kernel, names),
        out_shape=list(shapes.values()),
        in_specs=[HBM_SPEC] * 2 + [VMEM_SPEC] * (len(OUTPUTS) - 2),
        out_specs=[HBM_SPEC] * 2 + [VMEM_SPEC] * (len(shapes) - 2),
        scratch_shapes=[
            pltpu.VMEM(shapes["out"].shape, BF16),
            pltpu.VMEM(shapes["d_in"].shape, F32),
            pltpu.SemaphoreType.DMA((4 * PIECES,)),
        ],
        compiler_params=pltpu.CompilerParams(vmem_limit_bytes=63 * MIB),
    )(*results)


def on_device(
    inputs, grad_out, window_valid, window_edge, merge_gain, merge_bias, merge_weight, attn_gain,
    attn_bias, query_key_value_weight, qv_bias, rel_table, proj_weight, proj_bias, mlp_gain,
    mlp_bias, up_weight, up_bias, down_weight, down_bias,
):
    vectors = dict(
        merge_gain=merge_gain, merge_bias=merge_bias, attn_gain=attn_gain, attn_bias=attn_bias,
        mlp_gain=mlp_gain, mlp_bias=mlp_bias, proj_bias=proj_bias, down_bias=down_bias,
    )
    blocks = {name: vector.reshape(-1, LANES) for name, vector in vectors.items()}
    arrays = dict(
        valid=window_valid, edge=window_edge, x=inputs, grad_out=grad_out, rel=rel_table.T,
        qv=qv_bias, ub=up_bias.reshape(-1, LANES), own_wm=merge_weight,
        own_wqkv=jnp.transpose(query_key_value_weight, (1, 0, 2)), own_wp=proj_weight,
        own_wu=up_weight, own_wd=down_weight, **blocks,
    )
    results = whole_call(lax.axis_size("sp") // 2, arrays)
    f32_like = lambda array: jax.ShapeDtypeStruct(array.shape, F32)
    shapes = dict(
        out=jax.ShapeDtypeStruct(grad_out.shape, BF16), d_in=f32_like(inputs),
        gm=f32_like(merge_weight), gqkv=f32_like(arrays["own_wqkv"]), gp=f32_like(proj_weight),
        gu=f32_like(up_weight), gd=f32_like(down_weight), qv=f32_like(qv_bias),
        rel=f32_like(arrays["rel"]), ub=f32_like(arrays["ub"]),
        **{name: f32_like(block) for name, block in blocks.items()},
    )
    done = dict(zip(shapes, finish_call(results, shapes), strict=True))
    flat = lambda name: done[name].reshape(-1)
    return (
        done["out"], done["d_in"], flat("merge_gain"), flat("merge_bias"), done["gm"],
        flat("attn_gain"), flat("attn_bias"), jnp.transpose(done["gqkv"], (1, 0, 2)), done["qv"],
        done["rel"].T, done["gp"], flat("proj_bias"), flat("mlp_gain"), flat("mlp_bias"),
        done["gu"], flat("ub"), done["gd"], flat("down_bias"),
    )


def solution(mesh):
    placed = (
        P(("sp", "tp"), None),
        P(("sp", "tp"), None),
        P("sp"),
        P("sp"),
        P(),
        P(),
        P(None, "tp"),
        P(),
        P(),
        P(None, None, "tp"),
        P(None, "tp"),
        P(None, "tp"),
        P("tp", None),
        P(),
        P(),
        P(),
        P(None, "tp"),
        P("tp"),
        P("tp", None),
        P(),
    )
    return jax.shard_map(
        on_device,
        mesh=mesh,
        in_specs=placed,
        out_specs=(
            P(("sp", "tp"), None),
            P(("sp", "tp"), None),
            P(),
            P(),
            P(None, "tp"),
            P(),
            P(),
            P(None, None, "tp"),
            P(None, "tp"),
            P(None, "tp"),
            P("tp", None),
            P(),
            P(),
            P(),
            P(None, "tp"),
            P("tp"),
            P("tp", None),
            P(),
        ),
        check_vma=False,
    )
```

```python
import functools
import math

import jax
import jax.numpy as jnp
from jax import lax
from jax.experimental import pallas as pl
from jax.experimental.pallas import tpu as pltpu
from jax.sharding import PartitionSpec as P

SIDE = 7
TOK = SIDE * SIDE
REL_SIDE = 2 * SIDE - 1
REL = REL_SIDE * REL_SIDE
SPAN = 64
GROUP = 4
HD = 32
LANES = 128
EPSILON = 1e-05
NEG_FILL = -1000000000.0
MIB = 1 << 20
F32 = jnp.float32
BF16 = jnp.bfloat16


def dot(left, right):
    return jnp.dot(left, right, preferred_element_type=F32)


def dot_cols(left, right):
    return lax.dot_general(left, right, (((1,), (1,)), ((), ())), preferred_element_type=F32)


def dot_rows(left, right):
    return lax.dot_general(left, right, (((0,), (0,)), ((), ())), preferred_element_type=F32)


def rows_at(index, size):
    return pl.ds(pl.multiple_of(index * size, size), size)


def each(count, body, unroll=1):
    def step(index, carry):
        body(index)
        return carry

    lax.fori_loop(0, count, step, 0, unroll=unroll)


def fold(values):
    total = values[0:8]
    for start in range(8, values.shape[0], 8):
        total = total + values[start : start + 8]
    return total


def iota(shape, dim):
    return lax.broadcasted_iota(jnp.int32, shape, dim)


def norm_rows(values):
    mean = jnp.mean(values, -1, keepdims=True)
    centred = values - mean
    inv = lax.rsqrt(jnp.mean(centred * centred, -1, keepdims=True) + EPSILON)
    return centred * inv, mean, inv


def norm_back(upstream, normed, inv, gain):
    scaled = upstream * gain
    return inv * (
        scaled
        - jnp.mean(scaled, -1, keepdims=True)
        - normed * jnp.mean(scaled * normed, -1, keepdims=True)
    )


def gelu_both(values):
    size = jnp.abs(values) * 0.7071067811865476
    bell = jnp.exp(-size * size)
    t = 1.0 / (1.0 + 0.3275911 * size)
    poly = t * (
        0.254829592
        + t * (-0.284496736 + t * (1.421413741 + t * (-1.453152027 + t * 1.061405429)))
    )
    tail = 0.5 * poly * bell
    phi = jnp.where(values >= 0, 1.0 - tail, tail)
    return values * phi, phi + values * bell * 0.3989422804014327


def window_row_col(index):
    row = (index * 37) >> 8
    return row, index - SIDE * row


def region_ids(index, edge, outside):
    row, col = window_row_col(index)
    high = SIDE - SIDE // 2
    region = (edge & 1) * (col >= high).astype(jnp.int32) + 2 * (edge >> 1) * (
        row >= high
    ).astype(jnp.int32)
    return jnp.where((index >= 0) & (index < TOK), region, outside)


def head_masks():
    lane = iota((1, LANES), 1)
    return [((lane >> 5) == head).astype(F32).astype(BF16) for head in range(GROUP)]


def spread_heads(block, masks):
    return jnp.concatenate([block * mask for mask in masks], axis=0)


def pick_heads(product):
    lane = iota((SPAN, LANES), 1)
    result = product[3 * SPAN : 4 * SPAN]
    for head in (2, 1, 0):
        result = jnp.where(
            lane < (head + 1) * HD, product[head * SPAN : (head + 1) * SPAN], result
        )
    return result


def same_head(rows, columns):
    return (
        (iota((rows, columns), 0) // (rows // GROUP))
        == (iota((rows, columns), 1) // (columns // GROUP))
    ).astype(F32).astype(BF16)


def offset_select(half):
    place = iota((LANES, LANES), 0)
    lane = iota((LANES, LANES), 1)
    token = lane - half * SPAN
    row, col = window_row_col(token & (SPAN - 1))
    wanted = (SIDE - 1) * (REL_SIDE + 1) - (REL_SIDE * row + col)
    hit = (place == wanted) & (token >= 0) & (token < TOK)
    return hit.astype(F32).astype(BF16)


def build_bias(table, spread_ref, bias_ref):
    heads = table.shape[0]

    def one(index):
        row = index // SIDE
        shift = index + (SIDE - 1) * row
        rolled = pltpu.roll(table, (2 * LANES - shift) % (2 * LANES), 1)
        spread_ref[rows_at(index, heads), :] = rolled[:, :LANES]

    spread_ref[...] = jnp.zeros_like(spread_ref)
    for index in range(TOK):
        one(index)
    low, high = offset_select(0), offset_select(1)
    for pair in range(heads // 2):
        first = spread_ref[pl.ds(2 * pair, SPAN, stride=heads), :].astype(BF16)
        second = spread_ref[pl.ds(2 * pair + 1, SPAN, stride=heads), :].astype(BF16)
        bias_ref[:, pair * LANES : (pair + 1) * LANES] = dot(first, low) + dot(second, high)


def split_bf16(values):
    high = values.astype(BF16)
    return high, (values - high.astype(F32)).astype(BF16)


def reduce_bias(bias_ref, spread_ref, heads):
    low, high = offset_select(0), offset_select(1)
    for pair in range(heads // 2):
        parts = split_bf16(bias_ref[:, pair * LANES : (pair + 1) * LANES])
        spread_ref[pl.ds(2 * pair, SPAN, stride=heads), :] = sum(
            dot_cols(part, low) for part in parts
        )
        spread_ref[pl.ds(2 * pair + 1, SPAN, stride=heads), :] = sum(
            dot_cols(part, high) for part in parts
        )
    total = jnp.zeros((heads, 2 * LANES), F32)
    blank = jnp.zeros((heads, LANES), F32)
    for index in range(TOK):
        shift = index + (SIDE - 1) * (index // SIDE)
        row = jnp.concatenate([spread_ref[index * heads : (index + 1) * heads, :], blank], axis=1)
        total = total + (pltpu.roll(row, shift, 1) if shift else row)
    return total


def shift_both(ref, forward):
    rows, columns = ref.shape
    down, right = (1, 1) if forward else (rows - 1, columns - 1)
    ref[...] = pltpu.roll(pltpu.roll(ref[...], down, 0), right, 1)


def attention_forward(first, edges, qkv, bias_ref, probs_ref, att_ref):
    masks = head_masks()
    size = GROUP * SPAN
    ones = same_head(size, size)
    first_half = iota((SPAN, LANES), 1) < SPAN
    groups = range(att_ref.shape[1] // LANES)

    def part_of(array, group, width):
        return array[:, group * width : (group + 1) * width]

    def tops(values):
        found = []
        for half in range(size // LANES):
            piece = part_of(values, half, LANES)
            low = jnp.max(jnp.where(first_half, piece, 2 * NEG_FILL), -1, keepdims=True)
            high = jnp.max(jnp.where(first_half, 2 * NEG_FILL, piece), -1, keepdims=True)
            found.append(jnp.where(first_half, low, high))
        return jnp.concatenate(found, axis=1)

    bias = bias_ref[...]
    states = []
    for index, edge in enumerate(edges):
        window = first + index
        base = pl.ds(pl.multiple_of(window * (TOK - 1), 16), SPAN)
        row_index = iota((SPAN, 1), 0) - window
        row_in = (row_index >= 0) & (row_index < TOK)
        row_region = region_ids(row_index, edge, 8)
        lane_region = region_ids((iota((1, size), 1) & (SPAN - 1)) - window, edge, 16)
        query, key, value = (qkv[part, base, :] for part in range(3))
        states.append((window, base, row_in, row_region == lane_region, query, key, value, bias))
        bias = pltpu.roll(pltpu.roll(bias, 1, 0), 1, 1)
    bias_ref[...] = bias

    logits = [
        [
            jnp.where(
                allowed,
                dot_cols(
                    part_of(query, group, LANES), spread_heads(part_of(key, group, LANES), masks)
                )
                * (HD**-0.5)
                + part_of(shifted, group, size),
                NEG_FILL,
            )
            for group in groups
        ]
        for _, _, _, allowed, query, key, _, shifted in states
    ]
    terms = [[jnp.exp(values - tops(values)) for values in row] for row in logits]
    totals = [[dot(values.astype(BF16), ones) for values in row] for row in terms]
    probs = [
        [
            (terms[index][group] * (state[2].astype(F32) / totals[index][group])).astype(BF16)
            for group in groups
        ]
        for index, state in enumerate(states)
    ]
    attended = [
        jnp.concatenate(
            [
                dot(probs[index][group], spread_heads(part_of(state[6], group, LANES), masks))
                for group in groups
            ],
            axis=1,
        )
        for index, state in enumerate(states)
    ]
    for index, (window, base, row_in, *_) in enumerate(states):
        for group in groups:
            probs_ref[window, :, pl.ds(group * size, size)] = probs[index][group]
        before = att_ref[base, :].astype(F32)
        att_ref[base, :] = jnp.where(row_in, attended[index], before).astype(BF16)


def attention_backward(windows, qkv, d_att, probs_ref, d_bias_ref, d_qkv):
    masks = head_masks()
    size = GROUP * SPAN
    ones = same_head(size, size)
    groups = range(d_att.shape[1] // LANES)
    factor = HD**-0.5

    def part_of(array, group, width):
        return array[:, group * width : (group + 1) * width]

    states = []
    for window in windows:
        base = pl.ds(pl.multiple_of(window * (TOK - 1), 16), SPAN)
        query, key, value = (qkv[part, base, :] for part in range(3))
        states.append((base, query, key, value, d_att[base, :], probs_ref[window]))
    d_bias = d_bias_ref[...]

    weighted = [
        [
            dot_cols(
                part_of(upstream, group, LANES),
                spread_heads(part_of(value, group, LANES), masks),
            )
            * part_of(probs, group, size).astype(F32)
            for group in groups
        ]
        for _, _, _, value, upstream, probs in states
    ]
    deltas = [[dot(values.astype(BF16), ones) for values in row] for row in weighted]
    d_logits = [
        [
            (
                weighted[index][group]
                - part_of(state[5], group, size).astype(F32) * deltas[index][group]
            ).astype(BF16)
            for group in groups
        ]
        for index, state in enumerate(states)
    ]
    for row in d_logits:
        d_bias = pltpu.roll(pltpu.roll(d_bias, SPAN - 1, 0), d_bias.shape[1] - 1, 1)
        d_bias = d_bias + jnp.concatenate([values.astype(F32) for values in row], axis=1)
    d_bias_ref[...] = d_bias
    results = []
    for index, (base, query, key, value, upstream, probs) in enumerate(states):
        row = d_logits[index]
        d_query = [
            dot(row[group], spread_heads(part_of(key, group, LANES), masks)) * factor
            for group in groups
        ]
        d_key = [
            pick_heads(dot_rows(row[group], part_of(query, group, LANES))) * factor
            for group in groups
        ]
        d_value = [
            pick_heads(dot_rows(part_of(probs, group, size), part_of(upstream, group, LANES)))
            for group in groups
        ]
        results.append([jnp.concatenate(values, axis=1) for values in (d_query, d_key, d_value)])
    for index, window in enumerate(windows):
        base = states[index][0]
        row_index = iota((SPAN, 1), 0) - window
        row_in = (row_index >= 0) & (row_index < TOK)
        for part in range(3):
            old = d_qkv[part, base, :].astype(F32)
            d_qkv[part, base, :] = jnp.where(row_in, results[index][part], old).astype(BF16)


def sum_rows(values):
    return jnp.sum(values, 0, keepdims=True)


class Local:
    def __init__(self, refs, first_window):
        self.__dict__.update(refs)
        self.first_window = first_window
        self.rows, self.wide = self.x.shape
        self.width = self.section.shape[1]
        self.units = self.hidden.shape[1]
        self.windows = self.rows // TOK
        self.heads = self.width // HD
        self.chunk = 112
        self.steps = self.rows // self.chunk
        self.tile = self.units // self.gu.shape[0]

    def gain(self, row, lanes):
        return self.gains[row : row + 1, :lanes]

    def stat(self, at, index):
        return self.stats[at, index : index + 1]

    def keep_stats(self, at, index, mean, inv):
        self.stats[at, index : index + 1] = mean
        self.stats[at, index + 1 : index + 2] = inv

    def spread_vectors(self):
        for row, ref in enumerate(self.vectors):
            values = ref[...].astype(F32)
            for block in range(values.shape[0]):
                lanes = slice(block * LANES, (block + 1) * LANES)
                self.gains[row : row + 1, lanes] = values[block : block + 1]

    def prepare(self):
        def keep_rows(window):
            base = pl.ds(pl.multiple_of(window * (TOK - 1), 16), SPAN)
            index = iota((SPAN, 1), 0) - window
            inside = (index >= 0) & (index < TOK)
            valid = self.valid[self.first_window + window].astype(F32)
            self.stats[base, 6:7] = jnp.where(inside, valid, self.stats[base, 6:7])

        each(self.windows, keep_rows)

    def table_bias(self):
        build_bias(self.table(), self.spread, self.bias)

    def merge_norm(self):
        gain, shift = self.gain(0, self.wide), self.gain(1, self.wide)

        def step(index):
            at = rows_at(index, self.chunk)
            normed, mean, inv = norm_rows(self.x[at, :].astype(F32))
            self.merged[at, :] = (normed * gain + shift).astype(BF16)
            self.keep_stats(at, 0, mean, inv)

        each(self.steps, step)

    def merge(self):
        self.section[...] = dot(self.merged[...], self.wm[...]).astype(BF16)

    def attn_norm(self):
        gain, shift = self.gain(2, self.width), self.gain(3, self.width)

        def step(index):
            at = rows_at(index, self.chunk)
            normed, mean, inv = norm_rows(self.section[at, :].astype(F32))
            self.attn_in[at, :] = (normed * gain + shift).astype(BF16)
            self.keep_stats(at, 2, mean, inv)

        each(self.steps, step)

    def project(self, part):
        product = dot(self.attn_in[...], self.wqkv[part])
        if part != 1:
            product = product + self.qkv_bias(part)
        self.qkv[part] = product.astype(BF16)

    def attend(self, first, last, together=4):
        def step(index):
            window = first + index * together
            edges = [self.edge[self.first_window + window + more] for more in range(together)]
            attention_forward(window, edges, self.qkv, self.bias, self.probs, self.att)

        each((last - first) // together, step)

    def attn_out(self):
        self.pre[...] = dot(self.att[...], self.wp[...])

    def mlp_norm(self):
        gain, shift = self.gain(4, self.width), self.gain(5, self.width)
        proj_bias = self.gain(6, self.width)

        def step(index):
            at = rows_at(index, self.chunk)
            total = self.section[at, :].astype(F32) + self.pre[at, :] + proj_bias
            self.resid[at, :] = total
            normed, mean, inv = norm_rows(total)
            self.mlp_in[at, :] = (normed * gain + shift).astype(BF16)
            self.keep_stats(at, 4, mean, inv)

        each(self.steps, step)

    def up(self, index):
        columns = rows_at(index, self.tile)
        self.pre[...] = dot(self.mlp_in[...], self.wu[:, columns])
        shift = self.up_bias(index)

        def activate(step):
            at = rows_at(step, self.chunk)
            value, rate = gelu_both(self.pre[at, :] + shift)
            self.hidden[at, columns] = value.astype(BF16)
            self.slope[at, columns] = rate.astype(BF16)

        each(self.steps, activate, 7)
        put_blocks(self.gd, index, dot_rows(self.hidden[:, columns], self.d_mlp[...]))

    def down(self):
        self.pre[...] = dot(self.hidden[...], self.wd[...])

    def grad_rows(self):
        def step(index, total):
            at = rows_at(index, self.chunk)
            grad = self.grad_out[at, :].astype(F32) * self.stat(at, 6)
            self.d_mlp[at, :] = grad.astype(BF16)
            return total + fold(grad)

        total = lax.fori_loop(
            0, self.steps, step, jnp.zeros((8, self.width), F32)
        )
        self.put_sum(7, total)

    def finish(self):
        down_bias = self.gain(7, self.width)

        def step(index):
            at = rows_at(index, self.chunk)
            block = (self.resid[at, :] + self.pre[at, :] + down_bias) * self.stat(at, 6)
            self.out[at, :] = block.astype(BF16)

        each(self.steps, step)

    def hidden_back(self, index):
        columns = rows_at(index, self.tile)
        self.pre[...] = dot_cols(self.d_mlp[...], self.wd[columns, :])

        def activate(step, total):
            at = rows_at(step, self.chunk)
            grad = (self.pre[at, :] * self.slope[at, columns].astype(F32)).astype(BF16)
            self.d_pre[at, columns] = grad
            return total + fold(grad.astype(F32))

        total = lax.fori_loop(0, self.steps, activate, jnp.zeros((8, self.tile), F32))
        self.put_up_sum(index, total)
        put_blocks(self.gu, index, dot_rows(self.mlp_in[...], self.d_pre[:, columns]))

    def up_back(self):
        self.pre[...] = dot_cols(self.d_pre[...], self.wu[...])

    def mlp_back(self):
        gain = self.gain(4, self.width)

        def step(index, totals):
            at = rows_at(index, self.chunk)
            inv = self.stat(at, 5)
            normed = (self.resid[at, :] - self.stat(at, 4)) * inv
            upstream = self.pre[at, :]
            d_resid = self.d_mlp[at, :].astype(F32) + norm_back(upstream, normed, inv, gain)
            self.d_resid[at, :] = d_resid
            self.d_attn[at, :] = d_resid.astype(BF16)
            return (
                totals[0] + fold(upstream * normed),
                totals[1] + fold(upstream),
                totals[2] + fold(d_resid),
            )

        blank = jnp.zeros((8, self.width), F32)
        totals = lax.fori_loop(0, self.steps, step, (blank, blank, blank))
        for row, total in zip((5, 6, 4), totals):
            self.put_sum(row, total)

    def proj_back(self):
        size = self.width // self.gp.shape[0]
        product = dot_rows(self.att[...], self.d_attn[...])
        for index in range(self.gp.shape[0]):
            put_blocks(self.gp, index, product[index * size : (index + 1) * size])
        self.att[...] = dot_cols(self.d_attn[...], self.wp[...]).astype(BF16)
        self.d_bias[...] = jnp.zeros_like(self.d_bias)

    def attend_back(self, first, last, together=2):
        def step(index):
            top = last - 1 - index * together
            windows = [top - less for less in range(together)]
            attention_backward(windows, self.qkv, self.att, self.probs, self.d_bias, self.qkv)

        each((last - first) // together, step)

    def bias_back(self):
        self.put_table(reduce_bias(self.d_bias, self.spread, self.heads))
        ones = jnp.full((8, self.rows), 1.0, BF16)
        self.put_sum(8, dot(ones, self.qkv[0]), True)
        self.put_sum(9, dot(ones, self.qkv[2]), True)

    def qkv_weight_back(self):
        for part in range(3):
            put_columns(self.gqkv, part, dot_rows(self.attn_in[...], self.qkv[part]))

    def qkv_back(self):
        self.pre[...] = (
            dot_cols(self.qkv[0], self.wqkv[0])
            + dot_cols(self.qkv[1], self.wqkv[1])
            + dot_cols(self.qkv[2], self.wqkv[2])
        )

    def attn_back(self):
        gain = self.gain(2, self.width)

        def step(index, totals):
            at = rows_at(index, self.chunk)
            inv = self.stat(at, 3)
            normed = (self.section[at, :].astype(F32) - self.stat(at, 2)) * inv
            upstream = self.pre[at, :]
            d_section = self.d_resid[at, :] + norm_back(upstream, normed, inv, gain)
            self.d_mlp[at, :] = d_section.astype(BF16)
            return totals[0] + fold(upstream * normed), totals[1] + fold(upstream)

        blank = jnp.zeros((8, self.width), F32)
        totals = lax.fori_loop(0, self.steps, step, (blank, blank))
        self.put_sum(2, totals[0])
        self.put_sum(3, totals[1])

    def merge_weight_back(self):
        put_columns(self.gm, 0, dot_rows(self.merged[...], self.d_mlp[...]))

    def merge_in_back(self):
        for half, ref in enumerate((self.pre, self.d_resid)):
            rows = slice(half * self.width, (half + 1) * self.width)
            ref[...] = dot_cols(self.d_mlp[...], self.wm[rows, :])

    def merge_back(self, first, last, totals=None):
        gain = self.gain(0, self.wide)

        def step(index, totals):
            at = rows_at(first + index, 16)
            inv = self.stat(at, 1)
            normed = (self.x[at, :].astype(F32) - self.stat(at, 0)) * inv
            upstream = jnp.concatenate([self.pre[at, :], self.d_resid[at, :]], axis=1)
            self.d_in[at, :] = norm_back(upstream, normed, inv, gain)
            return totals[0] + fold(upstream * normed), totals[1] + fold(upstream)

        blank = jnp.zeros((8, self.wide), F32)
        totals = lax.fori_loop(0, last - first, step, totals or (blank, blank), unroll=7)
        if last == self.rows // 16:
            self.put_sum(0, totals[0])
            self.put_sum(1, totals[1])
        return totals

    def put_sum(self, row, values, summed=False):
        values = values[0:1] if summed else sum_rows(values)
        for block in range(values.shape[1] // LANES):
            place = SUM_ROWS[row] + block
            self.sums[place : place + 1, :] = values[:, block * LANES : (block + 1) * LANES]

    def put_up_sum(self, index, total):
        values = sum_rows(total)
        blocks = self.tile // LANES
        for block in range(blocks):
            place = SUM_ROWS[10] + index * blocks + block
            self.sums[pl.ds(place, 1), :] = values[:, block * LANES : (block + 1) * LANES]

    def put_table(self, values):
        for half in range(2):
            place = SUM_ROWS[11] + half * self.heads
            self.sums[place : place + self.heads, :] = values[:, half * LANES : (half + 1) * LANES]


SUM_ROWS = (0, 8, 16, 20, 24, 28, 32, 36, 40, 44, 48, 64)
SUM_SIZE = 128


def put_blocks(ref, shard, values):
    rows = values.shape[0]
    for block in range(values.shape[1] // LANES):
        at = pl.ds(block * rows, rows)
        ref[shard, at, :] = values[:, block * LANES : (block + 1) * LANES].astype(BF16)


def put_columns(ref, part, values):
    rows = values.shape[0]
    for shard in range(ref.shape[0]):
        piece = values[:, shard * LANES : (shard + 1) * LANES]
        ref[shard, part * rows : (part + 1) * rows, :] = piece.astype(BF16)


def local_scratch(rows, wide, width, units):
    heads = width // HD
    windows = rows // TOK
    return dict(
        merged=pltpu.VMEM((rows, wide), BF16),
        section=pltpu.VMEM((rows, width), BF16),
        attn_in=pltpu.VMEM((rows, width), BF16),
        qkv=pltpu.VMEM((3, rows, width), BF16),
        probs=pltpu.VMEM((windows, SPAN, heads * SPAN), BF16),
        att=pltpu.VMEM((rows, width), BF16),
        resid=pltpu.VMEM((rows, width), F32),
        mlp_in=pltpu.VMEM((rows, width), BF16),
        hidden=pltpu.VMEM((rows, units), BF16),
        slope=pltpu.VMEM((rows, units), BF16),
        pre=pltpu.VMEM((rows, width), F32),
        d_mlp=pltpu.VMEM((rows, width), BF16),
        d_pre=pltpu.VMEM((rows, units), BF16),
        d_attn=pltpu.VMEM((rows, width), BF16),
        d_resid=pltpu.VMEM((rows, width), F32),
        gains=pltpu.VMEM((8, wide), F32),
        stats=pltpu.VMEM((rows, 8), F32),
        bias=pltpu.VMEM((SPAN, heads * SPAN), F32),
        d_bias=pltpu.VMEM((SPAN, heads * SPAN), F32),
        spread=pltpu.VMEM((SPAN * heads, LANES), F32),
    )


MESH_ID = pl.DeviceIdType.MESH


class Links:
    def __init__(self, send_sems, recv_sems, plan):
        self.send_sems, self.recv_sems, self.plan = send_sems, recv_sems, plan
        self.sent = []
        self.sp, self.tp = lax.axis_index("sp"), lax.axis_index("tp")

    def place(self, way):
        kind, distance = way
        if kind == "tp":
            return self.sp, self.tp ^ distance
        return self.sp ^ distance, self.tp

    def copy(self, name, way, source, target):
        slot = self.plan.setdefault(name, len(self.plan))
        return pltpu.make_async_remote_copy(
            src_ref=source,
            dst_ref=target,
            send_sem=self.send_sems.at[slot],
            recv_sem=self.recv_sems.at[slot],
            device_id=self.place(way),
            device_id_type=MESH_ID,
        )

    def send(self, name, way, source, target):
        copy = self.copy(name, way, source, target)
        copy.start()
        self.sent.append(copy)

    def receive(self, name, way, target):
        self.copy(name, way, target, target).wait_recv()

    def keep(self, name, source, target):
        slot = self.plan.setdefault(name, len(self.plan))
        copy = pltpu.make_async_copy(source, target, self.recv_sems.at[slot])
        copy.start()
        return copy

    def greet(self, ways):
        barrier = pltpu.get_barrier_semaphore()
        for way in ways:
            pl.semaphore_signal(
                barrier, inc=1, device_id=self.place(way), device_id_type=MESH_ID
            )
        pl.semaphore_wait(barrier, len(ways))

    def drain(self):
        for copy in self.sent:
            copy.wait_send()


CORE, ACROSS, BESIDE = ("tp", 1), ("tp", 2), ("sp", 1)


def far_ways(sp_size):
    return [("sp", 2 * step) for step in range(1, sp_size // 2)]


class Gather:
    def __init__(self, links, name, own, whole, view, split):
        self.links, self.name, self.own, self.whole = links, name, own, whole
        self.view, self.split = view, split
        self.half = links.sp & 1

    def part(self, shard, half=None):
        return self.view(self.whole, shard, half)

    def label(self, step):
        return (self.name, step)

    def start(self):
        links = self.links
        mine = links.tp
        self.local = links.keep(self.label("own"), self.own, self.part(mine))
        half = self.half if self.split else None
        links.send(
            self.label("x"), ACROSS, self.view(self.own, None, half), self.part(mine, half)
        )
        links.send(self.label("c"), CORE, self.own, self.part(mine))

    def forward(self):
        links = self.links
        other = links.tp ^ 2
        half = self.half if self.split else None
        block = self.part(other, half)
        links.receive(self.label("x"), ACROSS, block)
        if self.split:
            links.send(self.label("y"), BESIDE, block, block)
        links.send(self.label("xc"), CORE, block, block)

    def forward_beside(self):
        if self.split:
            links = self.links
            block = self.part(links.tp ^ 2, 1 - self.half)
            links.receive(self.label("y"), BESIDE, block)
            links.send(self.label("yc"), CORE, block, block)

    def finish(self):
        links = self.links
        self.local.wait()
        links.receive(self.label("c"), CORE, self.part(links.tp ^ 1))
        half = self.half if self.split else None
        links.receive(self.label("xc"), CORE, self.part(links.tp ^ 3, half))
        if self.split:
            links.receive(self.label("yc"), CORE, self.part(links.tp ^ 3, 1 - self.half))


def column_view(size, halves):
    def view(ref, shard, half):
        rank = len(ref.shape)
        rows = ref.shape[rank - 2]
        at = slice(None) if half is None else pl.ds(
            pl.multiple_of(half * (rows // 2), 16), rows // 2
        )
        lanes = slice(None) if shard is None else pl.ds(pl.multiple_of(shard * size, LANES), size)
        return ref.at[(slice(None),) * (rank - 2) + (at, lanes)]

    return view


def row_view(size):
    def view(ref, shard, half):
        start = 0 if shard is None else shard * size
        if half is None:
            return ref.at[pl.ds(start, size), :]
        start = start + half * (size // 2)
        return ref.at[pl.ds(pl.multiple_of(start, 16), size // 2), :]

    return view


def lead_view(ref, shard, half):
    return ref if shard is None else ref.at[shard]


def add_rows(target, start, rows, terms, chunk=128):
    chunk = math.gcd(rows, chunk)

    def step(index):
        offset = index * chunk

        def at(first):
            return pl.ds(pl.multiple_of(first + offset, 16), chunk)

        total = None
        for ref, first in terms:
            value = ref[at(first), :].astype(F32)
            total = value if total is None else total + value
        target[at(start), :] = total.astype(target.dtype)

    each(rows // chunk, step)


class Reduce:
    def __init__(self, links, name, grads, core_in, first_in, second_in, far_in, result, group,
                 across_first):
        self.links, self.name, self.grads = links, name, grads
        self.core_in, self.first_in, self.second_in = core_in, first_in, second_in
        self.far_in, self.result, self.group = far_in, result, group
        self.rows = grads.shape[1]
        self.half_rows = self.rows // 2
        self.piece = self.half_rows // group
        self.half = links.sp & 1
        self.seat = links.sp >> 1
        self.across = links.tp >> 1
        if across_first:
            middle = self.core_add_across, self.across_beside, self.beside_last
        else:
            middle = self.core_add_beside, self.beside_across, self.across_last
        self.steps = dict(
            far=self.core_far, near=self.core_near, add=middle[0], first=middle[1],
            second=middle[2], spread=self.far_add, back=self.far_done, last=self.beside_done,
        )

    def run(self, step):
        self.steps.pop(step)()

    def label(self, *step):
        return (self.name,) + step

    def rows_of(self, ref, half, piece=None):
        if piece is None:
            return ref.at[pl.ds(pl.multiple_of(half * self.half_rows, 16), self.half_rows), :]
        start = half * self.half_rows + piece * self.piece
        return ref.at[pl.ds(pl.multiple_of(start, 16), self.piece), :]

    def core_send(self, across, name):
        shard = (self.links.tp & 1) ^ 1 | 2 * across
        self.links.send(
            self.label(name), CORE, self.grads.at[shard], self.core_in.at[across]
        )

    def core_far(self):
        self.core_send(self.across ^ 1, "cf")

    def core_near(self):
        self.core_send(self.across, "cn")

    def receive_far(self):
        self.links.receive(self.label("cf"), CORE, self.core_in.at[self.across ^ 1])

    def receive_near(self):
        self.links.receive(self.label("cn"), CORE, self.core_in.at[self.across])

    def core_add_across(self):
        self.receive_far()
        other = self.links.tp ^ 2
        block = self.grads.at[other]
        add_rows(block, 0, self.rows, [(block, 0), (self.core_in.at[self.across ^ 1], 0)])
        self.links.send(self.label("x"), ACROSS, block, self.first_in)

    def across_beside(self):
        links = self.links
        self.receive_near()
        links.receive(self.label("x"), ACROSS, self.first_in)
        block = self.grads.at[links.tp]
        terms = [(block, 0), (self.core_in.at[self.across], 0), (self.first_in, 0)]
        add_rows(block, 0, self.rows, terms)
        links.send(
            self.label("y"), BESIDE, self.rows_of(block, 1 - self.half), self.second_in
        )

    def beside_last(self):
        self.links.receive(self.label("y"), BESIDE, self.second_in)
        self.add_and_spread([(self.second_in, 0)])

    def core_add_beside(self):
        links = self.links
        self.receive_far()
        self.receive_near()
        for across in range(2):
            block = self.grads.at[(links.tp & 1) | 2 * across]
            add_rows(block, 0, self.rows, [(block, 0), (self.core_in.at[across], 0)])
            links.send(
                self.label("y", across), BESIDE, self.rows_of(block, 1 - self.half),
                self.first_in.at[across],
            )

    def beside_across(self):
        links = self.links
        for across in range(2):
            links.receive(self.label("y", across), BESIDE, self.first_in.at[across])
        block = self.grads.at[links.tp ^ 2]
        mine = self.half * self.half_rows
        terms = [(block, mine), (self.first_in.at[self.across ^ 1], 0)]
        add_rows(block, mine, self.half_rows, terms)
        links.send(self.label("x"), ACROSS, self.rows_of(block, self.half), self.second_in)

    def across_last(self):
        self.links.receive(self.label("x"), ACROSS, self.second_in)
        self.add_and_spread([(self.first_in.at[self.across], 0), (self.second_in, 0)])

    def add_and_spread(self, terms):
        block = self.grads.at[self.links.tp]
        mine = self.half * self.half_rows
        add_rows(block, mine, self.half_rows, [(block, mine)] + terms)
        for step in range(1, self.group):
            self.links.send(
                self.label("z", step), ("sp", 2 * step),
                self.rows_of(block, self.half, self.seat ^ step), self.far_in.at[step - 1],
            )

    def far_add(self):
        links = self.links
        block = self.grads.at[links.tp]
        mine = self.half * self.half_rows + self.seat * self.piece
        terms = [(block, mine)]
        for step in range(1, self.group):
            links.receive(self.label("z", step), ("sp", 2 * step), self.far_in.at[step - 1])
            terms.append((self.far_in.at[step - 1], 0))
        add_rows(self.result, mine, self.piece, terms)
        done = self.rows_of(self.result, self.half, self.seat)
        for step in range(1, self.group):
            links.send(self.label("a", step), ("sp", 2 * step), done, done)

    def far_done(self):
        links = self.links
        for step in range(1, self.group):
            links.receive(
                self.label("a", step), ("sp", 2 * step),
                self.rows_of(self.result, self.half, self.seat ^ step),
            )
        done = self.rows_of(self.result, self.half)
        links.send(self.label("b"), BESIDE, done, done)

    def beside_done(self):
        self.links.receive(
            self.label("b"), BESIDE, self.rows_of(self.result, 1 - self.half)
        )


class Total:
    def __init__(self, links, name, stages, inboxes, far_in, result, group):
        self.links, self.name, self.stages, self.inboxes = links, name, stages, inboxes
        self.far_in, self.result, self.group = far_in, result, group
        self.piece = result.shape[0] // group
        self.seat = links.sp >> 1
        self.ways = (CORE, ACROSS, BESIDE)
        self.steps = [
            functools.partial(self.exchange, 0), functools.partial(self.add, 0),
            functools.partial(self.add, 1), functools.partial(self.add, 2), self.far_add,
            self.far_done,
        ]

    def run(self):
        self.steps.pop(0)()

    def label(self, *step):
        return (self.name,) + step

    def at(self, ref, piece):
        return ref.at[pl.ds(pl.multiple_of(piece * self.piece, 8), self.piece), :]

    def exchange(self, stage):
        self.links.send(
            self.label("e", stage), self.ways[stage], self.stages.at[stage],
            self.inboxes.at[stage],
        )

    def add(self, stage):
        self.links.receive(self.label("e", stage), self.ways[stage], self.inboxes.at[stage])
        self.stages[stage + 1] = self.stages[stage] + self.inboxes[stage]
        if stage < 2:
            self.exchange(stage + 1)
            return
        for step in range(1, self.group):
            self.links.send(
                self.label("z", step), ("sp", 2 * step),
                self.at(self.stages.at[3], self.seat ^ step), self.far_in.at[step - 1],
            )

    def far_add(self):
        total = self.at(self.stages.at[3], self.seat)[...]
        for step in range(1, self.group):
            self.links.receive(self.label("z", step), ("sp", 2 * step), self.far_in.at[step - 1])
            total = total + self.far_in[step - 1]
        done = self.at(self.result, self.seat)
        done[...] = total
        for step in range(1, self.group):
            self.links.send(self.label("a", step), ("sp", 2 * step), done, done)

    def far_done(self):
        for step in range(1, self.group):
            self.links.receive(
                self.label("a", step), ("sp", 2 * step), self.at(self.result, self.seat ^ step)
            )


UNITS = (
    ("gd", 0, 1024, True), ("gd", 1024, 1024, True),
    ("gu", 0, 1024, True), ("gu", 1024, 1024, True),
    ("gp", 0, 512, True),
    ("gqkv", 0, 1024, True), ("gqkv", 1024, 512, False),
    ("gm", 0, 512, True), ("gm", 512, 512, False),
)
GRADS = ("gd", "gu", "gp", "gqkv", "gm")
WEIGHTS = ("wm", "wqkv", "wp", "wu", "wd")
VECTORS = (
    "merge_gain", "merge_bias", "attn_gain", "attn_bias", "mlp_gain", "mlp_bias", "proj_bias",
    "down_bias",
)
INPUTS = (
    ("valid", "edge", "rel", "qv", "ub") + VECTORS + ("h_x", "h_grad_out")
    + tuple("own_" + name for name in WEIGHTS)
)
OUTPUTS = ("h_out", "h_d_in") + tuple("r_" + name for name in GRADS) + ("r_sums",)


def unit_name(name, first):
    return name + str(first)


def whole_kernel(names, group, plan, *refs):
    refs = dict(zip(names, refs, strict=True))
    links = Links(refs.pop("send_sems"), refs.pop("recv_sems"), plan)
    arriving = [
        links.keep(name, refs.pop("h_" + name), refs[name]) for name in ("x", "grad_out")
    ]
    rows = refs["x"].shape[0]
    own_pack, packs = refs.pop("pack"), refs.pop("packs")
    rel, qv, ub = refs.pop("rel"), refs.pop("qv"), refs.pop("ub")
    heads_here = rel.shape[0]
    own_pack[...] = jnp.zeros_like(own_pack)
    own_pack[0:heads_here, 0:REL] = rel[...].astype(F32)
    own_pack[4:6, 0:LANES] = qv[...].astype(F32)
    for block in range(ub.shape[0]):
        lanes = slice(block * LANES, (block + 1) * LANES)
        own_pack[6:7, lanes] = ub[block : block + 1, :].astype(F32)

    own = {name: refs.pop("own_" + name) for name in WEIGHTS}
    whole = {name: refs[name] for name in WEIGHTS}
    for part, name in enumerate(("wq", "wk", "wv")):
        own[name], whole[name] = own["wqkv"].at[part], whole["wqkv"].at[part]
    columns = column_view(LANES, True)
    views = dict(
        wm=columns, wq=columns, wk=columns, wv=columns, wp=row_view(own["wp"].shape[0]),
        wu=column_view(own["wu"].shape[1], True), wd=row_view(own["wd"].shape[0]),
    )
    gathers = {"pack": Gather(links, "pack", own_pack, packs, lead_view, False)}
    for name in ("wm", "wq", "wk", "wv", "wp", "wu", "wd"):
        gathers[name] = Gather(links, name, own[name], whole[name], views[name], name != "wm")
    links.greet([CORE, ACROSS, BESIDE] + far_ways(2 * group))
    for gather in gathers.values():
        gather.start()

    results = {name: refs.pop("r_" + name) for name in GRADS}
    reduces = {}
    for name, first, size, across_first in UNITS:
        unit = unit_name(name, first)
        part = pl.ds(first, size)
        reduces[unit] = Reduce(
            links, unit, refs[name].at[:, part, :], refs.pop("c_" + unit),
            refs.pop("f_" + unit), refs.pop("s_" + unit), refs.pop("z_" + unit),
            results[name].at[part, :], group, across_first,
        )
    stages, inboxes = refs.pop("sum_stages"), refs.pop("sum_inboxes")
    refs["sums"] = stages.at[0]
    total = Total(links, "sums", stages, inboxes, refs.pop("sum_far"), refs.pop("r_sums"), group)
    shards = packs.shape[0]

    def table():
        return jnp.concatenate(
            [packs[shard, 0:heads_here, : 2 * LANES] for shard in range(shards)], axis=0
        )

    def qkv_bias(part):
        row = 4 if part == 0 else 5
        return jnp.concatenate(
            [packs[shard, row : row + 1, :LANES] for shard in range(shards)], axis=1
        )

    def up_bias(index):
        return packs[index, 6:7, :]

    refs["vectors"] = [refs.pop(name) for name in VECTORS]
    refs.update(table=table, qkv_bias=qkv_bias, up_bias=up_bias)
    h_out, h_d_in = refs.pop("h_out"), refs.pop("h_d_in")
    local = Local(refs, links.tp * (rows // TOK))

    def forward(*names):
        for name in names:
            gathers[name].forward()

    def beside(*names):
        for name in names:
            gathers[name].forward_beside()

    def ready(*names):
        for name in names:
            gathers[name].finish()

    def run(step, *units):
        for unit in units:
            reduces[unit].run(step)

    gd0, gd1, gu0, gu1, gp0 = "gd0", "gd1024", "gu0", "gu1024", "gp0"
    qkv0, qkv1, gm0, gm1 = "gqkv0", "gqkv1024", "gm0", "gm512"
    windows = local.windows

    for copy in arriving:
        copy.wait()
    stages[0] = jnp.zeros_like(stages[0])
    local.spread_vectors()
    local.merge_norm()
    local.prepare()
    forward("pack")
    local.grad_rows()
    ready("pack")
    local.table_bias()
    forward("wm")
    ready("wm")
    local.merge()
    forward("wq")
    local.attn_norm()
    forward("wk", "wv")
    beside("wq")
    ready("wq")
    local.project(0)
    beside("wk")
    ready("wk")
    local.project(1)
    beside("wv")
    ready("wv")
    local.project(2)
    forward("wp")
    local.attend(0, windows // 4)
    beside("wp")
    forward("wu")
    local.attend(windows // 4, windows // 2)
    ready("wp")
    local.attend(windows // 2, windows)
    forward("wd")
    local.attn_out()
    beside("wu")
    local.mlp_norm()
    ready("wu")

    tiles = [links.tp ^ bits for bits in (3, 2, 1, 0)]
    local.up(tiles[0])
    run("far", gd0, gd1)
    beside("wd")
    local.up(tiles[1])
    run("add", gd0, gd1)
    local.up(tiles[2])
    run("near", gd0, gd1)
    local.up(tiles[3])
    ready("wd")
    local.hidden_back(tiles[0])
    run("far", gu0, gu1)
    local.hidden_back(tiles[1])
    run("add", gu0, gu1)
    local.hidden_back(tiles[2])
    run("near", gu0, gu1)
    run("first", gd0)
    local.hidden_back(tiles[3])
    local.up_back()
    local.mlp_back()
    run("second", gd0)
    run("first", gd1)
    local.proj_back()
    run("far", gp0)
    run("near", gp0)

    def attend_back(index):
        local.attend_back((3 - index) * windows // 4, (4 - index) * windows // 4)

    attend_back(0)
    run("add", gp0)
    attend_back(1)
    run("spread", gd0)
    run("first", gu0)
    run("second", gd1)
    attend_back(2)
    attend_back(3)
    local.qkv_weight_back()
    run("far", qkv0, qkv1)
    run("near", qkv0, qkv1)
    run("back", gd0)
    run("spread", gd1)
    run("second", gu0)
    run("first", gu1)
    local.qkv_back()
    run("add", qkv0, qkv1)
    run("first", gp0)
    local.attn_back()
    run("spread", gu0)
    run("back", gd1)
    run("second", gu1)
    local.merge_weight_back()
    run("far", gm0, gm1)
    run("near", gm0, gm1)
    run("second", gp0)
    run("first", qkv1)
    local.merge_in_back()
    run("add", gm0, gm1)
    run("back", gu0)
    run("spread", gu1, gp0)
    third = rows // 16 // 7
    totals = local.merge_back(0, 3 * third)
    run("first", qkv0)
    run("second", qkv1)
    local.merge_back(3 * third, 7 * third, totals)
    done = [links.keep("d_in", local.d_in, h_d_in)]
    run("back", gp0, gu1)
    run("first", gm1, gm0)
    local.bias_back()
    total.run()
    run("second", qkv0)
    run("spread", qkv1)
    local.down()
    total.run()
    run("second", gm1, gm0)
    local.finish()
    done.append(links.keep("out", local.out, h_out))
    total.run()
    run("spread", qkv0)
    run("back", qkv1)
    run("spread", gm1, gm0)
    total.run()
    run("last", gd0, gd1, gu0, gu1, gp0)
    run("back", qkv0)
    total.run()
    run("back", gm1, gm0)
    total.run()
    run("last", qkv0, qkv1, gm0, gm1)
    assert not any(reduce.steps for reduce in reduces.values())
    for copy in done:
        copy.wait()
    links.drain()


def finish_kernel(names, *refs):
    refs = dict(zip(names, refs, strict=True))
    tp = lax.axis_index("tp")
    pieces, number = [], 0
    for name in ("d_in", "out"):
        source, target, held = refs["h_" + name], refs["o_" + name], refs["v_" + name]
        size = held.shape[0] // PIECES
        for index in range(PIECES):
            at = pl.ds(index * size, size)
            sems = refs["sems"].at[number], refs["sems"].at[number + 1]
            number += 2
            pieces.append(
                (
                    pltpu.make_async_copy(source.at[at], held.at[at], sems[0]),
                    pltpu.make_async_copy(held.at[at], target.at[at], sems[1]),
                )
            )
    for incoming, _ in pieces:
        incoming.start()
    sums = refs["r_sums"]
    for row, name in enumerate(
        ("merge_gain", "merge_bias", "attn_gain", "attn_bias", "proj_bias", "mlp_gain",
         "mlp_bias", "down_bias")
    ):
        out = refs["o_" + name]
        out[...] = sums[SUM_ROWS[row] : SUM_ROWS[row] + out.shape[0], :]
    for index in range(2):
        refs["o_qv"][index : index + 1, :] = sums[pl.ds(SUM_ROWS[8 + index] + tp, 1), :]
    blocks = refs["o_ub"].shape[0]
    for index in range(blocks):
        refs["o_ub"][index : index + 1, :] = sums[
            pl.ds(SUM_ROWS[10] + tp * blocks + index, 1), :
        ]
    mine = refs["o_rel"].shape[0]
    heads = SHARDS * mine
    for index in range(mine):
        first = SUM_ROWS[11] + tp * mine + index
        low, high = sums[pl.ds(first, 1), :], sums[pl.ds(first + heads, 1), :]
        refs["o_rel"][index : index + 1, :LANES] = low
        refs["o_rel"][index : index + 1, LANES:] = high[:, : REL - LANES]
    for name in GRADS:
        result, out = refs["r_" + name], refs["o_" + name]
        if len(out.shape) == 3:
            rows = out.shape[1]
            for part in range(out.shape[0]):
                out[part] = result[part * rows : (part + 1) * rows, :].astype(F32)
        else:
            rows = out.shape[0]
            for block in range(out.shape[1] // LANES):
                lanes = slice(block * LANES, (block + 1) * LANES)
                out[:, lanes] = result[block * rows : (block + 1) * rows, :].astype(F32)
    for incoming, outgoing in pieces:
        incoming.wait()
        outgoing.start()
    for _, outgoing in pieces:
        outgoing.wait()


SHARDS = 4
PIECES = 7
VMEM_SPEC = pl.BlockSpec(memory_space=pltpu.VMEM)
SMEM_SPEC = pl.BlockSpec(memory_space=pltpu.SMEM)
HBM_SPEC = pl.BlockSpec(memory_space=pl.ANY)


def whole_call(group, inputs):
    rows, wide = inputs["h_x"].shape
    width = inputs["own_wu"].shape[0]
    units = SHARDS * inputs["own_wu"].shape[1]
    depth = dict(gd=units, gu=units, gp=width, gqkv=3 * width, gm=wide)
    scratch = local_scratch(rows, wide, width, units)
    scratch.update(
        wm=pltpu.VMEM((wide, width), BF16),
        wqkv=pltpu.VMEM((3, width, width), BF16),
        wp=pltpu.VMEM((width, width), BF16),
        wu=pltpu.VMEM((width, units), BF16),
        wd=pltpu.VMEM((units, width), BF16),
        pack=pltpu.VMEM((8, units // SHARDS), F32),
        packs=pltpu.VMEM((SHARDS, 8, units // SHARDS), F32),
        x=pltpu.VMEM((rows, wide), BF16),
        grad_out=pltpu.VMEM((rows, width), BF16),
        out=pltpu.VMEM((rows, width), BF16),
        d_in=pltpu.VMEM((rows, wide), F32),
    )
    for name in GRADS:
        scratch[name] = pltpu.VMEM((SHARDS, depth[name], LANES), BF16)
    for name, first, size, across_first in UNITS:
        unit = unit_name(name, first)
        half = size // 2
        scratch["c_" + unit] = pltpu.VMEM((2, size, LANES), BF16)
        first_shape = (size, LANES) if across_first else (2, half, LANES)
        scratch["f_" + unit] = pltpu.VMEM(first_shape, BF16)
        scratch["s_" + unit] = pltpu.VMEM((half, LANES), BF16)
        scratch["z_" + unit] = pltpu.VMEM((group - 1, half // group, LANES), BF16)
    scratch["sum_stages"] = pltpu.VMEM((4, SUM_SIZE, LANES), F32)
    scratch["sum_inboxes"] = pltpu.VMEM((3, SUM_SIZE, LANES), F32)
    scratch["sum_far"] = pltpu.VMEM((group - 1, SUM_SIZE // group, LANES), F32)
    count = 8 * 6 + len(UNITS) * (5 + 2 * group) + 8 + 2 * group
    scratch["send_sems"] = pltpu.SemaphoreType.DMA((count,))
    scratch["recv_sems"] = pltpu.SemaphoreType.DMA((count,))
    outs = dict(
        h_out=jax.ShapeDtypeStruct((rows, width), BF16),
        h_d_in=jax.ShapeDtypeStruct((rows, wide), F32),
        r_sums=jax.ShapeDtypeStruct((SUM_SIZE, LANES), F32),
    )
    for name in GRADS:
        outs["r_" + name] = jax.ShapeDtypeStruct((depth[name], LANES), BF16)
    names = INPUTS + OUTPUTS + tuple(scratch)
    in_vmem = 3 + len(VECTORS)
    return pl.pallas_call(
        functools.partial(whole_kernel, names, group, {}),
        out_shape=[outs[name] for name in OUTPUTS],
        in_specs=[SMEM_SPEC] * 2 + [VMEM_SPEC] * in_vmem + [HBM_SPEC] * (2 + len(WEIGHTS)),
        out_specs=[HBM_SPEC] * 2 + [VMEM_SPEC] * (len(OUTPUTS) - 2),
        scratch_shapes=list(scratch.values()),
        compiler_params=pltpu.CompilerParams(
            vmem_limit_bytes=63 * MIB, collective_id=0, has_side_effects=True
        ),
    )(*[inputs[name] for name in INPUTS])


def finish_call(results, shapes):
    names = OUTPUTS + tuple("o_" + name for name in shapes) + ("v_out", "v_d_in", "sems")
    return pl.pallas_call(
        functools.partial(finish_kernel, names),
        out_shape=list(shapes.values()),
        in_specs=[HBM_SPEC] * 2 + [VMEM_SPEC] * (len(OUTPUTS) - 2),
        out_specs=[HBM_SPEC] * 2 + [VMEM_SPEC] * (len(shapes) - 2),
        scratch_shapes=[
            pltpu.VMEM(shapes["out"].shape, BF16),
            pltpu.VMEM(shapes["d_in"].shape, F32),
            pltpu.SemaphoreType.DMA((4 * PIECES,)),
        ],
        compiler_params=pltpu.CompilerParams(vmem_limit_bytes=63 * MIB),
    )(*results)


def on_device(
    inputs, grad_out, window_valid, window_edge, merge_gain, merge_bias, merge_weight, attn_gain,
    attn_bias, query_key_value_weight, qv_bias, rel_table, proj_weight, proj_bias, mlp_gain,
    mlp_bias, up_weight, up_bias, down_weight, down_bias,
):
    vectors = dict(
        merge_gain=merge_gain, merge_bias=merge_bias, attn_gain=attn_gain, attn_bias=attn_bias,
        mlp_gain=mlp_gain, mlp_bias=mlp_bias, proj_bias=proj_bias, down_bias=down_bias,
    )
    blocks = {name: vector.reshape(-1, LANES) for name, vector in vectors.items()}
    arrays = dict(
        valid=window_valid, edge=window_edge, h_x=inputs, h_grad_out=grad_out, rel=rel_table.T,
        qv=qv_bias, ub=up_bias.reshape(-1, LANES), own_wm=merge_weight,
        own_wqkv=jnp.transpose(query_key_value_weight, (1, 0, 2)), own_wp=proj_weight,
        own_wu=up_weight, own_wd=down_weight, **blocks,
    )
    results = whole_call(lax.axis_size("sp") // 2, arrays)
    f32_like = lambda array: jax.ShapeDtypeStruct(array.shape, F32)
    shapes = dict(
        out=jax.ShapeDtypeStruct(grad_out.shape, BF16), d_in=f32_like(inputs),
        gm=f32_like(merge_weight), gqkv=f32_like(arrays["own_wqkv"]), gp=f32_like(proj_weight),
        gu=f32_like(up_weight), gd=f32_like(down_weight), qv=f32_like(qv_bias),
        rel=f32_like(arrays["rel"]), ub=f32_like(arrays["ub"]),
        **{name: f32_like(block) for name, block in blocks.items()},
    )
    done = dict(zip(shapes, finish_call(results, shapes), strict=True))
    flat = lambda name: done[name].reshape(-1)
    return (
        done["out"], done["d_in"], flat("merge_gain"), flat("merge_bias"), done["gm"],
        flat("attn_gain"), flat("attn_bias"), jnp.transpose(done["gqkv"], (1, 0, 2)), done["qv"],
        done["rel"].T, done["gp"], flat("proj_bias"), flat("mlp_gain"), flat("mlp_bias"),
        done["gu"], flat("ub"), done["gd"], flat("down_bias"),
    )


def solution(mesh):
    placed = (
        P(("sp", "tp"), None),
        P(("sp", "tp"), None),
        P("sp"),
        P("sp"),
        P(),
        P(),
        P(None, "tp"),
        P(),
        P(),
        P(None, None, "tp"),
        P(None, "tp"),
        P(None, "tp"),
        P("tp", None),
        P(),
        P(),
        P(),
        P(None, "tp"),
        P("tp"),
        P("tp", None),
        P(),
    )
    return jax.shard_map(
        on_device,
        mesh=mesh,
        in_specs=placed,
        out_specs=(
            P(("sp", "tp"), None),
            P(("sp", "tp"), None),
            P(),
            P(),
            P(None, "tp"),
            P(),
            P(),
            P(None, None, "tp"),
            P(None, "tp"),
            P(None, "tp"),
            P("tp", None),
            P(),
            P(),
            P(),
            P(None, "tp"),
            P("tp"),
            P("tp", None),
            P(),
        ),
        check_vma=False,
    )
```

```python
import functools
import math

import jax
import jax.numpy as jnp
from jax import lax
from jax.experimental import pallas as pl
from jax.experimental.pallas import tpu as pltpu
from jax.sharding import PartitionSpec as P

SIDE = 7
TOK = SIDE * SIDE
REL_SIDE = 2 * SIDE - 1
REL = REL_SIDE * REL_SIDE
SPAN = 64
GROUP = 4
HD = 32
LANES = 128
EPSILON = 1e-05
NEG_FILL = -1000000000.0
MIB = 1 << 20
F32 = jnp.float32
BF16 = jnp.bfloat16


def dot(left, right):
    return jnp.dot(left, right, preferred_element_type=F32)


def dot_cols(left, right):
    return lax.dot_general(left, right, (((1,), (1,)), ((), ())), preferred_element_type=F32)


def dot_rows(left, right):
    return lax.dot_general(left, right, (((0,), (0,)), ((), ())), preferred_element_type=F32)


def rows_at(index, size):
    return pl.ds(pl.multiple_of(index * size, size), size)


def each(count, body, unroll=1):
    def step(index, carry):
        body(index)
        return carry

    lax.fori_loop(0, count, step, 0, unroll=unroll)


def fold(values):
    total = values[0:8]
    for start in range(8, values.shape[0], 8):
        total = total + values[start : start + 8]
    return total


def iota(shape, dim):
    return lax.broadcasted_iota(jnp.int32, shape, dim)


def norm_rows(values):
    mean = jnp.mean(values, -1, keepdims=True)
    centred = values - mean
    inv = lax.rsqrt(jnp.mean(centred * centred, -1, keepdims=True) + EPSILON)
    return centred * inv, mean, inv


def norm_back(upstream, normed, inv, gain):
    scaled = upstream * gain
    return inv * (
        scaled
        - jnp.mean(scaled, -1, keepdims=True)
        - normed * jnp.mean(scaled * normed, -1, keepdims=True)
    )


def gelu_both(values):
    size = jnp.abs(values) * 0.7071067811865476
    bell = jnp.exp(-size * size)
    t = 1.0 / (1.0 + 0.3275911 * size)
    poly = t * (
        0.254829592
        + t * (-0.284496736 + t * (1.421413741 + t * (-1.453152027 + t * 1.061405429)))
    )
    tail = 0.5 * poly * bell
    phi = jnp.where(values >= 0, 1.0 - tail, tail)
    return values * phi, phi + values * bell * 0.3989422804014327


def window_row_col(index):
    row = (index * 37) >> 8
    return row, index - SIDE * row


def region_ids(index, edge, outside):
    row, col = window_row_col(index)
    high = SIDE - SIDE // 2
    region = (edge & 1) * (col >= high).astype(jnp.int32) + 2 * (edge >> 1) * (
        row >= high
    ).astype(jnp.int32)
    return jnp.where((index >= 0) & (index < TOK), region, outside)


def head_masks():
    lane = iota((1, LANES), 1)
    return [((lane >> 5) == head).astype(F32).astype(BF16) for head in range(GROUP)]


def spread_heads(block, masks):
    return jnp.concatenate([block * mask for mask in masks], axis=0)


def pick_heads(product):
    lane = iota((SPAN, LANES), 1)
    result = product[3 * SPAN : 4 * SPAN]
    for head in (2, 1, 0):
        result = jnp.where(
            lane < (head + 1) * HD, product[head * SPAN : (head + 1) * SPAN], result
        )
    return result


def same_head(rows, columns):
    return (
        (iota((rows, columns), 0) // (rows // GROUP))
        == (iota((rows, columns), 1) // (columns // GROUP))
    ).astype(F32).astype(BF16)


def offset_select(half):
    place = iota((LANES, LANES), 0)
    lane = iota((LANES, LANES), 1)
    token = lane - half * SPAN
    row, col = window_row_col(token & (SPAN - 1))
    wanted = (SIDE - 1) * (REL_SIDE + 1) - (REL_SIDE * row + col)
    hit = (place == wanted) & (token >= 0) & (token < TOK)
    return hit.astype(F32).astype(BF16)


def build_bias(table, spread_ref, bias_ref):
    heads = table.shape[0]

    def one(index):
        row = index // SIDE
        shift = index + (SIDE - 1) * row
        rolled = pltpu.roll(table, (2 * LANES - shift) % (2 * LANES), 1)
        spread_ref[rows_at(index, heads), :] = rolled[:, :LANES]

    spread_ref[...] = jnp.zeros_like(spread_ref)
    for index in range(TOK):
        one(index)
    low, high = offset_select(0), offset_select(1)
    for pair in range(heads // 2):
        first = spread_ref[pl.ds(2 * pair, SPAN, stride=heads), :].astype(BF16)
        second = spread_ref[pl.ds(2 * pair + 1, SPAN, stride=heads), :].astype(BF16)
        bias_ref[:, pair * LANES : (pair + 1) * LANES] = dot(first, low) + dot(second, high)


def split_bf16(values):
    high = values.astype(BF16)
    return high, (values - high.astype(F32)).astype(BF16)


def reduce_bias(bias_ref, spread_ref, heads):
    low, high = offset_select(0), offset_select(1)
    for pair in range(heads // 2):
        parts = split_bf16(bias_ref[:, pair * LANES : (pair + 1) * LANES])
        spread_ref[pl.ds(2 * pair, SPAN, stride=heads), :] = sum(
            dot_cols(part, low) for part in parts
        )
        spread_ref[pl.ds(2 * pair + 1, SPAN, stride=heads), :] = sum(
            dot_cols(part, high) for part in parts
        )
    total = jnp.zeros((heads, 2 * LANES), F32)
    blank = jnp.zeros((heads, LANES), F32)
    for index in range(TOK):
        shift = index + (SIDE - 1) * (index // SIDE)
        row = jnp.concatenate([spread_ref[index * heads : (index + 1) * heads, :], blank], axis=1)
        total = total + (pltpu.roll(row, shift, 1) if shift else row)
    return total


def shift_both(ref, forward):
    rows, columns = ref.shape
    down, right = (1, 1) if forward else (rows - 1, columns - 1)
    ref[...] = pltpu.roll(pltpu.roll(ref[...], down, 0), right, 1)


def attention_forward(first, edges, qkv, bias_ref, probs_ref, att_ref):
    masks = head_masks()
    size = GROUP * SPAN
    ones = same_head(size, size)
    first_half = iota((SPAN, LANES), 1) < SPAN
    groups = range(att_ref.shape[1] // LANES)

    def part_of(array, group, width):
        return array[:, group * width : (group + 1) * width]

    def tops(values):
        found = []
        for half in range(size // LANES):
            piece = part_of(values, half, LANES)
            low = jnp.max(jnp.where(first_half, piece, 2 * NEG_FILL), -1, keepdims=True)
            high = jnp.max(jnp.where(first_half, 2 * NEG_FILL, piece), -1, keepdims=True)
            found.append(jnp.where(first_half, low, high))
        return jnp.concatenate(found, axis=1)

    bias = bias_ref[...]
    states = []
    for index, edge in enumerate(edges):
        window = first + index
        base = pl.ds(pl.multiple_of(window * (TOK - 1), 16), SPAN)
        row_index = iota((SPAN, 1), 0) - window
        row_in = (row_index >= 0) & (row_index < TOK)
        row_region = region_ids(row_index, edge, 8)
        lane_region = region_ids((iota((1, size), 1) & (SPAN - 1)) - window, edge, 16)
        query, key, value = (qkv[part, base, :] for part in range(3))
        states.append((window, base, row_in, row_region == lane_region, query, key, value, bias))
        bias = pltpu.roll(pltpu.roll(bias, 1, 0), 1, 1)
    bias_ref[...] = bias

    logits = [
        [
            jnp.where(
                allowed,
                dot_cols(
                    part_of(query, group, LANES), spread_heads(part_of(key, group, LANES), masks)
                )
                * (HD**-0.5)
                + part_of(shifted, group, size),
                NEG_FILL,
            )
            for group in groups
        ]
        for _, _, _, allowed, query, key, _, shifted in states
    ]
    terms = [[jnp.exp(values - tops(values)) for values in row] for row in logits]
    totals = [[dot(values.astype(BF16), ones) for values in row] for row in terms]
    probs = [
        [
            (terms[index][group] * (state[2].astype(F32) / totals[index][group])).astype(BF16)
            for group in groups
        ]
        for index, state in enumerate(states)
    ]
    attended = [
        jnp.concatenate(
            [
                dot(probs[index][group], spread_heads(part_of(state[6], group, LANES), masks))
                for group in groups
            ],
            axis=1,
        )
        for index, state in enumerate(states)
    ]
    for index, (window, base, row_in, *_) in enumerate(states):
        for group in groups:
            probs_ref[window, :, pl.ds(group * size, size)] = probs[index][group]
        before = att_ref[base, :].astype(F32)
        att_ref[base, :] = jnp.where(row_in, attended[index], before).astype(BF16)


def attention_backward(windows, qkv, d_att, probs_ref, d_bias_ref, d_qkv):
    masks = head_masks()
    size = GROUP * SPAN
    ones = same_head(size, size)
    groups = range(d_att.shape[1] // LANES)
    factor = HD**-0.5

    def part_of(array, group, width):
        return array[:, group * width : (group + 1) * width]

    states = []
    for window in windows:
        base = pl.ds(pl.multiple_of(window * (TOK - 1), 16), SPAN)
        query, key, value = (qkv[part, base, :] for part in range(3))
        states.append((base, query, key, value, d_att[base, :], probs_ref[window]))
    d_bias = d_bias_ref[...]

    weighted = [
        [
            dot_cols(
                part_of(upstream, group, LANES),
                spread_heads(part_of(value, group, LANES), masks),
            )
            * part_of(probs, group, size).astype(F32)
            for group in groups
        ]
        for _, _, _, value, upstream, probs in states
    ]
    deltas = [[dot(values.astype(BF16), ones) for values in row] for row in weighted]
    d_logits = [
        [
            (
                weighted[index][group]
                - part_of(state[5], group, size).astype(F32) * deltas[index][group]
            ).astype(BF16)
            for group in groups
        ]
        for index, state in enumerate(states)
    ]
    for row in d_logits:
        d_bias = pltpu.roll(pltpu.roll(d_bias, SPAN - 1, 0), d_bias.shape[1] - 1, 1)
        d_bias = d_bias + jnp.concatenate([values.astype(F32) for values in row], axis=1)
    d_bias_ref[...] = d_bias
    results = []
    for index, (base, query, key, value, upstream, probs) in enumerate(states):
        row = d_logits[index]
        d_query = [
            dot(row[group], spread_heads(part_of(key, group, LANES), masks)) * factor
            for group in groups
        ]
        d_key = [
            pick_heads(dot_rows(row[group], part_of(query, group, LANES))) * factor
            for group in groups
        ]
        d_value = [
            pick_heads(dot_rows(part_of(probs, group, size), part_of(upstream, group, LANES)))
            for group in groups
        ]
        results.append([jnp.concatenate(values, axis=1) for values in (d_query, d_key, d_value)])
    for index, window in enumerate(windows):
        base = states[index][0]
        row_index = iota((SPAN, 1), 0) - window
        row_in = (row_index >= 0) & (row_index < TOK)
        for part in range(3):
            old = d_qkv[part, base, :].astype(F32)
            d_qkv[part, base, :] = jnp.where(row_in, results[index][part], old).astype(BF16)


def sum_rows(values):
    return jnp.sum(values, 0, keepdims=True)


class Local:
    def __init__(self, refs, first_window):
        self.__dict__.update(refs)
        self.first_window = first_window
        self.rows, self.wide = self.x.shape
        self.width = self.section.shape[1]
        self.units = self.hidden.shape[1]
        self.windows = self.rows // TOK
        self.heads = self.width // HD
        self.chunk = 112
        self.steps = self.rows // self.chunk
        self.tile = self.units // self.gu.shape[0]

    def gain(self, row, lanes):
        return self.gains[row : row + 1, :lanes]

    def stat(self, at, index):
        return self.stats[at, index : index + 1]

    def keep_stats(self, at, index, mean, inv):
        self.stats[at, index : index + 1] = mean
        self.stats[at, index + 1 : index + 2] = inv

    def tiles(self):
        return [lax.axis_index("tp") ^ bits for bits in (3, 2, 1, 0)]

    def begin(self):
        for copy in self.arriving:
            copy.wait()
        self.early[...] = jnp.zeros_like(self.early)
        self.spread_vectors()

    def spread_vectors(self):
        for row, ref in enumerate(self.vectors):
            values = ref[...].astype(F32)
            for block in range(values.shape[0]):
                lanes = slice(block * LANES, (block + 1) * LANES)
                self.gains[row : row + 1, lanes] = values[block : block + 1]

    def prepare(self):
        def keep_rows(window):
            base = pl.ds(pl.multiple_of(window * (TOK - 1), 16), SPAN)
            index = iota((SPAN, 1), 0) - window
            inside = (index >= 0) & (index < TOK)
            valid = self.valid[self.first_window + window].astype(F32)
            self.stats[base, 6:7] = jnp.where(inside, valid, self.stats[base, 6:7])

        each(self.windows, keep_rows)

    def table_bias(self):
        build_bias(self.table(), self.spread, self.bias)

    def merge_norm(self):
        gain, shift = self.gain(0, self.wide), self.gain(1, self.wide)

        def step(index):
            at = rows_at(index, self.chunk)
            normed, mean, inv = norm_rows(self.x[at, :].astype(F32))
            self.merged[at, :] = (normed * gain + shift).astype(BF16)
            self.keep_stats(at, 0, mean, inv)

        each(self.steps, step)

    def merge(self):
        self.section[...] = dot(self.merged[...], self.wm[...]).astype(BF16)

    def attn_norm(self):
        gain, shift = self.gain(2, self.width), self.gain(3, self.width)

        def step(index):
            at = rows_at(index, self.chunk)
            normed, mean, inv = norm_rows(self.section[at, :].astype(F32))
            self.attn_in[at, :] = (normed * gain + shift).astype(BF16)
            self.keep_stats(at, 2, mean, inv)

        each(self.steps, step)

    def project(self, part):
        product = dot(self.attn_in[...], self.wqkv[part])
        if part != 1:
            product = product + self.qkv_bias(part)
        self.qkv[part] = product.astype(BF16)

    def attend(self, first, last, together=4):
        def step(index):
            window = first + index * together
            edges = [self.edge[self.first_window + window + more] for more in range(together)]
            attention_forward(window, edges, self.qkv, self.bias, self.probs, self.att)

        each((last - first) // together, step)

    def attn_out(self):
        self.pre[...] = dot(self.att[...], self.wp[...])

    def mlp_norm(self):
        gain, shift = self.gain(4, self.width), self.gain(5, self.width)
        proj_bias = self.gain(6, self.width)

        def step(index):
            at = rows_at(index, self.chunk)
            total = self.section[at, :].astype(F32) + self.pre[at, :] + proj_bias
            self.resid[at, :] = total
            normed, mean, inv = norm_rows(total)
            self.mlp_in[at, :] = (normed * gain + shift).astype(BF16)
            self.keep_stats(at, 4, mean, inv)

        each(self.steps, step)

    def up(self, index):
        columns = rows_at(index, self.tile)
        self.pre[...] = dot(self.mlp_in[...], self.wu[:, columns])
        shift = self.up_bias(index)

        def activate(step):
            at = rows_at(step, self.chunk)
            value, rate = gelu_both(self.pre[at, :] + shift)
            self.hidden[at, columns] = value.astype(BF16)
            self.slope[at, columns] = rate.astype(BF16)

        each(self.steps, activate, 7)
        put_blocks(self.gd, index, dot_rows(self.hidden[:, columns], self.d_mlp[...]))

    def down(self):
        self.pre[...] = dot(self.hidden[...], self.wd[...])

    def grad_rows(self):
        def step(index, total):
            at = rows_at(index, self.chunk)
            grad = self.grad_out[at, :].astype(F32) * self.stat(at, 6)
            self.d_mlp[at, :] = grad.astype(BF16)
            return total + fold(grad)

        total = lax.fori_loop(
            0, self.steps, step, jnp.zeros((8, self.width), F32)
        )
        self.put_sum(7, total)

    def finish(self):
        down_bias = self.gain(7, self.width)

        def step(index):
            at = rows_at(index, self.chunk)
            block = (self.resid[at, :] + self.pre[at, :] + down_bias) * self.stat(at, 6)
            self.out[at, :] = block.astype(BF16)

        each(self.steps, step)

    def hidden_back(self, index):
        columns = rows_at(index, self.tile)
        self.pre[...] = dot_cols(self.d_mlp[...], self.wd[columns, :])

        def activate(step, total):
            at = rows_at(step, self.chunk)
            grad = (self.pre[at, :] * self.slope[at, columns].astype(F32)).astype(BF16)
            self.d_pre[at, columns] = grad
            return total + fold(grad.astype(F32))

        total = lax.fori_loop(0, self.steps, activate, jnp.zeros((8, self.tile), F32))
        self.put_up_sum(index, total)
        put_blocks(self.gu, index, dot_rows(self.mlp_in[...], self.d_pre[:, columns]))

    def up_back(self):
        self.pre[...] = dot_cols(self.d_pre[...], self.wu[...])

    def mlp_back(self):
        gain = self.gain(4, self.width)

        def step(index, totals):
            at = rows_at(index, self.chunk)
            inv = self.stat(at, 5)
            normed = (self.resid[at, :] - self.stat(at, 4)) * inv
            upstream = self.pre[at, :]
            d_resid = self.d_mlp[at, :].astype(F32) + norm_back(upstream, normed, inv, gain)
            self.d_resid[at, :] = d_resid
            self.d_attn[at, :] = d_resid.astype(BF16)
            return (
                totals[0] + fold(upstream * normed),
                totals[1] + fold(upstream),
                totals[2] + fold(d_resid),
            )

        blank = jnp.zeros((8, self.width), F32)
        totals = lax.fori_loop(0, self.steps, step, (blank, blank, blank))
        for row, total in zip((5, 6, 4), totals):
            self.put_sum(row, total)

    def proj_back(self):
        size = self.width // self.gp.shape[0]
        product = dot_rows(self.att[...], self.d_attn[...])
        for index in range(self.gp.shape[0]):
            put_blocks(self.gp, index, product[index * size : (index + 1) * size])
        self.att[...] = dot_cols(self.d_attn[...], self.wp[...]).astype(BF16)
        self.d_bias[...] = jnp.zeros_like(self.d_bias)

    def attend_back(self, first, last, together=2):
        def step(index):
            top = last - 1 - index * together
            windows = [top - less for less in range(together)]
            attention_backward(windows, self.qkv, self.att, self.probs, self.d_bias, self.qkv)

        each((last - first) // together, step)

    def bias_back(self):
        self.put_table(reduce_bias(self.d_bias, self.spread, self.heads))
        ones = jnp.full((8, self.rows), 1.0, BF16)
        self.put_sum(8, dot(ones, self.qkv[0]), True)
        self.put_sum(9, dot(ones, self.qkv[2]), True)

    def qkv_weight_back(self):
        for part in range(3):
            put_columns(self.gqkv, part, dot_rows(self.attn_in[...], self.qkv[part]))

    def qkv_back(self):
        self.pre[...] = (
            dot_cols(self.qkv[0], self.wqkv[0])
            + dot_cols(self.qkv[1], self.wqkv[1])
            + dot_cols(self.qkv[2], self.wqkv[2])
        )

    def attn_back(self):
        gain = self.gain(2, self.width)

        def step(index, totals):
            at = rows_at(index, self.chunk)
            inv = self.stat(at, 3)
            normed = (self.section[at, :].astype(F32) - self.stat(at, 2)) * inv
            upstream = self.pre[at, :]
            d_section = self.d_resid[at, :] + norm_back(upstream, normed, inv, gain)
            self.d_mlp[at, :] = d_section.astype(BF16)
            return totals[0] + fold(upstream * normed), totals[1] + fold(upstream)

        blank = jnp.zeros((8, self.width), F32)
        totals = lax.fori_loop(0, self.steps, step, (blank, blank))
        self.put_sum(2, totals[0])
        self.put_sum(3, totals[1])

    def merge_weight_back(self):
        put_columns(self.gm, 0, dot_rows(self.merged[...], self.d_mlp[...]))

    def merge_in_back(self):
        for half, ref in enumerate((self.pre, self.d_resid)):
            rows = slice(half * self.width, (half + 1) * self.width)
            ref[...] = dot_cols(self.d_mlp[...], self.wm[rows, :])

    def merge_back(self, first, last, totals=None):
        gain = self.gain(0, self.wide)

        def step(index, totals):
            at = rows_at(first + index, 16)
            inv = self.stat(at, 1)
            normed = (self.x[at, :].astype(F32) - self.stat(at, 0)) * inv
            upstream = jnp.concatenate([self.pre[at, :], self.d_resid[at, :]], axis=1)
            self.d_in[at, :] = norm_back(upstream, normed, inv, gain)
            return totals[0] + fold(upstream * normed), totals[1] + fold(upstream)

        blank = jnp.zeros((8, self.wide), F32)
        totals = lax.fori_loop(0, last - first, step, totals or (blank, blank), unroll=7)
        if last == self.rows // 16:
            self.put_sum(0, totals[0])
            self.put_sum(1, totals[1])
        return totals

    def put_sum(self, row, values, summed=False):
        values = values[0:1] if summed else sum_rows(values)
        place, ref = SUM_ROWS[row], self.late
        if place >= LATE_ROWS:
            place, ref = place - LATE_ROWS, self.early
        for block in range(values.shape[1] // LANES):
            lanes = slice(block * LANES, (block + 1) * LANES)
            ref[place + block : place + block + 1, :] = values[:, lanes]

    def put_up_sum(self, index, total):
        values = sum_rows(total)
        blocks = self.tile // LANES
        for block in range(blocks):
            place = SUM_ROWS[10] - LATE_ROWS + index * blocks + block
            self.early[pl.ds(place, 1), :] = values[:, block * LANES : (block + 1) * LANES]

    def put_table(self, values):
        for half in range(2):
            place = SUM_ROWS[11] - LATE_ROWS + half * self.heads
            lanes = slice(half * LANES, (half + 1) * LANES)
            self.early[place : place + self.heads, :] = values[:, lanes]


SUM_ROWS = (0, 8, 16, 20, 24, 28, 32, 36, 40, 44, 48, 64)
LATE_ROWS = 16
SUM_SIZE = 96


def put_blocks(ref, shard, values):
    rows = values.shape[0]
    for block in range(values.shape[1] // LANES):
        at = pl.ds(block * rows, rows)
        ref[shard, at, :] = values[:, block * LANES : (block + 1) * LANES].astype(BF16)


def put_columns(ref, part, values):
    rows = values.shape[0]
    for shard in range(ref.shape[0]):
        piece = values[:, shard * LANES : (shard + 1) * LANES]
        ref[shard, part * rows : (part + 1) * rows, :] = piece.astype(BF16)


def local_scratch(rows, wide, width, units):
    heads = width // HD
    windows = rows // TOK
    return dict(
        merged=pltpu.VMEM((rows, wide), BF16),
        section=pltpu.VMEM((rows, width), BF16),
        attn_in=pltpu.VMEM((rows, width), BF16),
        qkv=pltpu.VMEM((3, rows, width), BF16),
        probs=pltpu.VMEM((windows, SPAN, heads * SPAN), BF16),
        att=pltpu.VMEM((rows, width), BF16),
        resid=pltpu.VMEM((rows, width), F32),
        mlp_in=pltpu.VMEM((rows, width), BF16),
        hidden=pltpu.VMEM((rows, units), BF16),
        slope=pltpu.VMEM((rows, units), BF16),
        pre=pltpu.VMEM((rows, width), F32),
        d_mlp=pltpu.VMEM((rows, width), BF16),
        d_pre=pltpu.VMEM((rows, units), BF16),
        d_attn=pltpu.VMEM((rows, width), BF16),
        d_resid=pltpu.VMEM((rows, width), F32),
        gains=pltpu.VMEM((8, wide), F32),
        stats=pltpu.VMEM((rows, 8), F32),
        bias=pltpu.VMEM((SPAN, heads * SPAN), F32),
        d_bias=pltpu.VMEM((SPAN, heads * SPAN), F32),
        spread=pltpu.VMEM((SPAN * heads, LANES), F32),
    )


MESH_ID = pl.DeviceIdType.MESH


class Links:
    def __init__(self, send_sems, recv_sems):
        self.send_sems, self.recv_sems = send_sems, recv_sems
        self.slots, self.sent = {}, []
        self.sp, self.tp = lax.axis_index("sp"), lax.axis_index("tp")

    def slot(self, label):
        return self.slots.setdefault(label, len(self.slots))

    def place(self, way):
        over_tp, distance = way
        if over_tp:
            return self.sp, self.tp ^ distance
        return self.sp ^ distance, self.tp

    def copy(self, label, way, source, target):
        slot = self.slot(label)
        return pltpu.make_async_remote_copy(
            src_ref=source,
            dst_ref=target,
            send_sem=self.send_sems.at[slot],
            recv_sem=self.recv_sems.at[slot],
            device_id=self.place(way),
            device_id_type=MESH_ID,
        )

    def send(self, label, way, source, target):
        copy = self.copy(label, way, source, target)
        copy.start()
        self.sent.append(copy)

    def receive(self, label, way, target):
        self.copy(label, way, target, target).wait_recv()

    def keep(self, label, source, target):
        copy = pltpu.make_async_copy(source, target, self.recv_sems.at[self.slot(label)])
        copy.start()
        return copy

    def greet(self, ways):
        barrier = pltpu.get_barrier_semaphore()
        for way in ways:
            pl.semaphore_signal(
                barrier, inc=1, device_id=self.place(way), device_id_type=MESH_ID
            )
        pl.semaphore_wait(barrier, len(ways))

    def drain(self):
        for copy in self.sent:
            copy.wait_send()


CORE, ACROSS, BESIDE = (True, 1), (True, 2), (False, 1)


def far(step):
    return False, 2 * step


class Gather:
    def __init__(self, links, label, own, whole, view, split=True):
        self.links, self.name, self.own, self.whole = links, label, own, whole
        self.view, self.split = view, split
        self.half = links.sp & 1 if split else None

    def part(self, shard, half=None):
        return self.view(self.whole, shard, half)

    def label(self, step):
        return self.name, step

    def start(self):
        links = self.links
        mine = links.tp
        source = self.view(self.own, None, None)
        self.local = links.keep(self.label(0), source, self.part(mine))
        links.send(
            self.label(1), ACROSS, self.view(self.own, None, self.half),
            self.part(mine, self.half),
        )
        links.send(self.label(2), CORE, source, self.part(mine))

    def forward(self):
        links = self.links
        block = self.part(links.tp ^ 2, self.half)
        links.receive(self.label(1), ACROSS, block)
        if self.split:
            links.send(self.label(3), BESIDE, block, block)
        links.send(self.label(4), CORE, block, block)

    def beside(self):
        links = self.links
        block = self.part(links.tp ^ 2, 1 - self.half)
        links.receive(self.label(3), BESIDE, block)
        links.send(self.label(5), CORE, block, block)

    def finish(self):
        links = self.links
        self.local.wait()
        links.receive(self.label(2), CORE, self.part(links.tp ^ 1))
        links.receive(self.label(4), CORE, self.part(links.tp ^ 3, self.half))
        if self.split:
            links.receive(self.label(5), CORE, self.part(links.tp ^ 3, 1 - self.half))


def column_view(size, first, rows):
    def view(ref, shard, half):
        start, count = (first, rows) if half is None else (first + half * (rows // 2), rows // 2)
        at = pl.ds(start if half is None else pl.multiple_of(start, 16), count)
        if shard is None:
            return ref.at[at, :]
        return ref.at[at, pl.ds(pl.multiple_of(shard * size, LANES), size)]

    return view


def row_view(size, first, rows):
    def view(ref, shard, half):
        start = first if shard is None else shard * size + first
        if half is None:
            return ref.at[pl.ds(start if shard is None else pl.multiple_of(start, 16), rows), :]
        return ref.at[pl.ds(pl.multiple_of(start + half * (rows // 2), 16), rows // 2), :]

    return view


def lead_view(ref, shard, half):
    return ref if shard is None else ref.at[shard]


def add_rows(target, start, rows, terms, chunk=128):
    chunk = math.gcd(rows, chunk)

    def step(index):
        offset = index * chunk

        def at(first):
            return pl.ds(pl.multiple_of(first + offset, 16), chunk)

        total = None
        for ref, first in terms:
            value = ref[at(first), :].astype(F32)
            total = value if total is None else total + value
        target[at(start), :] = total.astype(target.dtype)

    each(rows // chunk, step)


class Reduce:
    def __init__(self, links, label, grads, core_in, first_in, second_in, far_in, result, group,
                 across_first):
        self.links, self.name, self.grads = links, label, grads
        self.core_in, self.first_in, self.second_in = core_in, first_in, second_in
        self.far_in, self.result, self.group = far_in, result, group
        self.rows = grads.shape[1]
        self.half_rows = self.rows // 2
        self.piece = self.half_rows // group
        self.half = links.sp & 1
        self.seat = links.sp >> 1
        self.across = links.tp >> 1
        if across_first:
            self.add, self.first = self.core_add_across, self.across_beside
            self.second = self.beside_last
        else:
            self.add, self.first = self.core_add_beside, self.beside_across
            self.second = self.across_last

    def label(self, *step):
        return (self.name,) + step

    def rows_of(self, ref, half, piece=None):
        if piece is None:
            return ref.at[pl.ds(pl.multiple_of(half * self.half_rows, 16), self.half_rows), :]
        start = half * self.half_rows + piece * self.piece
        return ref.at[pl.ds(pl.multiple_of(start, 16), self.piece), :]

    def core_send(self, across, step):
        shard = (self.links.tp & 1) ^ 1 | 2 * across
        self.links.send(
            self.label(step), CORE, self.grads.at[shard], self.core_in.at[across]
        )

    def far(self):
        self.core_send(self.across ^ 1, 0)

    def near(self):
        self.core_send(self.across, 1)

    def receive_far(self):
        self.links.receive(self.label(0), CORE, self.core_in.at[self.across ^ 1])

    def receive_near(self):
        self.links.receive(self.label(1), CORE, self.core_in.at[self.across])

    def core_add_across(self):
        self.receive_far()
        other = self.links.tp ^ 2
        block = self.grads.at[other]
        add_rows(block, 0, self.rows, [(block, 0), (self.core_in.at[self.across ^ 1], 0)])
        self.links.send(self.label(2), ACROSS, block, self.first_in)

    def across_beside(self):
        links = self.links
        self.receive_near()
        links.receive(self.label(2), ACROSS, self.first_in)
        block = self.grads.at[links.tp]
        terms = [(block, 0), (self.core_in.at[self.across], 0), (self.first_in, 0)]
        add_rows(block, 0, self.rows, terms)
        links.send(
            self.label(3), BESIDE, self.rows_of(block, 1 - self.half), self.second_in
        )

    def beside_last(self):
        self.links.receive(self.label(3), BESIDE, self.second_in)
        self.add_and_spread([(self.second_in, 0)])

    def core_add_beside(self):
        links = self.links
        self.receive_far()
        self.receive_near()
        for across in range(2):
            block = self.grads.at[(links.tp & 1) | 2 * across]
            add_rows(block, 0, self.rows, [(block, 0), (self.core_in.at[across], 0)])
            links.send(
                self.label(3, across), BESIDE, self.rows_of(block, 1 - self.half),
                self.first_in.at[across],
            )

    def beside_across(self):
        links = self.links
        for across in range(2):
            links.receive(self.label(3, across), BESIDE, self.first_in.at[across])
        block = self.grads.at[links.tp ^ 2]
        mine = self.half * self.half_rows
        terms = [(block, mine), (self.first_in.at[self.across ^ 1], 0)]
        add_rows(block, mine, self.half_rows, terms)
        links.send(self.label(2), ACROSS, self.rows_of(block, self.half), self.second_in)

    def across_last(self):
        self.links.receive(self.label(2), ACROSS, self.second_in)
        self.add_and_spread([(self.first_in.at[self.across], 0), (self.second_in, 0)])

    def add_and_spread(self, terms):
        block = self.grads.at[self.links.tp]
        mine = self.half * self.half_rows
        add_rows(block, mine, self.half_rows, [(block, mine)] + terms)
        for step in range(1, self.group):
            self.links.send(
                self.label(4, step), far(step),
                self.rows_of(block, self.half, self.seat ^ step), self.far_in.at[step - 1],
            )

    def spread(self):
        links = self.links
        block = self.grads.at[links.tp]
        mine = self.half * self.half_rows + self.seat * self.piece
        terms = [(block, mine)]
        for step in range(1, self.group):
            links.receive(self.label(4, step), far(step), self.far_in.at[step - 1])
            terms.append((self.far_in.at[step - 1], 0))
        add_rows(self.result, mine, self.piece, terms)
        done = self.rows_of(self.result, self.half, self.seat)
        for step in range(1, self.group):
            links.send(self.label(5, step), far(step), done, done)

    def back(self):
        links = self.links
        for step in range(1, self.group):
            links.receive(
                self.label(5, step), far(step),
                self.rows_of(self.result, self.half, self.seat ^ step),
            )
        done = self.rows_of(self.result, self.half)
        links.send(self.label(6), BESIDE, done, done)

    def last(self):
        self.links.receive(
            self.label(6), BESIDE, self.rows_of(self.result, 1 - self.half)
        )


class Total:
    def __init__(self, links, label, stages, inboxes, seats, result):
        self.links, self.name, self.stages, self.inboxes = links, label, stages, inboxes
        self.seats, self.result = seats, result
        self.group = seats.shape[0]
        self.seat = links.sp >> 1

    def exchange(self, stage, way):
        self.links.send((self.name, stage), way, self.stages.at[stage], self.inboxes.at[stage])

    def take(self, stage, way):
        self.links.receive((self.name, stage), way, self.inboxes.at[stage])
        return self.stages[stage] + self.inboxes[stage]

    def send(self):
        self.exchange(0, CORE)

    def core(self):
        self.stages[1] = self.take(0, CORE)
        self.exchange(1, ACROSS)

    def across(self):
        self.stages[2] = self.take(1, ACROSS)
        self.exchange(2, BESIDE)

    def beside(self):
        mine = self.seats.at[self.seat]
        mine[...] = self.take(2, BESIDE)
        for step in range(1, self.group):
            self.links.send((self.name, 3, step), far(step), mine, mine)

    def last(self):
        for step in range(1, self.group):
            self.links.receive((self.name, 3, step), far(step), self.seats.at[self.seat ^ step])
        total = self.seats[0]
        for seat in range(1, self.group):
            total = total + self.seats[seat]
        self.result[...] = total


def schedule(local, g, u, done):
    windows = local.windows
    tiles = local.tiles()

    def attend_back(first, last):
        local.attend_back(windows - last * windows // 8, windows - first * windows // 8)

    local.begin()
    local.merge_norm()
    g.pack.forward()
    local.prepare()
    g.wm0.forward()
    local.grad_rows()
    g.wm1.forward()
    g.pack.finish()
    local.table_bias()
    g.wq.forward()
    g.wm0.beside()
    g.wk.forward()
    g.wm0.finish()
    g.wm1.beside()
    g.wv.forward()
    g.wm1.finish()
    local.merge()
    g.wq.beside()
    local.attn_norm()
    g.wk.beside()
    g.wv.beside()
    g.wu0.forward()
    g.wq.finish()
    local.project(0)
    g.wu1.forward()
    g.wk.finish()
    local.project(1)
    g.wv.finish()
    local.project(2)
    local.attend(0, windows // 4)
    g.wp.forward()
    local.attend(windows // 4, windows // 2)
    g.wu0.beside()
    g.wd0.forward()
    local.attend(windows // 2, 3 * windows // 4)
    local.attend(3 * windows // 4, windows)
    g.wu1.beside()
    g.wp.beside()
    g.wd1.forward()
    g.wp.finish()
    local.attn_out()
    local.mlp_norm()
    g.wd0.beside()
    g.wu0.finish()
    g.wu1.finish()
    local.up(tiles[0])
    g.wd1.beside()
    u.gd0.far()
    u.gd1.far()
    local.up(tiles[1])
    u.gd0.add()
    local.up(tiles[2])
    u.gd0.near()
    u.gd1.near()
    local.up(tiles[3])
    g.wd0.finish()
    g.wd1.finish()
    local.hidden_back(tiles[0])
    u.gd1.add()
    u.gu0.far()
    u.gu1.far()
    local.hidden_back(tiles[1])
    u.gu0.add()
    u.gd0.first()
    u.gu1.add()
    local.hidden_back(tiles[2])
    u.gu0.near()
    u.gu1.near()
    local.hidden_back(tiles[3])
    local.up_back()
    u.gd1.first()
    local.mlp_back()
    u.gu0.first()
    local.proj_back()
    u.gd0.second()
    u.gp0.far()
    u.gp0.near()
    attend_back(0, 2)
    u.gp0.add()
    attend_back(2, 4)
    u.gu1.first()
    u.gu0.second()
    attend_back(4, 6)
    u.gd0.spread()
    u.gd1.second()
    u.gp0.first()
    attend_back(6, 8)
    local.qkv_weight_back()
    u.gp0.second()
    u.gu1.second()
    u.gu0.spread()
    u.qkv0.far()
    u.qkv0.near()
    u.qkv1.far()
    u.qkv1.near()
    u.qkv2.far()
    u.qkv2.near()
    local.qkv_back()
    u.qkv1.add()
    u.gd0.back()
    u.qkv0.add()
    u.qkv2.add()
    local.attn_back()
    u.gd1.spread()
    local.merge_weight_back()
    u.gp0.spread()
    u.gm0.far()
    u.gm0.near()
    u.gm1.far()
    u.gm1.near()
    local.merge_in_back()
    u.qkv0.first()
    u.gm0.add()
    u.qkv1.first()
    u.gm1.add()
    u.gu1.spread()
    part = local.rows // 16 // 7
    totals = local.merge_back(0, 2 * part)
    totals = local.merge_back(2 * part, 5 * part, totals)
    u.qkv2.first()
    u.gu0.back()
    u.qkv0.second()
    local.bias_back()
    u.early.send()
    u.gm0.first()
    local.merge_back(5 * part, 7 * part, totals)
    done.d_in()
    u.late.send()
    u.gm1.first()
    u.early.core()
    u.gd1.back()
    u.qkv1.second()
    local.down()
    u.gp0.back()
    u.qkv2.second()
    u.late.core()
    local.finish()
    done.out()
    u.gu1.back()
    u.gm1.second()
    u.early.across()
    u.qkv0.spread()
    u.gm0.second()
    u.late.across()
    u.qkv1.spread()
    u.qkv2.spread()
    u.gm1.spread()
    u.qkv0.back()
    u.gm0.spread()
    u.early.beside()
    u.late.beside()
    u.qkv1.back()
    u.qkv2.back()
    u.gm1.back()
    u.gm0.back()
    u.gd0.last()
    u.gu0.last()
    u.gd1.last()
    u.gp0.last()
    u.gu1.last()
    u.qkv0.last()
    u.qkv1.last()
    u.qkv2.last()
    u.gm1.last()
    u.early.last()
    u.gm0.last()
    u.late.last()


SHARDS = 4
PIECES = 7


class Refs:
    def __init__(self, names, refs):
        self.__dict__.update(zip(names, refs, strict=True))


UNITS = dict(
    gd0=(0, 1024, True),
    gd1=(1024, 1024, False),
    gu0=(0, 1024, True),
    gu1=(1024, 1024, True),
    gp0=(0, 512, False),
    qkv0=(0, 512, True),
    qkv1=(512, 512, False),
    qkv2=(1024, 512, True),
    gm0=(0, 512, True),
    gm1=(512, 512, False),
)


def fill_pack(pack, rel, qv, ub):
    pack[...] = jnp.zeros_like(pack)
    pack[0 : rel.shape[0], 0:REL] = rel[...].astype(F32)
    pack[4:6, 0:LANES] = qv[...].astype(F32)
    for block in range(ub.shape[0]):
        lanes = slice(block * LANES, (block + 1) * LANES)
        pack[6:7, lanes] = ub[block : block + 1, :].astype(F32)


def gathers_of(links, r):
    wide, here = r.own_wm.shape
    width, tile = r.own_wu.shape
    columns = functools.partial(column_view, here)
    up = functools.partial(column_view, tile)
    down = functools.partial(row_view, tile)
    parts = dict(
        pack=(r.pack, r.packs, lead_view, False),
        wm0=(r.own_wm, r.wm, columns(0, wide // 2)),
        wm1=(r.own_wm, r.wm, columns(wide // 2, wide // 2)),
        wq=(r.own_wqkv.at[0], r.wqkv.at[0], columns(0, width)),
        wk=(r.own_wqkv.at[1], r.wqkv.at[1], columns(0, width)),
        wv=(r.own_wqkv.at[2], r.wqkv.at[2], columns(0, width)),
        wu0=(r.own_wu, r.wu, up(0, width // 2)),
        wu1=(r.own_wu, r.wu, up(width // 2, width // 2)),
        wp=(r.own_wp, r.wp, row_view(here, 0, here)),
        wd0=(r.own_wd, r.wd, down(0, tile // 2)),
        wd1=(r.own_wd, r.wd, down(tile // 2, tile // 2)),
    )
    made = [Gather(links, label, *part) for label, part in enumerate(parts.values())]
    return Refs(parts, made)


def reduces_of(links, r, boxes, first_label):
    grads = (r.gd, r.gd, r.gu, r.gu, r.gp, r.gqkv, r.gqkv, r.gqkv, r.gm, r.gm)
    results = (r.rd, r.rd, r.ru, r.ru, r.rp, r.rqkv, r.rqkv, r.rqkv, r.rm, r.rm)
    made = []
    for index, (first, size, across_first) in enumerate(UNITS.values()):
        at = pl.ds(first, size)
        group = boxes[index][3].shape[0] + 1
        made.append(
            Reduce(
                links, first_label + index, grads[index].at[:, at, :], *boxes[index],
                results[index].at[at, :], group, across_first,
            )
        )
    return Refs(UNITS, made)


def whole_kernel(names, group, *refs):
    boxes = refs[len(names) :]
    r = Refs(names, refs[: len(names)])
    links = Links(r.send_sems, r.recv_sems)
    arriving = [links.keep((-1, 0), r.h_x, r.x), links.keep((-1, 1), r.h_grad_out, r.grad_out)]
    fill_pack(r.pack, r.rel, r.qv, r.ub)
    links.greet([CORE, ACROSS, BESIDE] + [far(step) for step in range(1, group)])
    g = gathers_of(links, r)
    for gather in vars(g).values():
        gather.start()
    u = reduces_of(links, r, [boxes[4 * unit : 4 * unit + 4] for unit in range(len(UNITS))], 100)
    late, early = pl.ds(0, LATE_ROWS), pl.ds(LATE_ROWS, SUM_SIZE - LATE_ROWS)
    u.late = Total(links, 200, r.late_stages, r.late_in, r.late_seats, r.sums.at[late, :])
    u.early = Total(links, 201, r.early_stages, r.early_in, r.early_seats, r.sums.at[early, :])
    here = r.rel.shape[0]

    def table():
        parts = [r.packs[shard, 0:here, : 2 * LANES] for shard in range(SHARDS)]
        return jnp.concatenate(parts, axis=0)

    def qkv_bias(part):
        row = 4 if part == 0 else 5
        parts = [r.packs[shard, row : row + 1, :LANES] for shard in range(SHARDS)]
        return jnp.concatenate(parts, axis=1)

    def up_bias(index):
        return r.packs[index, 6:7, :]

    vectors = (
        r.merge_gain, r.merge_bias, r.attn_gain, r.attn_bias, r.mlp_gain, r.mlp_bias, r.proj_bias,
        r.down_bias,
    )
    fields = dict(
        vars(r), table=table, qkv_bias=qkv_bias, up_bias=up_bias, vectors=vectors,
        arriving=arriving, early=r.early_stages.at[0], late=r.late_stages.at[0],
    )
    local = Local(fields, links.tp * (r.x.shape[0] // TOK))
    leaving = []

    def put_d_in():
        leaving.append(links.keep((-1, 2), r.d_in, r.h_d_in))

    def put_out():
        leaving.append(links.keep((-1, 3), r.out, r.h_out))

    schedule(local, g, u, Refs(dict(d_in=0, out=0), (put_d_in, put_out)))
    for copy in leaving:
        copy.wait()
    links.drain()


def wide_rows(result, out):
    rows = out.shape[0]
    for block in range(out.shape[1] // LANES):
        lanes = slice(block * LANES, (block + 1) * LANES)
        out[:, lanes] = result[block * rows : (block + 1) * rows, :].astype(F32)


def finish_kernel(names, *refs):
    r = Refs(names, refs)
    tp = lax.axis_index("tp")
    pieces = []
    for source, target, held in ((r.h_d_in, r.o_d_in, r.v_d_in), (r.h_out, r.o_out, r.v_out)):
        size = held.shape[0] // PIECES
        for index in range(PIECES):
            at = pl.ds(index * size, size)
            number = 2 * len(pieces)
            pieces.append(
                (
                    pltpu.make_async_copy(source.at[at], held.at[at], r.sems.at[number]),
                    pltpu.make_async_copy(held.at[at], target.at[at], r.sems.at[number + 1]),
                )
            )
    for incoming, _ in pieces:
        incoming.start()
    vectors = (
        r.o_merge_gain, r.o_merge_bias, r.o_attn_gain, r.o_attn_bias, r.o_proj_bias, r.o_mlp_gain,
        r.o_mlp_bias, r.o_down_bias,
    )
    for row, out in enumerate(vectors):
        out[...] = r.sums[SUM_ROWS[row] : SUM_ROWS[row] + out.shape[0], :]
    for index in range(2):
        r.o_qv[index : index + 1, :] = r.sums[pl.ds(SUM_ROWS[8 + index] + tp, 1), :]
    blocks = r.o_ub.shape[0]
    for index in range(blocks):
        place = pl.ds(SUM_ROWS[10] + tp * blocks + index, 1)
        r.o_ub[index : index + 1, :] = r.sums[place, :]
    mine = r.o_rel.shape[0]
    for index in range(mine):
        first = SUM_ROWS[11] + tp * mine + index
        low, high = r.sums[pl.ds(first, 1), :], r.sums[pl.ds(first + SHARDS * mine, 1), :]
        r.o_rel[index : index + 1, :LANES] = low
        r.o_rel[index : index + 1, LANES:] = high[:, : REL - LANES]
    for incoming, outgoing in pieces:
        incoming.wait()
        outgoing.start()
    for result, out in ((r.rp, r.o_gp), (r.ru, r.o_gu), (r.rd, r.o_gd), (r.rm, r.o_gm)):
        wide_rows(result, out)
    rows = r.o_gqkv.shape[1]
    for part in range(r.o_gqkv.shape[0]):
        r.o_gqkv[part] = r.rqkv[part * rows : (part + 1) * rows, :].astype(F32)
    for _, outgoing in pieces:
        outgoing.wait()


VMEM_SPEC = pl.BlockSpec(memory_space=pltpu.VMEM)
SMEM_SPEC = pl.BlockSpec(memory_space=pltpu.SMEM)
HBM_SPEC = pl.BlockSpec(memory_space=pl.ANY)


def whole_call(group, small, large):
    rows, wide = large["h_x"].shape
    width, tile = large["own_wu"].shape
    units = SHARDS * tile
    scratch = local_scratch(rows, wide, width, units)
    block = lambda *shape: pltpu.VMEM(shape, BF16)
    exact = lambda *shape: pltpu.VMEM(shape, F32)
    early = SUM_SIZE - LATE_ROWS
    count = 11 * 6 + len(UNITS) * (6 + 2 * group) + 2 * (3 + group) + 4
    scratch.update(
        wm=block(wide, width), wqkv=block(3, width, width), wp=block(width, width),
        wu=block(width, units), wd=block(units, width), pack=exact(8, tile),
        packs=exact(SHARDS, 8, tile), x=block(rows, wide), grad_out=block(rows, width),
        out=block(rows, width), d_in=exact(rows, wide), gd=block(SHARDS, units, LANES),
        gu=block(SHARDS, units, LANES), gp=block(SHARDS, width, LANES),
        gqkv=block(SHARDS, 3 * width, LANES), gm=block(SHARDS, wide, LANES),
        late_stages=exact(3, LATE_ROWS, LANES), late_in=exact(3, LATE_ROWS, LANES),
        late_seats=exact(group, LATE_ROWS, LANES), early_stages=exact(3, early, LANES),
        early_in=exact(3, early, LANES), early_seats=exact(group, early, LANES),
        send_sems=pltpu.SemaphoreType.DMA((count,)), recv_sems=pltpu.SemaphoreType.DMA((count,)),
    )
    boxes = []
    for _, size, across_first in UNITS.values():
        half = size // 2
        boxes += [
            block(2, size, LANES),
            block(size, LANES) if across_first else block(2, half, LANES),
            block(half, LANES),
            block(group - 1, half // group, LANES),
        ]
    result = lambda size: jax.ShapeDtypeStruct((size, LANES), BF16)
    outs = dict(
        h_out=jax.ShapeDtypeStruct((rows, width), BF16),
        h_d_in=jax.ShapeDtypeStruct((rows, wide), F32),
        rd=result(units), ru=result(units), rp=result(width), rqkv=result(3 * width),
        rm=result(wide), sums=jax.ShapeDtypeStruct((SUM_SIZE, LANES), F32),
    )
    names = tuple(small) + tuple(large) + tuple(outs) + tuple(scratch)
    made = pl.pallas_call(
        functools.partial(whole_kernel, names, group),
        out_shape=list(outs.values()),
        in_specs=[SMEM_SPEC] * 2 + [VMEM_SPEC] * (len(small) - 2) + [HBM_SPEC] * len(large),
        out_specs=[HBM_SPEC] * 2 + [VMEM_SPEC] * (len(outs) - 2),
        scratch_shapes=list(scratch.values()) + boxes,
        compiler_params=pltpu.CompilerParams(
            vmem_limit_bytes=63 * MIB, collective_id=0, has_side_effects=True
        ),
    )(*small.values(), *large.values())
    return dict(zip(outs, made, strict=True))


def finish_call(results, shapes):
    (rows, width), (_, wide) = shapes["o_out"].shape, shapes["o_d_in"].shape
    scratch = dict(
        v_out=pltpu.VMEM((rows, width), BF16), v_d_in=pltpu.VMEM((rows, wide), F32),
        sems=pltpu.SemaphoreType.DMA((4 * PIECES,)),
    )
    names = tuple(results) + tuple(shapes) + tuple(scratch)
    made = pl.pallas_call(
        functools.partial(finish_kernel, names),
        out_shape=list(shapes.values()),
        in_specs=[HBM_SPEC] * 2 + [VMEM_SPEC] * (len(results) - 2),
        out_specs=[HBM_SPEC] * 2 + [VMEM_SPEC] * (len(shapes) - 2),
        scratch_shapes=list(scratch.values()),
        compiler_params=pltpu.CompilerParams(vmem_limit_bytes=63 * MIB),
    )(*results.values())
    return Refs(shapes, made)


def on_device(
    inputs, grad_out, window_valid, window_edge, merge_gain, merge_bias, merge_weight, attn_gain,
    attn_bias, query_key_value_weight, qv_bias, rel_table, proj_weight, proj_bias, mlp_gain,
    mlp_bias, up_weight, up_bias, down_weight, down_bias,
):
    lines = lambda vector: vector.reshape(-1, LANES)
    small = dict(
        valid=window_valid, edge=window_edge, rel=rel_table.T, qv=qv_bias, ub=lines(up_bias),
        merge_gain=lines(merge_gain), merge_bias=lines(merge_bias), attn_gain=lines(attn_gain),
        attn_bias=lines(attn_bias), mlp_gain=lines(mlp_gain), mlp_bias=lines(mlp_bias),
        proj_bias=lines(proj_bias), down_bias=lines(down_bias),
    )
    qkv = jnp.transpose(query_key_value_weight, (1, 0, 2))
    large = dict(
        h_x=inputs, h_grad_out=grad_out, own_wm=merge_weight, own_wqkv=qkv, own_wp=proj_weight,
        own_wu=up_weight, own_wd=down_weight,
    )
    results = whole_call(lax.axis_size("sp") // 2, small, large)
    like = lambda array: jax.ShapeDtypeStruct(array.shape, F32)
    shapes = dict(
        o_out=jax.ShapeDtypeStruct(grad_out.shape, BF16), o_d_in=like(inputs),
        o_gm=like(merge_weight), o_gqkv=like(qkv), o_gp=like(proj_weight), o_gu=like(up_weight),
        o_gd=like(down_weight), o_qv=like(qv_bias), o_rel=like(rel_table.T),
        o_ub=like(lines(up_bias)), o_merge_gain=like(lines(merge_gain)),
        o_merge_bias=like(lines(merge_bias)), o_attn_gain=like(lines(attn_gain)),
        o_attn_bias=like(lines(attn_bias)), o_proj_bias=like(lines(proj_bias)),
        o_mlp_gain=like(lines(mlp_gain)), o_mlp_bias=like(lines(mlp_bias)),
        o_down_bias=like(lines(down_bias)),
    )
    done = finish_call(results, shapes)
    flat = lambda block: block.reshape(-1)
    return (
        done.o_out, done.o_d_in, flat(done.o_merge_gain), flat(done.o_merge_bias), done.o_gm,
        flat(done.o_attn_gain), flat(done.o_attn_bias), jnp.transpose(done.o_gqkv, (1, 0, 2)),
        done.o_qv, done.o_rel.T, done.o_gp, flat(done.o_proj_bias), flat(done.o_mlp_gain),
        flat(done.o_mlp_bias), done.o_gu, flat(done.o_ub), done.o_gd, flat(done.o_down_bias),
    )


def solution(mesh):
    placed = (
        P(("sp", "tp"), None),
        P(("sp", "tp"), None),
        P("sp"),
        P("sp"),
        P(),
        P(),
        P(None, "tp"),
        P(),
        P(),
        P(None, None, "tp"),
        P(None, "tp"),
        P(None, "tp"),
        P("tp", None),
        P(),
        P(),
        P(),
        P(None, "tp"),
        P("tp"),
        P("tp", None),
        P(),
    )
    return jax.shard_map(
        on_device,
        mesh=mesh,
        in_specs=placed,
        out_specs=(
            P(("sp", "tp"), None),
            P(("sp", "tp"), None),
            P(),
            P(),
            P(None, "tp"),
            P(),
            P(),
            P(None, None, "tp"),
            P(None, "tp"),
            P(None, "tp"),
            P("tp", None),
            P(),
            P(),
            P(),
            P(None, "tp"),
            P("tp"),
            P("tp", None),
            P(),
        ),
        check_vma=False,
    )
```

```python
import functools
import math

import jax
import jax.numpy as jnp
from jax import lax
from jax.experimental import pallas as pl
from jax.experimental.pallas import tpu as pltpu
from jax.sharding import PartitionSpec as P

SIDE = 7
TOK = SIDE * SIDE
REL_SIDE = 2 * SIDE - 1
REL = REL_SIDE * REL_SIDE
SPAN = 64
GROUP = 4
HD = 32
LANES = 128
EPSILON = 1e-05
NEG_FILL = -1000000000.0
MIB = 1 << 20
F32 = jnp.float32
BF16 = jnp.bfloat16


def dot(left, right):
    return jnp.dot(left, right, preferred_element_type=F32)


def dot_cols(left, right):
    return lax.dot_general(left, right, (((1,), (1,)), ((), ())), preferred_element_type=F32)


def dot_rows(left, right):
    return lax.dot_general(left, right, (((0,), (0,)), ((), ())), preferred_element_type=F32)


def rows_at(index, size):
    return pl.ds(pl.multiple_of(index * size, size), size)


def each(count, body, unroll=1):
    def step(index, carry):
        body(index)
        return carry

    lax.fori_loop(0, count, step, 0, unroll=unroll)


def fold(values):
    total = values[0:8]
    for start in range(8, values.shape[0], 8):
        total = total + values[start : start + 8]
    return total


def iota(shape, dim):
    return lax.broadcasted_iota(jnp.int32, shape, dim)


def norm_rows(values):
    mean = jnp.mean(values, -1, keepdims=True)
    centred = values - mean
    inv = lax.rsqrt(jnp.mean(centred * centred, -1, keepdims=True) + EPSILON)
    return centred * inv, mean, inv


def norm_back(upstream, normed, inv, gain):
    scaled = upstream * gain
    return inv * (
        scaled
        - jnp.mean(scaled, -1, keepdims=True)
        - normed * jnp.mean(scaled * normed, -1, keepdims=True)
    )


def gelu_both(values):
    bell = jnp.exp2(values * values * -0.7213475204444817)
    span = 1.0 + 0.23164190 * jnp.abs(values)
    t = pltpu.reciprocal(span, approx=True)
    t = t * (2.0 - span * t)
    poly = t * (
        0.127414796
        + t * (-0.142248368 + t * (0.7107068705 + t * (-0.7265760135 + t * 0.5307027145)))
    )
    tail = poly * bell
    phi = jnp.where(values >= 0, 1.0 - tail, tail)
    return values * phi, phi + values * bell * 0.3989422804014327


def window_row_col(index):
    row = (index * 37) >> 8
    return row, index - SIDE * row


def region_ids(index, edge, outside):
    row, col = window_row_col(index)
    high = SIDE - SIDE // 2
    region = (edge & 1) * (col >= high).astype(jnp.int32) + 2 * (edge >> 1) * (
        row >= high
    ).astype(jnp.int32)
    return jnp.where((index >= 0) & (index < TOK), region, outside)


def head_masks():
    lane = iota((1, LANES), 1)
    return [((lane >> 5) == head).astype(F32).astype(BF16) for head in range(GROUP)]


def spread_heads(block, masks):
    return jnp.concatenate([block * mask for mask in masks], axis=0)


def pick_heads(product):
    lane = iota((SPAN, LANES), 1)
    result = product[3 * SPAN : 4 * SPAN]
    for head in (2, 1, 0):
        result = jnp.where(
            lane < (head + 1) * HD, product[head * SPAN : (head + 1) * SPAN], result
        )
    return result


def same_head(rows, columns):
    return (
        (iota((rows, columns), 0) // (rows // GROUP))
        == (iota((rows, columns), 1) // (columns // GROUP))
    ).astype(F32).astype(BF16)


def offset_select(half):
    place = iota((LANES, LANES), 0)
    lane = iota((LANES, LANES), 1)
    token = lane - half * SPAN
    row, col = window_row_col(token & (SPAN - 1))
    wanted = (SIDE - 1) * (REL_SIDE + 1) - (REL_SIDE * row + col)
    hit = (place == wanted) & (token >= 0) & (token < TOK)
    return hit.astype(F32).astype(BF16)


def build_bias(table, spread_ref, bias_ref):
    heads = table.shape[0]

    def one(index):
        row = index // SIDE
        shift = index + (SIDE - 1) * row
        rolled = pltpu.roll(table, (2 * LANES - shift) % (2 * LANES), 1)
        spread_ref[rows_at(index, heads), :] = rolled[:, :LANES]

    spread_ref[...] = jnp.zeros_like(spread_ref)
    for index in range(TOK):
        one(index)
    low, high = offset_select(0), offset_select(1)
    for pair in range(heads // 2):
        first = spread_ref[pl.ds(2 * pair, SPAN, stride=heads), :].astype(BF16)
        second = spread_ref[pl.ds(2 * pair + 1, SPAN, stride=heads), :].astype(BF16)
        bias_ref[:, pair * LANES : (pair + 1) * LANES] = dot(first, low) + dot(second, high)


def split_bf16(values):
    high = values.astype(BF16)
    return high, (values - high.astype(F32)).astype(BF16)


def reduce_bias(bias_ref, spread_ref, heads):
    low, high = offset_select(0), offset_select(1)
    for pair in range(heads // 2):
        parts = split_bf16(bias_ref[:, pair * LANES : (pair + 1) * LANES])
        spread_ref[pl.ds(2 * pair, SPAN, stride=heads), :] = sum(
            dot_cols(part, low) for part in parts
        )
        spread_ref[pl.ds(2 * pair + 1, SPAN, stride=heads), :] = sum(
            dot_cols(part, high) for part in parts
        )
    total = jnp.zeros((heads, 2 * LANES), F32)
    blank = jnp.zeros((heads, LANES), F32)
    for index in range(TOK):
        shift = index + (SIDE - 1) * (index // SIDE)
        row = jnp.concatenate([spread_ref[index * heads : (index + 1) * heads, :], blank], axis=1)
        total = total + (pltpu.roll(row, shift, 1) if shift else row)
    return total


def shift_both(ref, forward):
    rows, columns = ref.shape
    down, right = (1, 1) if forward else (rows - 1, columns - 1)
    ref[...] = pltpu.roll(pltpu.roll(ref[...], down, 0), right, 1)


def attention_forward(first, edges, qkv, bias_ref, probs_ref, att_ref):
    masks = head_masks()
    size = GROUP * SPAN
    ones = same_head(size, size)
    first_half = iota((SPAN, LANES), 1) < SPAN
    groups = range(att_ref.shape[1] // LANES)

    def part_of(array, group, width):
        return array[:, group * width : (group + 1) * width]

    def tops(values):
        found = []
        for half in range(size // LANES):
            piece = part_of(values, half, LANES)
            low = jnp.max(jnp.where(first_half, piece, 2 * NEG_FILL), -1, keepdims=True)
            high = jnp.max(jnp.where(first_half, 2 * NEG_FILL, piece), -1, keepdims=True)
            found.append(jnp.where(first_half, low, high))
        return jnp.concatenate(found, axis=1)

    bias = bias_ref[...]
    states = []
    for index, edge in enumerate(edges):
        window = first + index
        base = pl.ds(pl.multiple_of(window * (TOK - 1), 16), SPAN)
        row_index = iota((SPAN, 1), 0) - window
        row_in = (row_index >= 0) & (row_index < TOK)
        row_region = region_ids(row_index, edge, 8)
        lane_region = region_ids((iota((1, size), 1) & (SPAN - 1)) - window, edge, 16)
        query, key, value = (qkv[part, base, :] for part in range(3))
        states.append((window, base, row_in, row_region == lane_region, query, key, value, bias))
        bias = pltpu.roll(pltpu.roll(bias, 1, 0), 1, 1)
    bias_ref[...] = bias

    logits = [
        [
            jnp.where(
                allowed,
                dot_cols(
                    part_of(query, group, LANES), spread_heads(part_of(key, group, LANES), masks)
                )
                * (HD**-0.5)
                + part_of(shifted, group, size),
                NEG_FILL,
            )
            for group in groups
        ]
        for _, _, _, allowed, query, key, _, shifted in states
    ]
    terms = [[jnp.exp(values - tops(values)) for values in row] for row in logits]
    totals = [[dot(values.astype(BF16), ones) for values in row] for row in terms]
    probs = [
        [
            (terms[index][group] * (state[2].astype(F32) / totals[index][group])).astype(BF16)
            for group in groups
        ]
        for index, state in enumerate(states)
    ]
    attended = [
        jnp.concatenate(
            [
                dot(probs[index][group], spread_heads(part_of(state[6], group, LANES), masks))
                for group in groups
            ],
            axis=1,
        )
        for index, state in enumerate(states)
    ]
    for index, (window, base, row_in, *_) in enumerate(states):
        for group in groups:
            probs_ref[window, :, pl.ds(group * size, size)] = probs[index][group]
        before = att_ref[base, :].astype(F32)
        att_ref[base, :] = jnp.where(row_in, attended[index], before).astype(BF16)


def attention_backward(windows, qkv, d_att, probs_ref, d_bias_ref, d_qkv):
    masks = head_masks()
    size = GROUP * SPAN
    ones = same_head(size, size)
    groups = range(d_att.shape[1] // LANES)
    factor = HD**-0.5

    def part_of(array, group, width):
        return array[:, group * width : (group + 1) * width]

    states = []
    for window in windows:
        base = pl.ds(pl.multiple_of(window * (TOK - 1), 16), SPAN)
        query, key, value = (qkv[part, base, :] for part in range(3))
        states.append((base, query, key, value, d_att[base, :], probs_ref[window]))
    d_bias = d_bias_ref[...]

    weighted = [
        [
            dot_cols(
                part_of(upstream, group, LANES),
                spread_heads(part_of(value, group, LANES), masks),
            )
            * part_of(probs, group, size).astype(F32)
            for group in groups
        ]
        for _, _, _, value, upstream, probs in states
    ]
    deltas = [[dot(values.astype(BF16), ones) for values in row] for row in weighted]
    d_logits = [
        [
            (
                weighted[index][group]
                - part_of(state[5], group, size).astype(F32) * deltas[index][group]
            ).astype(BF16)
            for group in groups
        ]
        for index, state in enumerate(states)
    ]
    for row in d_logits:
        d_bias = pltpu.roll(pltpu.roll(d_bias, SPAN - 1, 0), d_bias.shape[1] - 1, 1)
        d_bias = d_bias + jnp.concatenate([values.astype(F32) for values in row], axis=1)
    d_bias_ref[...] = d_bias
    results = []
    for index, (base, query, key, value, upstream, probs) in enumerate(states):
        row = d_logits[index]
        d_query = [
            dot(row[group], spread_heads(part_of(key, group, LANES), masks)) * factor
            for group in groups
        ]
        d_key = [
            pick_heads(dot_rows(row[group], part_of(query, group, LANES))) * factor
            for group in groups
        ]
        d_value = [
            pick_heads(dot_rows(part_of(probs, group, size), part_of(upstream, group, LANES)))
            for group in groups
        ]
        results.append([jnp.concatenate(values, axis=1) for values in (d_query, d_key, d_value)])
    for index, window in enumerate(windows):
        base = states[index][0]
        row_index = iota((SPAN, 1), 0) - window
        row_in = (row_index >= 0) & (row_index < TOK)
        for part in range(3):
            old = d_qkv[part, base, :].astype(F32)
            d_qkv[part, base, :] = jnp.where(row_in, results[index][part], old).astype(BF16)


def sum_rows(values):
    return jnp.sum(values, 0, keepdims=True)


class Local:
    def __init__(self, refs, first_window):
        self.__dict__.update(refs)
        self.first_window = first_window
        self.rows, self.wide = self.x.shape
        self.width = self.section.shape[1]
        self.units = self.hidden.shape[1]
        self.windows = self.rows // TOK
        self.heads = self.width // HD
        self.chunk = self.rows
        self.steps = self.rows // self.chunk
        self.tile = self.units // self.gu.shape[0]

    def gain(self, row, lanes):
        return self.gains[row : row + 1, :lanes]

    def stat(self, at, index):
        return self.stats[at, index : index + 1]

    def keep_stats(self, at, index, mean, inv):
        self.stats[at, index : index + 1] = mean
        self.stats[at, index + 1 : index + 2] = inv

    def tiles(self):
        return [lax.axis_index("tp") ^ bits for bits in (3, 2, 1, 0)]

    def begin(self):
        for copy in self.arriving:
            copy.wait()
        self.early[...] = jnp.zeros_like(self.early)
        self.spread_vectors()

    def spread_vectors(self):
        for row, ref in enumerate(self.vectors):
            values = ref[...].astype(F32)
            for block in range(values.shape[0]):
                lanes = slice(block * LANES, (block + 1) * LANES)
                self.gains[row : row + 1, lanes] = values[block : block + 1]

    def prepare(self):
        def keep_rows(window):
            base = pl.ds(pl.multiple_of(window * (TOK - 1), 16), SPAN)
            index = iota((SPAN, 1), 0) - window
            inside = (index >= 0) & (index < TOK)
            valid = self.valid[self.first_window + window].astype(F32)
            self.stats[base, 6:7] = jnp.where(inside, valid, self.stats[base, 6:7])

        each(self.windows, keep_rows)

    def table_bias(self):
        build_bias(self.table(), self.spread, self.bias)

    def merge_norm(self):
        gain, shift = self.gain(0, self.wide), self.gain(1, self.wide)

        def step(index):
            at = rows_at(index, self.chunk)
            normed, mean, inv = norm_rows(self.x[at, :].astype(F32))
            self.merged[at, :] = (normed * gain + shift).astype(BF16)
            self.keep_stats(at, 0, mean, inv)

        each(self.steps, step)

    def merge(self):
        self.section[...] = dot(self.merged[...], self.wm[...]).astype(BF16)

    def attn_norm(self):
        gain, shift = self.gain(2, self.width), self.gain(3, self.width)

        def step(index):
            at = rows_at(index, self.chunk)
            normed, mean, inv = norm_rows(self.section[at, :].astype(F32))
            self.attn_in[at, :] = (normed * gain + shift).astype(BF16)
            self.keep_stats(at, 2, mean, inv)

        each(self.steps, step)

    def project(self, part):
        product = dot(self.attn_in[...], self.wqkv[part])
        if part != 1:
            product = product + self.qkv_bias(part)
        self.qkv[part] = product.astype(BF16)

    def attend(self, first, last, together=4):
        def step(index):
            window = first + index * together
            edges = [self.edge[self.first_window + window + more] for more in range(together)]
            attention_forward(window, edges, self.qkv, self.bias, self.probs, self.att)

        each((last - first) // together, step)

    def attn_out(self):
        self.pre[...] = dot(self.att[...], self.wp[...])

    def mlp_norm(self):
        gain, shift = self.gain(4, self.width), self.gain(5, self.width)
        proj_bias = self.gain(6, self.width)

        def step(index):
            at = rows_at(index, self.chunk)
            total = self.section[at, :].astype(F32) + self.pre[at, :] + proj_bias
            self.resid[at, :] = total
            normed, mean, inv = norm_rows(total)
            self.mlp_in[at, :] = (normed * gain + shift).astype(BF16)
            self.keep_stats(at, 4, mean, inv)

        each(self.steps, step)

    def up(self, index):
        columns = rows_at(index, self.tile)
        shift = self.up_bias(index)
        value, rate = gelu_both(dot(self.mlp_in[...], self.wu[:, columns]) + shift)
        self.hidden[:, columns] = value.astype(BF16)
        self.slope[:, columns] = rate.astype(BF16)
        put_blocks(self.gd, index, dot_rows(value.astype(BF16), self.d_mlp[...]))

    def down(self):
        self.pre[...] = dot(self.hidden[...], self.wd[...])

    def grad_rows(self):
        def step(index, total):
            at = rows_at(index, self.chunk)
            grad = self.grad_out[at, :].astype(F32) * self.stat(at, 6)
            self.d_mlp[at, :] = grad.astype(BF16)
            return total + fold(grad)

        total = lax.fori_loop(
            0, self.steps, step, jnp.zeros((8, self.width), F32)
        )
        self.put_sum(7, total)

    def finish(self):
        down_bias = self.gain(7, self.width)

        def step(index):
            at = rows_at(index, self.chunk)
            block = (self.resid[at, :] + self.pre[at, :] + down_bias) * self.stat(at, 6)
            self.out[at, :] = block.astype(BF16)

        each(self.steps, step)

    def hidden_back(self, index):
        columns = rows_at(index, self.tile)
        slope = self.slope[:, columns].astype(F32)
        grad = (dot_cols(self.d_mlp[...], self.wd[columns, :]) * slope).astype(BF16)
        self.d_pre[:, columns] = grad
        self.put_up_sum(index, fold(grad.astype(F32)))
        put_blocks(self.gu, index, dot_rows(self.mlp_in[...], grad))

    def up_back(self):
        self.pre[...] = dot_cols(self.d_pre[...], self.wu[...])

    def mlp_back(self):
        gain = self.gain(4, self.width)

        def step(index, totals):
            at = rows_at(index, self.chunk)
            inv = self.stat(at, 5)
            normed = (self.resid[at, :] - self.stat(at, 4)) * inv
            upstream = self.pre[at, :]
            d_resid = self.d_mlp[at, :].astype(F32) + norm_back(upstream, normed, inv, gain)
            self.d_resid[at, :] = d_resid
            self.d_attn[at, :] = d_resid.astype(BF16)
            return (
                totals[0] + fold(upstream * normed),
                totals[1] + fold(upstream),
                totals[2] + fold(d_resid),
            )

        blank = jnp.zeros((8, self.width), F32)
        totals = lax.fori_loop(0, self.steps, step, (blank, blank, blank))
        for row, total in zip((5, 6, 4), totals):
            self.put_sum(row, total)

    def proj_back(self):
        size = self.width // self.gp.shape[0]
        product = dot_rows(self.att[...], self.d_attn[...])
        for index in range(self.gp.shape[0]):
            put_blocks(self.gp, index, product[index * size : (index + 1) * size])
        self.att[...] = dot_cols(self.d_attn[...], self.wp[...]).astype(BF16)
        self.d_bias[...] = jnp.zeros_like(self.d_bias)

    def attend_back(self, first, last, together=4):
        def step(index):
            top = last - 1 - index * together
            windows = [top - less for less in range(together)]
            attention_backward(windows, self.qkv, self.att, self.probs, self.d_bias, self.qkv)

        each((last - first) // together, step)

    def bias_back(self):
        self.put_table(reduce_bias(self.d_bias, self.spread, self.heads))
        ones = jnp.full((8, self.rows), 1.0, BF16)
        self.put_sum(8, dot(ones, self.qkv[0]), True)
        self.put_sum(9, dot(ones, self.qkv[2]), True)

    def qkv_weight_back(self):
        for part in range(3):
            put_columns(self.gqkv, part, dot_rows(self.attn_in[...], self.qkv[part]))

    def qkv_back(self):
        self.pre[...] = (
            dot_cols(self.qkv[0], self.wqkv[0])
            + dot_cols(self.qkv[1], self.wqkv[1])
            + dot_cols(self.qkv[2], self.wqkv[2])
        )

    def attn_back(self):
        gain = self.gain(2, self.width)

        def step(index, totals):
            at = rows_at(index, self.chunk)
            inv = self.stat(at, 3)
            normed = (self.section[at, :].astype(F32) - self.stat(at, 2)) * inv
            upstream = self.pre[at, :]
            d_section = self.d_resid[at, :] + norm_back(upstream, normed, inv, gain)
            self.d_mlp[at, :] = d_section.astype(BF16)
            return totals[0] + fold(upstream * normed), totals[1] + fold(upstream)

        blank = jnp.zeros((8, self.width), F32)
        totals = lax.fori_loop(0, self.steps, step, (blank, blank))
        self.put_sum(2, totals[0])
        self.put_sum(3, totals[1])

    def merge_weight_back(self):
        put_columns(self.gm, 0, dot_rows(self.merged[...], self.d_mlp[...]))

    def merge_in_back(self):
        for half, ref in enumerate((self.pre, self.d_resid)):
            rows = slice(half * self.width, (half + 1) * self.width)
            ref[...] = dot_cols(self.d_mlp[...], self.wm[rows, :])

    def merge_back(self, first, last, totals=None):
        gain = self.gain(0, self.wide)

        def step(index, totals):
            at = pl.ds(first * 16, (last - first) * 16)
            inv = self.stat(at, 1)
            normed = (self.x[at, :].astype(F32) - self.stat(at, 0)) * inv
            upstream = jnp.concatenate([self.pre[at, :], self.d_resid[at, :]], axis=1)
            self.d_in[at, :] = norm_back(upstream, normed, inv, gain)
            return totals[0] + fold(upstream * normed), totals[1] + fold(upstream)

        blank = jnp.zeros((8, self.wide), F32)
        totals = step(0, totals or (blank, blank))
        if last == self.rows // 16:
            self.put_sum(0, totals[0])
            self.put_sum(1, totals[1])
        return totals

    def put_sum(self, row, values, summed=False):
        values = values[0:1] if summed else sum_rows(values)
        place, ref = SUM_ROWS[row], self.late
        if place >= LATE_ROWS:
            place, ref = place - LATE_ROWS, self.early
        for block in range(values.shape[1] // LANES):
            lanes = slice(block * LANES, (block + 1) * LANES)
            ref[place + block : place + block + 1, :] = values[:, lanes]

    def put_up_sum(self, index, total):
        values = sum_rows(total)
        blocks = self.tile // LANES
        for block in range(blocks):
            place = SUM_ROWS[10] - LATE_ROWS + index * blocks + block
            self.early[pl.ds(place, 1), :] = values[:, block * LANES : (block + 1) * LANES]

    def put_table(self, values):
        for half in range(2):
            place = SUM_ROWS[11] - LATE_ROWS + half * self.heads
            lanes = slice(half * LANES, (half + 1) * LANES)
            self.early[place : place + self.heads, :] = values[:, lanes]


SUM_ROWS = (0, 8, 16, 20, 24, 28, 32, 36, 40, 44, 48, 64)
LATE_ROWS = 16
SUM_SIZE = 96


def put_blocks(ref, shard, values):
    rows = values.shape[0]
    for block in range(values.shape[1] // LANES):
        at = pl.ds(block * rows, rows)
        ref[shard, at, :] = values[:, block * LANES : (block + 1) * LANES].astype(BF16)


def put_columns(ref, part, values):
    rows = values.shape[0]
    for shard in range(ref.shape[0]):
        piece = values[:, shard * LANES : (shard + 1) * LANES]
        ref[shard, part * rows : (part + 1) * rows, :] = piece.astype(BF16)


def local_scratch(rows, wide, width, units):
    heads = width // HD
    windows = rows // TOK
    return dict(
        merged=pltpu.VMEM((rows, wide), BF16),
        section=pltpu.VMEM((rows, width), BF16),
        attn_in=pltpu.VMEM((rows, width), BF16),
        qkv=pltpu.VMEM((3, rows, width), BF16),
        probs=pltpu.VMEM((windows, SPAN, heads * SPAN), BF16),
        att=pltpu.VMEM((rows, width), BF16),
        resid=pltpu.VMEM((rows, width), F32),
        mlp_in=pltpu.VMEM((rows, width), BF16),
        hidden=pltpu.VMEM((rows, units), BF16),
        slope=pltpu.VMEM((rows, units), BF16),
        pre=pltpu.VMEM((rows, width), F32),
        d_mlp=pltpu.VMEM((rows, width), BF16),
        d_pre=pltpu.VMEM((rows, units), BF16),
        d_attn=pltpu.VMEM((rows, width), BF16),
        d_resid=pltpu.VMEM((rows, width), F32),
        gains=pltpu.VMEM((8, wide), F32),
        stats=pltpu.VMEM((rows, 8), F32),
        bias=pltpu.VMEM((SPAN, heads * SPAN), F32),
        d_bias=pltpu.VMEM((SPAN, heads * SPAN), F32),
        spread=pltpu.VMEM((SPAN * heads, LANES), F32),
    )


MESH_ID = pl.DeviceIdType.MESH


class Links:
    def __init__(self, send_sems, recv_sems):
        self.send_sems, self.recv_sems = send_sems, recv_sems
        self.slots, self.sent = {}, []
        self.sp, self.tp = lax.axis_index("sp"), lax.axis_index("tp")

    def slot(self, label):
        return self.slots.setdefault(label, len(self.slots))

    def place(self, way):
        over_tp, distance = way
        if over_tp:
            return self.sp, self.tp ^ distance
        return self.sp ^ distance, self.tp

    def copy(self, label, way, source, target):
        slot = self.slot(label)
        return pltpu.make_async_remote_copy(
            src_ref=source,
            dst_ref=target,
            send_sem=self.send_sems.at[slot],
            recv_sem=self.recv_sems.at[slot],
            device_id=self.place(way),
            device_id_type=MESH_ID,
        )

    def send(self, label, way, source, target):
        copy = self.copy(label, way, source, target)
        copy.start()
        self.sent.append(copy)

    def receive(self, label, way, target):
        self.copy(label, way, target, target).wait_recv()

    def keep(self, label, source, target):
        copy = pltpu.make_async_copy(source, target, self.recv_sems.at[self.slot(label)])
        copy.start()
        return copy

    def greet(self, ways):
        barrier = pltpu.get_barrier_semaphore()
        for way in ways:
            pl.semaphore_signal(
                barrier, inc=1, device_id=self.place(way), device_id_type=MESH_ID
            )
        pl.semaphore_wait(barrier, len(ways))

    def drain(self):
        for copy in self.sent:
            copy.wait_send()


CORE, ACROSS, BESIDE = (True, 1), (True, 2), (False, 1)


def far(step):
    return False, 2 * step


class Gather:
    def __init__(self, links, label, own, whole, view, split=True):
        self.links, self.name, self.own, self.whole = links, label, own, whole
        self.view, self.split = view, split
        self.half = links.sp & 1 if split else None

    def part(self, shard, half=None):
        return self.view(self.whole, shard, half)

    def label(self, step):
        return self.name, step

    def start(self):
        links = self.links
        mine = links.tp
        source = self.view(self.own, None, None)
        self.local = links.keep(self.label(0), source, self.part(mine))
        links.send(
            self.label(1), ACROSS, self.view(self.own, None, self.half),
            self.part(mine, self.half),
        )
        links.send(self.label(2), CORE, source, self.part(mine))

    def forward(self):
        links = self.links
        block = self.part(links.tp ^ 2, self.half)
        links.receive(self.label(1), ACROSS, block)
        if self.split:
            links.send(self.label(3), BESIDE, block, block)
        links.send(self.label(4), CORE, block, block)

    def beside(self):
        links = self.links
        block = self.part(links.tp ^ 2, 1 - self.half)
        links.receive(self.label(3), BESIDE, block)
        links.send(self.label(5), CORE, block, block)

    def finish(self):
        links = self.links
        self.local.wait()
        links.receive(self.label(2), CORE, self.part(links.tp ^ 1))
        links.receive(self.label(4), CORE, self.part(links.tp ^ 3, self.half))
        if self.split:
            links.receive(self.label(5), CORE, self.part(links.tp ^ 3, 1 - self.half))


def column_view(size, first, rows):
    def view(ref, shard, half):
        start, count = (first, rows) if half is None else (first + half * (rows // 2), rows // 2)
        at = pl.ds(start if half is None else pl.multiple_of(start, 16), count)
        if shard is None:
            return ref.at[at, :]
        return ref.at[at, pl.ds(pl.multiple_of(shard * size, LANES), size)]

    return view


def row_view(size, first, rows):
    def view(ref, shard, half):
        start = first if shard is None else shard * size + first
        if half is None:
            return ref.at[pl.ds(start if shard is None else pl.multiple_of(start, 16), rows), :]
        return ref.at[pl.ds(pl.multiple_of(start + half * (rows // 2), 16), rows // 2), :]

    return view


def lead_view(ref, shard, half):
    return ref if shard is None else ref.at[shard]


def add_rows(target, start, rows, terms, chunk=512):
    chunk = math.gcd(rows, chunk)

    def step(index):
        offset = index * chunk

        def at(first):
            return pl.ds(pl.multiple_of(first + offset, 16), chunk)

        total = None
        for ref, first in terms:
            value = ref[at(first), :].astype(F32)
            total = value if total is None else total + value
        target[at(start), :] = total.astype(target.dtype)

    each(rows // chunk, step)


class Reduce:
    def __init__(self, links, label, grads, core_in, first_in, second_in, far_in, result, group,
                 across_first):
        self.links, self.name, self.grads = links, label, grads
        self.core_in, self.first_in, self.second_in = core_in, first_in, second_in
        self.far_in, self.result, self.group = far_in, result, group
        self.rows = grads.shape[1]
        self.half_rows = self.rows // 2
        self.piece = self.half_rows // group
        self.half = links.sp & 1
        self.seat = links.sp >> 1
        self.across = links.tp >> 1
        if across_first:
            self.add, self.first = self.core_add_across, self.across_beside
            self.second = self.beside_last
        else:
            self.add, self.first = self.core_add_beside, self.beside_across
            self.second = self.across_last

    def label(self, *step):
        return (self.name,) + step

    def rows_of(self, ref, half, piece=None):
        if piece is None:
            return ref.at[pl.ds(pl.multiple_of(half * self.half_rows, 16), self.half_rows), :]
        start = half * self.half_rows + piece * self.piece
        return ref.at[pl.ds(pl.multiple_of(start, 16), self.piece), :]

    def core_send(self, across, step):
        shard = (self.links.tp & 1) ^ 1 | 2 * across
        self.links.send(
            self.label(step), CORE, self.grads.at[shard], self.core_in.at[across]
        )

    def far(self):
        self.core_send(self.across ^ 1, 0)

    def near(self):
        self.core_send(self.across, 1)

    def receive_far(self):
        self.links.receive(self.label(0), CORE, self.core_in.at[self.across ^ 1])

    def receive_near(self):
        self.links.receive(self.label(1), CORE, self.core_in.at[self.across])

    def core_add_across(self):
        self.receive_far()
        other = self.links.tp ^ 2
        block = self.grads.at[other]
        add_rows(block, 0, self.rows, [(block, 0), (self.core_in.at[self.across ^ 1], 0)])
        self.links.send(self.label(2), ACROSS, block, self.first_in)

    def across_beside(self):
        links = self.links
        self.receive_near()
        links.receive(self.label(2), ACROSS, self.first_in)
        block = self.grads.at[links.tp]
        terms = [(block, 0), (self.core_in.at[self.across], 0), (self.first_in, 0)]
        add_rows(block, 0, self.rows, terms)
        links.send(
            self.label(3), BESIDE, self.rows_of(block, 1 - self.half), self.second_in
        )

    def beside_last(self):
        self.links.receive(self.label(3), BESIDE, self.second_in)
        self.add_and_spread([(self.second_in, 0)])

    def core_add_beside(self):
        links = self.links
        self.receive_far()
        self.receive_near()
        for across in range(2):
            block = self.grads.at[(links.tp & 1) | 2 * across]
            add_rows(block, 0, self.rows, [(block, 0), (self.core_in.at[across], 0)])
            links.send(
                self.label(3, across), BESIDE, self.rows_of(block, 1 - self.half),
                self.first_in.at[across],
            )

    def beside_across(self):
        links = self.links
        for across in range(2):
            links.receive(self.label(3, across), BESIDE, self.first_in.at[across])
        block = self.grads.at[links.tp ^ 2]
        mine = self.half * self.half_rows
        terms = [(block, mine), (self.first_in.at[self.across ^ 1], 0)]
        add_rows(block, mine, self.half_rows, terms)
        links.send(self.label(2), ACROSS, self.rows_of(block, self.half), self.second_in)

    def across_last(self):
        self.links.receive(self.label(2), ACROSS, self.second_in)
        self.add_and_spread([(self.first_in.at[self.across], 0), (self.second_in, 0)])

    def add_and_spread(self, terms):
        block = self.grads.at[self.links.tp]
        mine = self.half * self.half_rows
        add_rows(block, mine, self.half_rows, [(block, mine)] + terms)
        for step in range(1, self.group):
            self.links.send(
                self.label(4, step), far(step),
                self.rows_of(block, self.half, self.seat ^ step), self.far_in.at[step - 1],
            )

    def spread(self):
        links = self.links
        block = self.grads.at[links.tp]
        mine = self.half * self.half_rows + self.seat * self.piece
        terms = [(block, mine)]
        for step in range(1, self.group):
            links.receive(self.label(4, step), far(step), self.far_in.at[step - 1])
            terms.append((self.far_in.at[step - 1], 0))
        add_rows(self.result, mine, self.piece, terms)
        done = self.rows_of(self.result, self.half, self.seat)
        for step in range(1, self.group):
            links.send(self.label(5, step), far(step), done, done)

    def back(self):
        links = self.links
        for step in range(1, self.group):
            links.receive(
                self.label(5, step), far(step),
                self.rows_of(self.result, self.half, self.seat ^ step),
            )
        done = self.rows_of(self.result, self.half)
        links.send(self.label(6), BESIDE, done, done)

    def last(self):
        self.links.receive(
            self.label(6), BESIDE, self.rows_of(self.result, 1 - self.half)
        )


class Total:
    def __init__(self, links, label, stages, inboxes, seats, result):
        self.links, self.name, self.stages, self.inboxes = links, label, stages, inboxes
        self.seats, self.result = seats, result
        self.group = seats.shape[0]
        self.seat = links.sp >> 1

    def exchange(self, stage, way):
        self.links.send((self.name, stage), way, self.stages.at[stage], self.inboxes.at[stage])

    def take(self, stage, way):
        self.links.receive((self.name, stage), way, self.inboxes.at[stage])
        return self.stages[stage] + self.inboxes[stage]

    def send(self):
        self.exchange(0, CORE)

    def core(self):
        self.stages[1] = self.take(0, CORE)
        self.exchange(1, ACROSS)

    def across(self):
        self.stages[2] = self.take(1, ACROSS)
        self.exchange(2, BESIDE)

    def beside(self):
        mine = self.seats.at[self.seat]
        mine[...] = self.take(2, BESIDE)
        for step in range(1, self.group):
            self.links.send((self.name, 3, step), far(step), mine, mine)

    def last(self):
        for step in range(1, self.group):
            self.links.receive((self.name, 3, step), far(step), self.seats.at[self.seat ^ step])
        total = self.seats[0]
        for seat in range(1, self.group):
            total = total + self.seats[seat]
        self.result[...] = total


def schedule(local, g, u, done):
    windows = local.windows
    tiles = local.tiles()

    def attend_back(first, last):
        local.attend_back(windows - last * windows // 8, windows - first * windows // 8)

    local.begin()
    local.merge_norm()
    local.prepare()
    local.grad_rows()
    g.pack.forward()
    g.wm0.forward()
    g.wm1.forward()
    g.wq.forward()
    g.wm0.beside()
    g.wk.forward()
    g.wm0.finish()
    g.wm1.beside()
    g.wv.forward()
    g.wm1.finish()
    local.merge()
    g.wq.beside()
    g.wp.forward()
    g.pack.finish()
    local.table_bias()
    g.wk.beside()
    g.wu0.forward()
    local.attn_norm()
    g.wv.beside()
    g.wq.finish()
    local.project(0)
    g.wu1.forward()
    g.wk.finish()
    local.project(1)
    g.wv.finish()
    local.project(2)
    g.wp.beside()
    g.wu2.forward()
    local.attend(0, windows // 4)
    g.wu0.beside()
    g.wu3.forward()
    local.attend(windows // 4, windows // 2)
    g.wu1.beside()
    local.attend(windows // 2, 3 * windows // 4)
    g.wu2.beside()
    g.wd0.forward()
    local.attend(3 * windows // 4, windows)
    g.wu3.beside()
    g.wp.finish()
    local.attn_out()
    g.wd1.forward()
    local.mlp_norm()
    g.wu0.finish()
    g.wu1.finish()
    g.wu2.finish()
    g.wu3.finish()
    local.up(tiles[0])
    g.wd0.beside()
    u.gd0.far()
    u.gd1.far()
    local.up(tiles[1])
    g.wd1.beside()
    u.gd0.add()
    local.up(tiles[2])
    u.gd0.near()
    u.gd1.near()
    local.up(tiles[3])
    u.gd1.add()
    g.wd0.finish()
    g.wd1.finish()
    local.hidden_back(tiles[0])
    u.gu0.far()
    u.gu1.far()
    local.hidden_back(tiles[1])
    local.hidden_back(tiles[2])
    u.gu1.add()
    u.gu0.add()
    u.gd0.first()
    u.gu0.near()
    u.gu1.near()
    local.hidden_back(tiles[3])
    local.up_back()
    u.gd1.first()
    local.mlp_back()
    local.proj_back()
    u.gd0.second()
    u.gp0.far()
    u.gp0.near()
    attend_back(0, 2)
    u.gu1.first()
    u.gp0.add()
    attend_back(2, 4)
    attend_back(4, 6)
    u.gu0.first()
    u.gd0.spread()
    attend_back(6, 8)
    u.gu1.second()
    local.qkv_weight_back()
    u.gd1.second()
    u.gp0.first()
    u.qkv0.far()
    u.qkv0.near()
    u.qkv1.far()
    u.qkv1.near()
    u.qkv2.far()
    u.qkv2.near()
    local.qkv_back()
    u.gd0.back()
    u.gu0.second()
    u.qkv1.add()
    u.qkv0.add()
    u.qkv2.add()
    local.attn_back()
    u.gp0.second()
    local.merge_weight_back()
    u.gu1.spread()
    u.gm0.far()
    u.gm0.near()
    u.gm1.far()
    u.gm1.near()
    local.down()
    u.gm0.add()
    u.gd1.spread()
    u.gm1.add()
    u.qkv0.first()
    u.qkv1.first()
    u.qkv2.first()
    u.gu0.spread()
    u.gp0.spread()
    local.finish()
    done.out()
    local.merge_in_back()
    u.gm0.first()
    u.gm1.first()
    u.gu1.back()
    part = local.rows // 16 // 7
    totals = local.merge_back(0, 2 * part)
    u.qkv1.second()
    u.qkv0.second()
    totals = local.merge_back(2 * part, 5 * part, totals)
    local.merge_back(5 * part, 7 * part, totals)
    done.d_in()
    u.late.send()
    u.qkv2.second()
    local.bias_back()
    u.early.send()
    u.gd1.back()
    u.late.core()
    u.gm0.second()
    u.gm1.second()
    u.early.core()
    u.gu0.back()
    u.gp0.back()
    u.late.across()
    u.qkv1.spread()
    u.early.across()
    u.qkv0.spread()
    u.gm0.spread()
    u.qkv2.spread()
    u.gm1.spread()
    u.late.beside()
    u.early.beside()
    u.qkv1.back()
    u.qkv0.back()
    u.gm0.back()
    u.qkv2.back()
    u.gm1.back()
    u.gd0.last()
    u.gu1.last()
    u.gd1.last()
    u.gu0.last()
    u.gp0.last()
    u.qkv1.last()
    u.qkv0.last()
    u.late.last()
    u.gm0.last()
    u.qkv2.last()
    u.gm1.last()
    u.early.last()


SHARDS = 4
PIECES = 7


class Refs:
    def __init__(self, names, refs):
        self.__dict__.update(zip(names, refs, strict=True))


UNITS = dict(
    gd0=(0, 1024, True),
    gd1=(1024, 1024, False),
    gu0=(0, 1024, True),
    gu1=(1024, 1024, True),
    gp0=(0, 512, False),
    qkv0=(0, 512, True),
    qkv1=(512, 512, False),
    qkv2=(1024, 512, True),
    gm0=(0, 512, True),
    gm1=(512, 512, False),
)


def fill_pack(pack, rel, qv, ub):
    pack[...] = jnp.zeros_like(pack)
    pack[0 : rel.shape[0], 0:REL] = rel[...].astype(F32)
    pack[4:6, 0:LANES] = qv[...].astype(F32)
    for block in range(ub.shape[0]):
        lanes = slice(block * LANES, (block + 1) * LANES)
        pack[6:7, lanes] = ub[block : block + 1, :].astype(F32)


def gathers_of(links, r):
    wide, here = r.own_wm.shape
    width, tile = r.own_wu.shape
    columns = functools.partial(column_view, here)
    up = functools.partial(column_view, tile)
    down = functools.partial(row_view, tile)
    parts = dict(
        pack=(r.pack, r.packs, lead_view, False),
        wm0=(r.own_wm, r.wm, columns(0, wide // 2)),
        wm1=(r.own_wm, r.wm, columns(wide // 2, wide // 2)),
        wq=(r.own_wqkv.at[0], r.wqkv.at[0], columns(0, width)),
        wk=(r.own_wqkv.at[1], r.wqkv.at[1], columns(0, width)),
        wv=(r.own_wqkv.at[2], r.wqkv.at[2], columns(0, width)),
        wp=(r.own_wp, r.wp, row_view(here, 0, here)),
        wu0=(r.own_wu, r.wu, up(0, width // 4)),
        wu1=(r.own_wu, r.wu, up(width // 4, width // 4)),
        wu2=(r.own_wu, r.wu, up(width // 2, width // 4)),
        wu3=(r.own_wu, r.wu, up(3 * width // 4, width // 4)),
        wd0=(r.own_wd, r.wd, down(0, tile // 2)),
        wd1=(r.own_wd, r.wd, down(tile // 2, tile // 2)),
    )
    made = [Gather(links, label, *part) for label, part in enumerate(parts.values())]
    return Refs(parts, made)


def reduces_of(links, r, boxes, first_label):
    grads = (r.gd, r.gd, r.gu, r.gu, r.gp, r.gqkv, r.gqkv, r.gqkv, r.gm, r.gm)
    results = (r.rd, r.rd, r.ru, r.ru, r.rp, r.rqkv, r.rqkv, r.rqkv, r.rm, r.rm)
    made = []
    for index, (first, size, across_first) in enumerate(UNITS.values()):
        at = pl.ds(first, size)
        group = boxes[index][3].shape[0] + 1
        made.append(
            Reduce(
                links, first_label + index, grads[index].at[:, at, :], *boxes[index],
                results[index].at[at, :], group, across_first,
            )
        )
    return Refs(UNITS, made)


def whole_kernel(names, group, *refs):
    boxes = refs[len(names) :]
    r = Refs(names, refs[: len(names)])
    links = Links(r.send_sems, r.recv_sems)
    arriving = [links.keep((-1, 0), r.h_x, r.x), links.keep((-1, 1), r.h_grad_out, r.grad_out)]
    fill_pack(r.pack, r.rel, r.qv, r.ub)
    links.greet([CORE, ACROSS, BESIDE] + [far(step) for step in range(1, group)])
    g = gathers_of(links, r)
    for gather in vars(g).values():
        gather.start()
    u = reduces_of(links, r, [boxes[4 * unit : 4 * unit + 4] for unit in range(len(UNITS))], 100)
    late, early = pl.ds(0, LATE_ROWS), pl.ds(LATE_ROWS, SUM_SIZE - LATE_ROWS)
    u.late = Total(links, 200, r.late_stages, r.late_in, r.late_seats, r.sums.at[late, :])
    u.early = Total(links, 201, r.early_stages, r.early_in, r.early_seats, r.sums.at[early, :])
    here = r.rel.shape[0]

    def table():
        parts = [r.packs[shard, 0:here, : 2 * LANES] for shard in range(SHARDS)]
        return jnp.concatenate(parts, axis=0)

    def qkv_bias(part):
        row = 4 if part == 0 else 5
        parts = [r.packs[shard, row : row + 1, :LANES] for shard in range(SHARDS)]
        return jnp.concatenate(parts, axis=1)

    def up_bias(index):
        return r.packs[index, 6:7, :]

    vectors = (
        r.merge_gain, r.merge_bias, r.attn_gain, r.attn_bias, r.mlp_gain, r.mlp_bias, r.proj_bias,
        r.down_bias,
    )
    fields = dict(
        vars(r), table=table, qkv_bias=qkv_bias, up_bias=up_bias, vectors=vectors,
        arriving=arriving, early=r.early_stages.at[0], late=r.late_stages.at[0],
    )
    local = Local(fields, links.tp * (r.x.shape[0] // TOK))
    leaving = []

    def put_d_in():
        leaving.append(links.keep((-1, 2), r.d_in, r.h_d_in))

    def put_out():
        leaving.append(links.keep((-1, 3), r.out, r.h_out))

    schedule(local, g, u, Refs(dict(d_in=0, out=0), (put_d_in, put_out)))
    for copy in leaving:
        copy.wait()
    links.drain()


def wide_rows(result, out):
    rows = out.shape[0]
    for block in range(out.shape[1] // LANES):
        lanes = slice(block * LANES, (block + 1) * LANES)
        out[:, lanes] = result[block * rows : (block + 1) * rows, :].astype(F32)


def finish_kernel(names, *refs):
    r = Refs(names, refs)
    tp = lax.axis_index("tp")
    pieces = []
    for source, target, held in ((r.h_d_in, r.o_d_in, r.v_d_in), (r.h_out, r.o_out, r.v_out)):
        size = held.shape[0] // PIECES
        for index in range(PIECES):
            at = pl.ds(index * size, size)
            number = 2 * len(pieces)
            pieces.append(
                (
                    pltpu.make_async_copy(source.at[at], held.at[at], r.sems.at[number]),
                    pltpu.make_async_copy(held.at[at], target.at[at], r.sems.at[number + 1]),
                )
            )
    for incoming, _ in pieces:
        incoming.start()
    vectors = (
        r.o_merge_gain, r.o_merge_bias, r.o_attn_gain, r.o_attn_bias, r.o_proj_bias, r.o_mlp_gain,
        r.o_mlp_bias, r.o_down_bias,
    )
    for row, out in enumerate(vectors):
        out[...] = r.sums[SUM_ROWS[row] : SUM_ROWS[row] + out.shape[0], :]
    for index in range(2):
        r.o_qv[index : index + 1, :] = r.sums[pl.ds(SUM_ROWS[8 + index] + tp, 1), :]
    blocks = r.o_ub.shape[0]
    for index in range(blocks):
        place = pl.ds(SUM_ROWS[10] + tp * blocks + index, 1)
        r.o_ub[index : index + 1, :] = r.sums[place, :]
    mine = r.o_rel.shape[0]
    for index in range(mine):
        first = SUM_ROWS[11] + tp * mine + index
        low, high = r.sums[pl.ds(first, 1), :], r.sums[pl.ds(first + SHARDS * mine, 1), :]
        r.o_rel[index : index + 1, :LANES] = low
        r.o_rel[index : index + 1, LANES:] = high[:, : REL - LANES]
    for incoming, outgoing in pieces:
        incoming.wait()
        outgoing.start()
    for result, out in ((r.rp, r.o_gp), (r.ru, r.o_gu), (r.rd, r.o_gd), (r.rm, r.o_gm)):
        wide_rows(result, out)
    rows = r.o_gqkv.shape[1]
    for part in range(r.o_gqkv.shape[0]):
        r.o_gqkv[part] = r.rqkv[part * rows : (part + 1) * rows, :].astype(F32)
    for _, outgoing in pieces:
        outgoing.wait()


VMEM_SPEC = pl.BlockSpec(memory_space=pltpu.VMEM)
SMEM_SPEC = pl.BlockSpec(memory_space=pltpu.SMEM)
HBM_SPEC = pl.BlockSpec(memory_space=pl.ANY)


def whole_call(group, small, large):
    rows, wide = large["h_x"].shape
    width, tile = large["own_wu"].shape
    units = SHARDS * tile
    scratch = local_scratch(rows, wide, width, units)
    block = lambda *shape: pltpu.VMEM(shape, BF16)
    exact = lambda *shape: pltpu.VMEM(shape, F32)
    early = SUM_SIZE - LATE_ROWS
    count = 13 * 6 + len(UNITS) * (6 + 2 * group) + 2 * (3 + group) + 4
    scratch.update(
        wm=block(wide, width), wqkv=block(3, width, width), wp=block(width, width),
        wu=block(width, units), wd=block(units, width), pack=exact(8, tile),
        packs=exact(SHARDS, 8, tile), x=block(rows, wide), grad_out=block(rows, width),
        out=block(rows, width), d_in=exact(rows, wide), gd=block(SHARDS, units, LANES),
        gu=block(SHARDS, units, LANES), gp=block(SHARDS, width, LANES),
        gqkv=block(SHARDS, 3 * width, LANES), gm=block(SHARDS, wide, LANES),
        late_stages=exact(3, LATE_ROWS, LANES), late_in=exact(3, LATE_ROWS, LANES),
        late_seats=exact(group, LATE_ROWS, LANES), early_stages=exact(3, early, LANES),
        early_in=exact(3, early, LANES), early_seats=exact(group, early, LANES),
        send_sems=pltpu.SemaphoreType.DMA((count,)), recv_sems=pltpu.SemaphoreType.DMA((count,)),
    )
    boxes = []
    for _, size, across_first in UNITS.values():
        half = size // 2
        boxes += [
            block(2, size, LANES),
            block(size, LANES) if across_first else block(2, half, LANES),
            block(half, LANES),
            block(group - 1, half // group, LANES),
        ]
    result = lambda size: jax.ShapeDtypeStruct((size, LANES), BF16)
    outs = dict(
        h_out=jax.ShapeDtypeStruct((rows, width), BF16),
        h_d_in=jax.ShapeDtypeStruct((rows, wide), F32),
        rd=result(units), ru=result(units), rp=result(width), rqkv=result(3 * width),
        rm=result(wide), sums=jax.ShapeDtypeStruct((SUM_SIZE, LANES), F32),
    )
    names = tuple(small) + tuple(large) + tuple(outs) + tuple(scratch)
    made = pl.pallas_call(
        functools.partial(whole_kernel, names, group),
        out_shape=list(outs.values()),
        in_specs=[SMEM_SPEC] * 2 + [VMEM_SPEC] * (len(small) - 2) + [HBM_SPEC] * len(large),
        out_specs=[HBM_SPEC] * 2 + [VMEM_SPEC] * (len(outs) - 2),
        scratch_shapes=list(scratch.values()) + boxes,
        compiler_params=pltpu.CompilerParams(
            vmem_limit_bytes=63 * MIB, collective_id=0, has_side_effects=True
        ),
    )(*small.values(), *large.values())
    return dict(zip(outs, made, strict=True))


def finish_call(results, shapes):
    (rows, width), (_, wide) = shapes["o_out"].shape, shapes["o_d_in"].shape
    scratch = dict(
        v_out=pltpu.VMEM((rows, width), BF16), v_d_in=pltpu.VMEM((rows, wide), F32),
        sems=pltpu.SemaphoreType.DMA((4 * PIECES,)),
    )
    names = tuple(results) + tuple(shapes) + tuple(scratch)
    made = pl.pallas_call(
        functools.partial(finish_kernel, names),
        out_shape=list(shapes.values()),
        in_specs=[HBM_SPEC] * 2 + [VMEM_SPEC] * (len(results) - 2),
        out_specs=[HBM_SPEC] * 2 + [VMEM_SPEC] * (len(shapes) - 2),
        scratch_shapes=list(scratch.values()),
        compiler_params=pltpu.CompilerParams(vmem_limit_bytes=63 * MIB),
    )(*results.values())
    return Refs(shapes, made)


def on_device(
    inputs, grad_out, window_valid, window_edge, merge_gain, merge_bias, merge_weight, attn_gain,
    attn_bias, query_key_value_weight, qv_bias, rel_table, proj_weight, proj_bias, mlp_gain,
    mlp_bias, up_weight, up_bias, down_weight, down_bias,
):
    lines = lambda vector: vector.reshape(-1, LANES)
    small = dict(
        valid=window_valid, edge=window_edge, rel=rel_table.T, qv=qv_bias, ub=lines(up_bias),
        merge_gain=lines(merge_gain), merge_bias=lines(merge_bias), attn_gain=lines(attn_gain),
        attn_bias=lines(attn_bias), mlp_gain=lines(mlp_gain), mlp_bias=lines(mlp_bias),
        proj_bias=lines(proj_bias), down_bias=lines(down_bias),
    )
    qkv = jnp.transpose(query_key_value_weight, (1, 0, 2))
    large = dict(
        h_x=inputs, h_grad_out=grad_out, own_wm=merge_weight, own_wqkv=qkv, own_wp=proj_weight,
        own_wu=up_weight, own_wd=down_weight,
    )
    results = whole_call(lax.axis_size("sp") // 2, small, large)
    like = lambda array: jax.ShapeDtypeStruct(array.shape, F32)
    shapes = dict(
        o_out=jax.ShapeDtypeStruct(grad_out.shape, BF16), o_d_in=like(inputs),
        o_gm=like(merge_weight), o_gqkv=like(qkv), o_gp=like(proj_weight), o_gu=like(up_weight),
        o_gd=like(down_weight), o_qv=like(qv_bias), o_rel=like(rel_table.T),
        o_ub=like(lines(up_bias)), o_merge_gain=like(lines(merge_gain)),
        o_merge_bias=like(lines(merge_bias)), o_attn_gain=like(lines(attn_gain)),
        o_attn_bias=like(lines(attn_bias)), o_proj_bias=like(lines(proj_bias)),
        o_mlp_gain=like(lines(mlp_gain)), o_mlp_bias=like(lines(mlp_bias)),
        o_down_bias=like(lines(down_bias)),
    )
    done = finish_call(results, shapes)
    flat = lambda block: block.reshape(-1)
    return (
        done.o_out, done.o_d_in, flat(done.o_merge_gain), flat(done.o_merge_bias), done.o_gm,
        flat(done.o_attn_gain), flat(done.o_attn_bias), jnp.transpose(done.o_gqkv, (1, 0, 2)),
        done.o_qv, done.o_rel.T, done.o_gp, flat(done.o_proj_bias), flat(done.o_mlp_gain),
        flat(done.o_mlp_bias), done.o_gu, flat(done.o_ub), done.o_gd, flat(done.o_down_bias),
    )


def solution(mesh):
    placed = (
        P(("sp", "tp"), None),
        P(("sp", "tp"), None),
        P("sp"),
        P("sp"),
        P(),
        P(),
        P(None, "tp"),
        P(),
        P(),
        P(None, None, "tp"),
        P(None, "tp"),
        P(None, "tp"),
        P("tp", None),
        P(),
        P(),
        P(),
        P(None, "tp"),
        P("tp"),
        P("tp", None),
        P(),
    )
    return jax.shard_map(
        on_device,
        mesh=mesh,
        in_specs=placed,
        out_specs=(
            P(("sp", "tp"), None),
            P(("sp", "tp"), None),
            P(),
            P(),
            P(None, "tp"),
            P(),
            P(),
            P(None, None, "tp"),
            P(None, "tp"),
            P(None, "tp"),
            P("tp", None),
            P(),
            P(),
            P(),
            P(None, "tp"),
            P("tp"),
            P("tp", None),
            P(),
        ),
        check_vma=False,
    )
```

```python
import functools
import math

import jax
import jax.numpy as jnp
from jax import lax
from jax.experimental import pallas as pl
from jax.experimental.pallas import tpu as pltpu
from jax.sharding import PartitionSpec as P

SIDE = 7
TOK = SIDE * SIDE
REL_SIDE = 2 * SIDE - 1
REL = REL_SIDE * REL_SIDE
SPAN = 64
GROUP = 4
HD = 32
LANES = 128
EPSILON = 1e-05
NEG_FILL = -1000000000.0
MIB = 1 << 20
F32 = jnp.float32
BF16 = jnp.bfloat16


def dot(left, right):
    return jnp.dot(left, right, preferred_element_type=F32)


def dot_cols(left, right):
    return lax.dot_general(left, right, (((1,), (1,)), ((), ())), preferred_element_type=F32)


def dot_rows(left, right):
    return lax.dot_general(left, right, (((0,), (0,)), ((), ())), preferred_element_type=F32)


def rows_at(index, size):
    return pl.ds(pl.multiple_of(index * size, size), size)


def each(count, body, unroll=1):
    def step(index, carry):
        body(index)
        return carry

    lax.fori_loop(0, count, step, 0, unroll=unroll)


def fold(values):
    total = values[0:8]
    for start in range(8, values.shape[0], 8):
        total = total + values[start : start + 8]
    return total


def iota(shape, dim):
    return lax.broadcasted_iota(jnp.int32, shape, dim)


def norm_rows(values):
    mean = jnp.mean(values, -1, keepdims=True)
    centred = values - mean
    inv = lax.rsqrt(jnp.mean(centred * centred, -1, keepdims=True) + EPSILON)
    return centred * inv, mean, inv


def norm_back(upstream, normed, inv, gain):
    scaled = upstream * gain
    return inv * (
        scaled
        - jnp.mean(scaled, -1, keepdims=True)
        - normed * jnp.mean(scaled * normed, -1, keepdims=True)
    )


def gelu_both(values):
    bell = jnp.exp2(values * values * -0.7213475204444817)
    span = 1.0 + 0.23164190 * jnp.abs(values)
    t = pltpu.reciprocal(span, approx=True)
    t = t * (2.0 - span * t)
    poly = t * (
        0.127414796
        + t * (-0.142248368 + t * (0.7107068705 + t * (-0.7265760135 + t * 0.5307027145)))
    )
    tail = poly * bell
    phi = jnp.where(values >= 0, 1.0 - tail, tail)
    return values * phi, phi + values * bell * 0.3989422804014327


def window_row_col(index):
    row = (index * 37) >> 8
    return row, index - SIDE * row


def region_ids(index, edge, outside):
    row, col = window_row_col(index)
    high = SIDE - SIDE // 2
    region = (edge & 1) * (col >= high).astype(jnp.int32) + 2 * (edge >> 1) * (
        row >= high
    ).astype(jnp.int32)
    return jnp.where((index >= 0) & (index < TOK), region, outside)


def head_masks():
    lane = iota((1, LANES), 1)
    return [((lane >> 5) == head).astype(F32).astype(BF16) for head in range(GROUP)]


def spread_heads(block, masks):
    return jnp.concatenate([block * mask for mask in masks], axis=0)


def pick_heads(product):
    lane = iota((SPAN, LANES), 1)
    result = product[3 * SPAN : 4 * SPAN]
    for head in (2, 1, 0):
        result = jnp.where(
            lane < (head + 1) * HD, product[head * SPAN : (head + 1) * SPAN], result
        )
    return result


def same_head(rows, columns):
    return (
        (iota((rows, columns), 0) // (rows // GROUP))
        == (iota((rows, columns), 1) // (columns // GROUP))
    ).astype(F32).astype(BF16)


def offset_select(half):
    place = iota((LANES, LANES), 0)
    lane = iota((LANES, LANES), 1)
    token = lane - half * SPAN
    row, col = window_row_col(token & (SPAN - 1))
    wanted = (SIDE - 1) * (REL_SIDE + 1) - (REL_SIDE * row + col)
    hit = (place == wanted) & (token >= 0) & (token < TOK)
    return hit.astype(F32).astype(BF16)


def build_bias(table, spread_ref, bias_ref):
    heads = table.shape[0]

    def one(index):
        row = index // SIDE
        shift = index + (SIDE - 1) * row
        rolled = pltpu.roll(table, (2 * LANES - shift) % (2 * LANES), 1)
        spread_ref[rows_at(index, heads), :] = rolled[:, :LANES]

    spread_ref[...] = jnp.zeros_like(spread_ref)
    for index in range(TOK):
        one(index)
    low, high = offset_select(0), offset_select(1)
    for pair in range(heads // 2):
        first = spread_ref[pl.ds(2 * pair, SPAN, stride=heads), :].astype(BF16)
        second = spread_ref[pl.ds(2 * pair + 1, SPAN, stride=heads), :].astype(BF16)
        bias_ref[:, pair * LANES : (pair + 1) * LANES] = dot(first, low) + dot(second, high)


def split_bf16(values):
    high = values.astype(BF16)
    return high, (values - high.astype(F32)).astype(BF16)


def reduce_bias(bias_ref, spread_ref, heads):
    low, high = offset_select(0), offset_select(1)
    for pair in range(heads // 2):
        parts = split_bf16(bias_ref[:, pair * LANES : (pair + 1) * LANES])
        spread_ref[pl.ds(2 * pair, SPAN, stride=heads), :] = sum(
            dot_cols(part, low) for part in parts
        )
        spread_ref[pl.ds(2 * pair + 1, SPAN, stride=heads), :] = sum(
            dot_cols(part, high) for part in parts
        )
    total = jnp.zeros((heads, 2 * LANES), F32)
    blank = jnp.zeros((heads, LANES), F32)
    for index in range(TOK):
        shift = index + (SIDE - 1) * (index // SIDE)
        row = jnp.concatenate([spread_ref[index * heads : (index + 1) * heads, :], blank], axis=1)
        total = total + (pltpu.roll(row, shift, 1) if shift else row)
    return total


def shift_both(ref, forward):
    rows, columns = ref.shape
    down, right = (1, 1) if forward else (rows - 1, columns - 1)
    ref[...] = pltpu.roll(pltpu.roll(ref[...], down, 0), right, 1)


def attention_forward(first, edges, qkv, bias_ref, probs_ref, att_ref):
    masks = head_masks()
    size = GROUP * SPAN
    ones = same_head(size, size)
    first_half = iota((SPAN, LANES), 1) < SPAN
    groups = range(att_ref.shape[1] // LANES)

    def part_of(array, group, width):
        return array[:, group * width : (group + 1) * width]

    def tops(values):
        found = []
        for half in range(size // LANES):
            piece = part_of(values, half, LANES)
            low = jnp.max(jnp.where(first_half, piece, 2 * NEG_FILL), -1, keepdims=True)
            high = jnp.max(jnp.where(first_half, 2 * NEG_FILL, piece), -1, keepdims=True)
            found.append(jnp.where(first_half, low, high))
        return jnp.concatenate(found, axis=1)

    bias = bias_ref[...]
    states = []
    for index, edge in enumerate(edges):
        window = first + index
        base = pl.ds(pl.multiple_of(window * (TOK - 1), 16), SPAN)
        row_index = iota((SPAN, 1), 0) - window
        row_in = (row_index >= 0) & (row_index < TOK)
        row_region = region_ids(row_index, edge, 8)
        lane_region = region_ids((iota((1, size), 1) & (SPAN - 1)) - window, edge, 16)
        query, key, value = (qkv[part, base, :] for part in range(3))
        states.append((window, base, row_in, row_region == lane_region, query, key, value, bias))
        bias = pltpu.roll(pltpu.roll(bias, 1, 0), 1, 1)
    bias_ref[...] = bias

    logits = [
        [
            jnp.where(
                allowed,
                dot_cols(
                    part_of(query, group, LANES), spread_heads(part_of(key, group, LANES), masks)
                )
                * (HD**-0.5)
                + part_of(shifted, group, size),
                NEG_FILL,
            )
            for group in groups
        ]
        for _, _, _, allowed, query, key, _, shifted in states
    ]
    terms = [[jnp.exp(values - tops(values)) for values in row] for row in logits]
    totals = [[dot(values.astype(BF16), ones) for values in row] for row in terms]
    probs = [
        [
            (terms[index][group] * (state[2].astype(F32) / totals[index][group])).astype(BF16)
            for group in groups
        ]
        for index, state in enumerate(states)
    ]
    attended = [
        jnp.concatenate(
            [
                dot(probs[index][group], spread_heads(part_of(state[6], group, LANES), masks))
                for group in groups
            ],
            axis=1,
        )
        for index, state in enumerate(states)
    ]
    for index, (window, base, row_in, *_) in enumerate(states):
        for group in groups:
            probs_ref[window, :, pl.ds(group * size, size)] = probs[index][group]
        before = att_ref[base, :].astype(F32)
        att_ref[base, :] = jnp.where(row_in, attended[index], before).astype(BF16)


def attention_backward(windows, qkv, d_att, probs_ref, d_bias_ref, d_qkv):
    masks = head_masks()
    size = GROUP * SPAN
    ones = same_head(size, size)
    groups = range(d_att.shape[1] // LANES)
    factor = HD**-0.5

    def part_of(array, group, width):
        return array[:, group * width : (group + 1) * width]

    states = []
    for window in windows:
        base = pl.ds(pl.multiple_of(window * (TOK - 1), 16), SPAN)
        query, key, value = (qkv[part, base, :] for part in range(3))
        states.append((base, query, key, value, d_att[base, :], probs_ref[window]))
    d_bias = d_bias_ref[...]

    weighted = [
        [
            dot_cols(
                part_of(upstream, group, LANES),
                spread_heads(part_of(value, group, LANES), masks),
            )
            * part_of(probs, group, size).astype(F32)
            for group in groups
        ]
        for _, _, _, value, upstream, probs in states
    ]
    deltas = [[dot(values.astype(BF16), ones) for values in row] for row in weighted]
    d_logits = [
        [
            (
                weighted[index][group]
                - part_of(state[5], group, size).astype(F32) * deltas[index][group]
            ).astype(BF16)
            for group in groups
        ]
        for index, state in enumerate(states)
    ]
    for row in d_logits:
        d_bias = pltpu.roll(pltpu.roll(d_bias, SPAN - 1, 0), d_bias.shape[1] - 1, 1)
        d_bias = d_bias + jnp.concatenate([values.astype(F32) for values in row], axis=1)
    d_bias_ref[...] = d_bias
    results = []
    for index, (base, query, key, value, upstream, probs) in enumerate(states):
        row = d_logits[index]
        d_query = [
            dot(row[group], spread_heads(part_of(key, group, LANES), masks)) * factor
            for group in groups
        ]
        d_key = [
            pick_heads(dot_rows(row[group], part_of(query, group, LANES))) * factor
            for group in groups
        ]
        d_value = [
            pick_heads(dot_rows(part_of(probs, group, size), part_of(upstream, group, LANES)))
            for group in groups
        ]
        results.append([jnp.concatenate(values, axis=1) for values in (d_query, d_key, d_value)])
    for index, window in enumerate(windows):
        base = states[index][0]
        row_index = iota((SPAN, 1), 0) - window
        row_in = (row_index >= 0) & (row_index < TOK)
        for part in range(3):
            old = d_qkv[part, base, :].astype(F32)
            d_qkv[part, base, :] = jnp.where(row_in, results[index][part], old).astype(BF16)


def sum_rows(values):
    return jnp.sum(values, 0, keepdims=True)


class Local:
    def __init__(self, refs, first_window):
        self.__dict__.update(refs)
        self.first_window = first_window
        self.rows, self.wide = self.x.shape
        self.width = self.section.shape[1]
        self.units = self.hidden.shape[1]
        self.windows = self.rows // TOK
        self.heads = self.width // HD
        self.chunk = self.rows
        self.steps = self.rows // self.chunk
        self.tile = self.units // self.gu.shape[0]

    def gain(self, row, lanes):
        return self.gains[row : row + 1, :lanes]

    def stat(self, at, index):
        return self.stats[at, index : index + 1]

    def keep_stats(self, at, index, mean, inv):
        self.stats[at, index : index + 1] = mean
        self.stats[at, index + 1 : index + 2] = inv

    def tiles(self):
        return [lax.axis_index("tp") ^ bits for bits in (3, 2, 1, 0)]

    def begin(self):
        for copy in self.arriving:
            copy.wait()
        self.early[...] = jnp.zeros_like(self.early)
        self.spread_vectors()

    def spread_vectors(self):
        for row, ref in enumerate(self.vectors):
            values = ref[...].astype(F32)
            for block in range(values.shape[0]):
                lanes = slice(block * LANES, (block + 1) * LANES)
                self.gains[row : row + 1, lanes] = values[block : block + 1]

    def prepare(self):
        def keep_rows(window):
            base = pl.ds(pl.multiple_of(window * (TOK - 1), 16), SPAN)
            index = iota((SPAN, 1), 0) - window
            inside = (index >= 0) & (index < TOK)
            valid = self.valid[self.first_window + window].astype(F32)
            self.stats[base, 6:7] = jnp.where(inside, valid, self.stats[base, 6:7])

        each(self.windows, keep_rows)

    def table_bias(self):
        build_bias(self.table(), self.spread, self.bias)

    def merge_norm(self):
        gain, shift = self.gain(0, self.wide), self.gain(1, self.wide)

        def step(index):
            at = rows_at(index, self.chunk)
            normed, mean, inv = norm_rows(self.x[at, :].astype(F32))
            self.merged[at, :] = (normed * gain + shift).astype(BF16)
            self.keep_stats(at, 0, mean, inv)

        each(self.steps, step)

    def merge(self):
        self.section[...] = dot(self.merged[...], self.wm[...]).astype(BF16)

    def attn_norm(self):
        gain, shift = self.gain(2, self.width), self.gain(3, self.width)

        def step(index):
            at = rows_at(index, self.chunk)
            normed, mean, inv = norm_rows(self.section[at, :].astype(F32))
            self.attn_in[at, :] = (normed * gain + shift).astype(BF16)
            self.keep_stats(at, 2, mean, inv)

        each(self.steps, step)

    def project(self, part):
        product = dot(self.attn_in[...], self.wqkv[part])
        if part != 1:
            product = product + self.qkv_bias(part)
        self.qkv[part] = product.astype(BF16)

    def attend(self, first, last, together=4):
        def step(index):
            window = first + index * together
            edges = [self.edge[self.first_window + window + more] for more in range(together)]
            attention_forward(window, edges, self.qkv, self.bias, self.probs, self.att)

        each((last - first) // together, step)

    def attn_out(self):
        self.pre[...] = dot(self.att[...], self.wp[...])

    def mlp_norm(self):
        gain, shift = self.gain(4, self.width), self.gain(5, self.width)
        proj_bias = self.gain(6, self.width)

        def step(index):
            at = rows_at(index, self.chunk)
            total = self.section[at, :].astype(F32) + self.pre[at, :] + proj_bias
            self.resid[at, :] = total
            normed, mean, inv = norm_rows(total)
            self.mlp_in[at, :] = (normed * gain + shift).astype(BF16)
            self.keep_stats(at, 4, mean, inv)

        each(self.steps, step)

    def up(self, index):
        columns = rows_at(index, self.tile)
        self.pre[...] = dot(self.mlp_in[...], self.wu[:, columns])
        shift = self.up_bias(index)

        def activate(step):
            at = rows_at(step, self.rows // 7)
            value, rate = gelu_both(self.pre[at, :] + shift)
            self.hidden[at, columns] = value.astype(BF16)
            self.slope[at, columns] = rate.astype(BF16)

        each(7, activate)
        put_blocks(self.gd, index, dot_rows(self.hidden[:, columns], self.d_mlp[...]))

    def down(self):
        self.pre[...] = dot(self.hidden[...], self.wd[...])

    def grad_rows(self):
        def step(index, total):
            at = rows_at(index, self.chunk)
            grad = self.grad_out[at, :].astype(F32) * self.stat(at, 6)
            self.d_mlp[at, :] = grad.astype(BF16)
            return total + fold(grad)

        total = lax.fori_loop(
            0, self.steps, step, jnp.zeros((8, self.width), F32)
        )
        self.put_sum(7, total)

    def finish(self):
        down_bias = self.gain(7, self.width)

        def step(index):
            at = rows_at(index, self.chunk)
            block = (self.resid[at, :] + self.pre[at, :] + down_bias) * self.stat(at, 6)
            self.out[at, :] = block.astype(BF16)

        each(self.steps, step)

    def hidden_back(self, index):
        columns = rows_at(index, self.tile)
        slope = self.slope[:, columns].astype(F32)
        grad = (dot_cols(self.d_mlp[...], self.wd[columns, :]) * slope).astype(BF16)
        self.d_pre[:, columns] = grad
        self.put_up_sum(index, fold(grad.astype(F32)))
        put_blocks(self.gu, index, dot_rows(self.mlp_in[...], grad))

    def hidden_back_pair(self):
        each(2, lambda index: self.hidden_back(lax.axis_index("tp") ^ (2 - index)))

    def up_back(self):
        self.pre[...] = dot_cols(self.d_pre[...], self.wu[...])

    def mlp_back(self):
        gain = self.gain(4, self.width)

        def step(index, totals):
            at = rows_at(index, self.chunk)
            inv = self.stat(at, 5)
            normed = (self.resid[at, :] - self.stat(at, 4)) * inv
            upstream = self.pre[at, :]
            d_resid = self.d_mlp[at, :].astype(F32) + norm_back(upstream, normed, inv, gain)
            self.d_resid[at, :] = d_resid
            self.d_attn[at, :] = d_resid.astype(BF16)
            return (
                totals[0] + fold(upstream * normed),
                totals[1] + fold(upstream),
                totals[2] + fold(d_resid),
            )

        blank = jnp.zeros((8, self.width), F32)
        totals = lax.fori_loop(0, self.steps, step, (blank, blank, blank))
        for row, total in zip((5, 6, 4), totals):
            self.put_sum(row, total)

    def proj_back(self):
        size = self.width // self.gp.shape[0]
        product = dot_rows(self.att[...], self.d_attn[...])
        for index in range(self.gp.shape[0]):
            put_blocks(self.gp, index, product[index * size : (index + 1) * size])
        self.att[...] = dot_cols(self.d_attn[...], self.wp[...]).astype(BF16)
        self.d_bias[...] = jnp.zeros_like(self.d_bias)

    def attend_back(self, first, last, together=2):
        def step(index):
            top = last - 1 - index * together
            windows = [top - less for less in range(together)]
            attention_backward(windows, self.qkv, self.att, self.probs, self.d_bias, self.qkv)

        each((last - first) // together, step)

    def bias_back(self):
        self.put_table(reduce_bias(self.d_bias, self.spread, self.heads))
        ones = jnp.full((8, self.rows), 1.0, BF16)
        self.put_sum(8, dot(ones, self.qkv[0]), True)
        self.put_sum(9, dot(ones, self.qkv[2]), True)

    def qkv_weight_back(self):
        for part in range(3):
            put_columns(self.gqkv, part, dot_rows(self.attn_in[...], self.qkv[part]))

    def qkv_back(self):
        self.pre[...] = (
            dot_cols(self.qkv[0], self.wqkv[0])
            + dot_cols(self.qkv[1], self.wqkv[1])
            + dot_cols(self.qkv[2], self.wqkv[2])
        )

    def attn_back(self):
        gain = self.gain(2, self.width)

        def step(index, totals):
            at = rows_at(index, self.chunk)
            inv = self.stat(at, 3)
            normed = (self.section[at, :].astype(F32) - self.stat(at, 2)) * inv
            upstream = self.pre[at, :]
            d_section = self.d_resid[at, :] + norm_back(upstream, normed, inv, gain)
            self.d_mlp[at, :] = d_section.astype(BF16)
            return totals[0] + fold(upstream * normed), totals[1] + fold(upstream)

        blank = jnp.zeros((8, self.width), F32)
        totals = lax.fori_loop(0, self.steps, step, (blank, blank))
        self.put_sum(2, totals[0])
        self.put_sum(3, totals[1])

    def merge_weight_back(self):
        put_columns(self.gm, 0, dot_rows(self.merged[...], self.d_mlp[...]))

    def merge_in_back(self):
        for half, ref in enumerate((self.pre, self.d_resid)):
            rows = slice(half * self.width, (half + 1) * self.width)
            ref[...] = dot_cols(self.d_mlp[...], self.wm[rows, :])

    def merge_back(self, first, last, totals=None):
        gain = self.gain(0, self.wide)

        def step(index, totals):
            at = pl.ds(first * 16, (last - first) * 16)
            inv = self.stat(at, 1)
            normed = (self.x[at, :].astype(F32) - self.stat(at, 0)) * inv
            upstream = jnp.concatenate([self.pre[at, :], self.d_resid[at, :]], axis=1)
            self.d_in[at, :] = norm_back(upstream, normed, inv, gain)
            return totals[0] + fold(upstream * normed), totals[1] + fold(upstream)

        blank = jnp.zeros((8, self.wide), F32)
        totals = step(0, totals or (blank, blank))
        if last == self.rows // 16:
            self.put_sum(0, totals[0])
            self.put_sum(1, totals[1])
        return totals

    def put_sum(self, row, values, summed=False):
        values = values[0:1] if summed else sum_rows(values)
        place, ref = SUM_ROWS[row], self.late
        if place >= LATE_ROWS:
            place, ref = place - LATE_ROWS, self.early
        for block in range(values.shape[1] // LANES):
            lanes = slice(block * LANES, (block + 1) * LANES)
            ref[place + block : place + block + 1, :] = values[:, lanes]

    def put_up_sum(self, index, total):
        values = sum_rows(total)
        blocks = self.tile // LANES
        for block in range(blocks):
            place = SUM_ROWS[10] - LATE_ROWS + index * blocks + block
            self.early[pl.ds(place, 1), :] = values[:, block * LANES : (block + 1) * LANES]

    def put_table(self, values):
        for half in range(2):
            place = SUM_ROWS[11] - LATE_ROWS + half * self.heads
            lanes = slice(half * LANES, (half + 1) * LANES)
            self.early[place : place + self.heads, :] = values[:, lanes]


SUM_ROWS = (0, 8, 16, 20, 24, 28, 32, 36, 40, 44, 48, 64)
LATE_ROWS = 16
SUM_SIZE = 96


def put_blocks(ref, shard, values):
    rows = values.shape[0]
    for block in range(values.shape[1] // LANES):
        at = pl.ds(block * rows, rows)
        ref[shard, at, :] = values[:, block * LANES : (block + 1) * LANES].astype(BF16)


def put_columns(ref, part, values):
    rows = values.shape[0]
    for shard in range(ref.shape[0]):
        piece = values[:, shard * LANES : (shard + 1) * LANES]
        ref[shard, part * rows : (part + 1) * rows, :] = piece.astype(BF16)


def local_scratch(rows, wide, width, units):
    heads = width // HD
    windows = rows // TOK
    return dict(
        merged=pltpu.VMEM((rows, wide), BF16),
        section=pltpu.VMEM((rows, width), BF16),
        attn_in=pltpu.VMEM((rows, width), BF16),
        qkv=pltpu.VMEM((3, rows, width), BF16),
        probs=pltpu.VMEM((windows, SPAN, heads * SPAN), BF16),
        att=pltpu.VMEM((rows, width), BF16),
        resid=pltpu.VMEM((rows, width), F32),
        mlp_in=pltpu.VMEM((rows, width), BF16),
        hidden=pltpu.VMEM((rows, units), BF16),
        slope=pltpu.VMEM((rows, units), BF16),
        pre=pltpu.VMEM((rows, width), F32),
        d_mlp=pltpu.VMEM((rows, width), BF16),
        d_pre=pltpu.VMEM((rows, units), BF16),
        d_attn=pltpu.VMEM((rows, width), BF16),
        d_resid=pltpu.VMEM((rows, width), F32),
        gains=pltpu.VMEM((8, wide), F32),
        stats=pltpu.VMEM((rows, 8), F32),
        bias=pltpu.VMEM((SPAN, heads * SPAN), F32),
        d_bias=pltpu.VMEM((SPAN, heads * SPAN), F32),
        spread=pltpu.VMEM((SPAN * heads, LANES), F32),
    )


MESH_ID = pl.DeviceIdType.MESH


class Links:
    def __init__(self, send_sems, recv_sems):
        self.send_sems, self.recv_sems = send_sems, recv_sems
        self.slots, self.sent = {}, []
        self.sp, self.tp = lax.axis_index("sp"), lax.axis_index("tp")

    def slot(self, label):
        return self.slots.setdefault(label, len(self.slots))

    def place(self, way):
        over_tp, distance = way
        if over_tp:
            return self.sp, self.tp ^ distance
        return self.sp ^ distance, self.tp

    def copy(self, label, way, source, target):
        slot = self.slot(label)
        return pltpu.make_async_remote_copy(
            src_ref=source,
            dst_ref=target,
            send_sem=self.send_sems.at[slot],
            recv_sem=self.recv_sems.at[slot],
            device_id=self.place(way),
            device_id_type=MESH_ID,
        )

    def send(self, label, way, source, target):
        copy = self.copy(label, way, source, target)
        copy.start()
        self.sent.append(copy)

    def receive(self, label, way, target):
        self.copy(label, way, target, target).wait_recv()

    def keep(self, label, source, target):
        copy = pltpu.make_async_copy(source, target, self.recv_sems.at[self.slot(label)])
        copy.start()
        return copy

    def greet(self, ways):
        barrier = pltpu.get_barrier_semaphore()
        for way in ways:
            pl.semaphore_signal(
                barrier, inc=1, device_id=self.place(way), device_id_type=MESH_ID
            )
        pl.semaphore_wait(barrier, len(ways))

    def drain(self):
        for copy in self.sent:
            copy.wait_send()


CORE, ACROSS, BESIDE = (True, 1), (True, 2), (False, 1)


def far(step):
    return False, 2 * step


class Gather:
    def __init__(self, links, label, own, whole, view, split=True):
        self.links, self.name, self.own, self.whole = links, label, own, whole
        self.view, self.split = view, split
        self.half = links.sp & 1 if split else None

    def part(self, shard, half=None):
        return self.view(self.whole, shard, half)

    def label(self, step):
        return self.name, step

    def start(self):
        links = self.links
        mine = links.tp
        source = self.view(self.own, None, None)
        self.local = links.keep(self.label(0), source, self.part(mine))
        links.send(
            self.label(1), ACROSS, self.view(self.own, None, self.half),
            self.part(mine, self.half),
        )
        links.send(self.label(2), CORE, source, self.part(mine))

    def forward(self):
        links = self.links
        block = self.part(links.tp ^ 2, self.half)
        links.receive(self.label(1), ACROSS, block)
        if self.split:
            links.send(self.label(3), BESIDE, block, block)
        links.send(self.label(4), CORE, block, block)

    def beside(self):
        links = self.links
        block = self.part(links.tp ^ 2, 1 - self.half)
        links.receive(self.label(3), BESIDE, block)
        links.send(self.label(5), CORE, block, block)

    def finish(self):
        links = self.links
        self.local.wait()
        links.receive(self.label(2), CORE, self.part(links.tp ^ 1))
        links.receive(self.label(4), CORE, self.part(links.tp ^ 3, self.half))
        if self.split:
            links.receive(self.label(5), CORE, self.part(links.tp ^ 3, 1 - self.half))


def column_view(size, first, rows):
    def view(ref, shard, half):
        start, count = (first, rows) if half is None else (first + half * (rows // 2), rows // 2)
        at = pl.ds(start if half is None else pl.multiple_of(start, 16), count)
        if shard is None:
            return ref.at[at, :]
        return ref.at[at, pl.ds(pl.multiple_of(shard * size, LANES), size)]

    return view


def row_view(size, first, rows):
    def view(ref, shard, half):
        start = first if shard is None else shard * size + first
        if half is None:
            return ref.at[pl.ds(start if shard is None else pl.multiple_of(start, 16), rows), :]
        return ref.at[pl.ds(pl.multiple_of(start + half * (rows // 2), 16), rows // 2), :]

    return view


def lead_view(ref, shard, half):
    return ref if shard is None else ref.at[shard]


def add_rows(target, start, rows, terms, chunk=512):
    chunk = math.gcd(rows, chunk)

    def step(index):
        offset = index * chunk

        def at(first):
            return pl.ds(pl.multiple_of(first + offset, 16), chunk)

        total = None
        for ref, first in terms:
            value = ref[at(first), :].astype(F32)
            total = value if total is None else total + value
        target[at(start), :] = total.astype(target.dtype)

    each(rows // chunk, step)


class Reduce:
    def __init__(self, links, label, grads, core_in, first_in, second_in, far_in, result, group,
                 across_first):
        self.links, self.name, self.grads = links, label, grads
        self.core_in, self.first_in, self.second_in = core_in, first_in, second_in
        self.far_in, self.result, self.group = far_in, result, group
        self.rows = grads.shape[1]
        self.half_rows = self.rows // 2
        self.piece = self.half_rows // group
        self.half = links.sp & 1
        self.seat = links.sp >> 1
        self.across = links.tp >> 1
        if across_first:
            self.add, self.first = self.core_add_across, self.across_beside
            self.second = self.beside_last
        else:
            self.add, self.first = self.core_add_beside, self.beside_across
            self.second = self.across_last

    def label(self, *step):
        return (self.name,) + step

    def rows_of(self, ref, half, piece=None):
        if piece is None:
            return ref.at[pl.ds(pl.multiple_of(half * self.half_rows, 16), self.half_rows), :]
        start = half * self.half_rows + piece * self.piece
        return ref.at[pl.ds(pl.multiple_of(start, 16), self.piece), :]

    def core_send(self, across, step):
        shard = (self.links.tp & 1) ^ 1 | 2 * across
        self.links.send(
            self.label(step), CORE, self.grads.at[shard], self.core_in.at[across]
        )

    def far(self):
        self.core_send(self.across ^ 1, 0)

    def near(self):
        self.core_send(self.across, 1)

    def receive_far(self):
        self.links.receive(self.label(0), CORE, self.core_in.at[self.across ^ 1])

    def receive_near(self):
        self.links.receive(self.label(1), CORE, self.core_in.at[self.across])

    def core_add_across(self):
        self.receive_far()
        other = self.links.tp ^ 2
        block = self.grads.at[other]
        add_rows(block, 0, self.rows, [(block, 0), (self.core_in.at[self.across ^ 1], 0)])
        self.links.send(self.label(2), ACROSS, block, self.first_in)

    def across_beside(self):
        links = self.links
        self.receive_near()
        links.receive(self.label(2), ACROSS, self.first_in)
        block = self.grads.at[links.tp]
        terms = [(block, 0), (self.core_in.at[self.across], 0), (self.first_in, 0)]
        add_rows(block, 0, self.rows, terms)
        links.send(
            self.label(3), BESIDE, self.rows_of(block, 1 - self.half), self.second_in
        )

    def beside_last(self):
        self.links.receive(self.label(3), BESIDE, self.second_in)
        self.add_and_spread([(self.second_in, 0)])

    def core_add_beside(self):
        links = self.links
        self.receive_far()
        self.receive_near()
        for across in range(2):
            block = self.grads.at[(links.tp & 1) | 2 * across]
            add_rows(block, 0, self.rows, [(block, 0), (self.core_in.at[across], 0)])
            links.send(
                self.label(3, across), BESIDE, self.rows_of(block, 1 - self.half),
                self.first_in.at[across],
            )

    def beside_across(self):
        links = self.links
        for across in range(2):
            links.receive(self.label(3, across), BESIDE, self.first_in.at[across])
        block = self.grads.at[links.tp ^ 2]
        mine = self.half * self.half_rows
        terms = [(block, mine), (self.first_in.at[self.across ^ 1], 0)]
        add_rows(block, mine, self.half_rows, terms)
        links.send(self.label(2), ACROSS, self.rows_of(block, self.half), self.second_in)

    def across_last(self):
        self.links.receive(self.label(2), ACROSS, self.second_in)
        self.add_and_spread([(self.first_in.at[self.across], 0), (self.second_in, 0)])

    def add_and_spread(self, terms):
        block = self.grads.at[self.links.tp]
        mine = self.half * self.half_rows
        add_rows(block, mine, self.half_rows, [(block, mine)] + terms)
        for step in range(1, self.group):
            self.links.send(
                self.label(4, step), far(step),
                self.rows_of(block, self.half, self.seat ^ step), self.far_in.at[step - 1],
            )

    def spread(self):
        links = self.links
        block = self.grads.at[links.tp]
        mine = self.half * self.half_rows + self.seat * self.piece
        terms = [(block, mine)]
        for step in range(1, self.group):
            links.receive(self.label(4, step), far(step), self.far_in.at[step - 1])
            terms.append((self.far_in.at[step - 1], 0))
        add_rows(self.result, mine, self.piece, terms)
        done = self.rows_of(self.result, self.half, self.seat)
        for step in range(1, self.group):
            links.send(self.label(5, step), far(step), done, done)

    def back(self):
        links = self.links
        for step in range(1, self.group):
            links.receive(
                self.label(5, step), far(step),
                self.rows_of(self.result, self.half, self.seat ^ step),
            )
        done = self.rows_of(self.result, self.half)
        links.send(self.label(6), BESIDE, done, done)

    def last(self):
        self.links.receive(
            self.label(6), BESIDE, self.rows_of(self.result, 1 - self.half)
        )


class Total:
    def __init__(self, links, label, stages, inboxes, seats, result):
        self.links, self.name, self.stages, self.inboxes = links, label, stages, inboxes
        self.seats, self.result = seats, result
        self.group = seats.shape[0]
        self.seat = links.sp >> 1

    def exchange(self, stage, way):
        self.links.send((self.name, stage), way, self.stages.at[stage], self.inboxes.at[stage])

    def take(self, stage, way):
        self.links.receive((self.name, stage), way, self.inboxes.at[stage])
        return self.stages[stage] + self.inboxes[stage]

    def send(self):
        self.exchange(0, CORE)

    def core(self):
        self.stages[1] = self.take(0, CORE)
        self.exchange(1, ACROSS)

    def across(self):
        self.stages[2] = self.take(1, ACROSS)
        self.exchange(2, BESIDE)

    def beside(self):
        mine = self.seats.at[self.seat]
        mine[...] = self.take(2, BESIDE)
        for step in range(1, self.group):
            self.links.send((self.name, 3, step), far(step), mine, mine)

    def last(self):
        for step in range(1, self.group):
            self.links.receive((self.name, 3, step), far(step), self.seats.at[self.seat ^ step])
        total = self.seats[0]
        for seat in range(1, self.group):
            total = total + self.seats[seat]
        self.result[...] = total


def schedule(local, g, u, done):
    windows = local.windows
    tiles = local.tiles()

    def attend_back(first, last):
        local.attend_back(windows - last * windows // 8, windows - first * windows // 8)

    local.begin()
    local.merge_norm()
    local.prepare()
    local.grad_rows()
    g.pack.forward()
    g.wm0.forward()
    g.wm1.forward()
    g.wq.forward()
    g.wm0.beside()
    g.wk.forward()
    g.wm0.finish()
    g.wm1.beside()
    g.wv.forward()
    g.wm1.finish()
    local.merge()
    g.wq.beside()
    g.wp.forward()
    g.pack.finish()
    local.table_bias()
    g.wk.beside()
    g.wu0.forward()
    local.attn_norm()
    g.wv.beside()
    g.wq.finish()
    local.project(0)
    g.wu1.forward()
    g.wk.finish()
    local.project(1)
    g.wv.finish()
    local.project(2)
    g.wp.beside()
    g.wu2.forward()
    local.attend(0, windows // 4)
    g.wu0.beside()
    g.wu3.forward()
    local.attend(windows // 4, windows // 2)
    g.wu1.beside()
    local.attend(windows // 2, 3 * windows // 4)
    g.wu2.beside()
    g.wd0.forward()
    local.attend(3 * windows // 4, windows)
    g.wu3.beside()
    g.wp.finish()
    local.attn_out()
    g.wd1.forward()
    local.mlp_norm()
    g.wu0.finish()
    g.wu1.finish()
    g.wu2.finish()
    g.wu3.finish()
    local.up(tiles[0])
    g.wd0.beside()
    u.gd0.far()
    u.gd1.far()
    local.up(tiles[1])
    g.wd1.beside()
    u.gd0.add()
    local.up(tiles[2])
    u.gd0.near()
    u.gd1.near()
    local.up(tiles[3])
    u.gd1.add()
    g.wd0.finish()
    g.wd1.finish()
    local.hidden_back(tiles[0])
    u.gu0.far()
    u.gu1.far()
    local.hidden_back_pair()
    u.gu1.add()
    u.gu0.add()
    u.gd0.first()
    u.gu0.near()
    u.gu1.near()
    local.hidden_back(tiles[3])
    local.up_back()
    u.gd1.first()
    local.mlp_back()
    local.proj_back()
    u.gd0.second()
    u.gp0.far()
    u.gp0.near()
    attend_back(0, 2)
    u.gu1.first()
    u.gp0.add()
    attend_back(2, 4)
    attend_back(4, 6)
    u.gu0.first()
    u.gd0.spread()
    attend_back(6, 8)
    u.gu1.second()
    local.qkv_weight_back()
    u.gd1.second()
    u.gp0.first()
    u.qkv0.far()
    u.qkv0.near()
    u.qkv1.far()
    u.qkv1.near()
    u.qkv2.far()
    u.qkv2.near()
    local.qkv_back()
    u.gd0.back()
    u.gu0.second()
    u.qkv1.add()
    u.qkv0.add()
    u.qkv2.add()
    local.attn_back()
    u.gp0.second()
    local.merge_weight_back()
    u.gu1.spread()
    u.gm0.far()
    u.gm0.near()
    u.gm1.far()
    u.gm1.near()
    local.down()
    u.gm0.add()
    u.gd1.spread()
    u.gm1.add()
    u.qkv0.first()
    u.qkv1.first()
    u.qkv2.first()
    u.gu0.spread()
    u.gp0.spread()
    local.finish()
    done.out()
    local.merge_in_back()
    u.gm0.first()
    u.gm1.first()
    u.gu1.back()
    part = local.rows // 16 // 7
    totals = local.merge_back(0, 2 * part)
    u.qkv1.second()
    u.qkv0.second()
    totals = local.merge_back(2 * part, 5 * part, totals)
    local.merge_back(5 * part, 7 * part, totals)
    done.d_in()
    u.late.send()
    u.qkv2.second()
    local.bias_back()
    u.early.send()
    u.gd1.back()
    u.late.core()
    u.gm0.second()
    u.gm1.second()
    u.early.core()
    u.gu0.back()
    u.gp0.back()
    u.late.across()
    u.qkv1.spread()
    u.early.across()
    u.qkv0.spread()
    u.gm0.spread()
    u.qkv2.spread()
    u.gm1.spread()
    u.late.beside()
    u.early.beside()
    u.qkv1.back()
    u.qkv0.back()
    u.gm0.back()
    u.qkv2.back()
    u.gm1.back()
    u.gd0.last()
    u.gu1.last()
    u.gd1.last()
    u.gu0.last()
    u.gp0.last()
    u.qkv1.last()
    u.qkv0.last()
    u.late.last()
    u.gm0.last()
    u.qkv2.last()
    u.gm1.last()
    u.early.last()


SHARDS = 4
PIECES = 7


class Refs:
    def __init__(self, names, refs):
        self.__dict__.update(zip(names, refs, strict=True))


UNITS = dict(
    gd0=(0, 1024, True),
    gd1=(1024, 1024, False),
    gu0=(0, 1024, True),
    gu1=(1024, 1024, True),
    gp0=(0, 512, False),
    qkv0=(0, 512, True),
    qkv1=(512, 512, False),
    qkv2=(1024, 512, True),
    gm0=(0, 512, True),
    gm1=(512, 512, False),
)


def fill_pack(pack, rel, qv, ub):
    pack[...] = jnp.zeros_like(pack)
    pack[0 : rel.shape[0], 0:REL] = rel[...].astype(F32)
    pack[4:6, 0:LANES] = qv[...].astype(F32)
    for block in range(ub.shape[0]):
        lanes = slice(block * LANES, (block + 1) * LANES)
        pack[6:7, lanes] = ub[block : block + 1, :].astype(F32)


def gathers_of(links, r):
    wide, here = r.own_wm.shape
    width, tile = r.own_wu.shape
    columns = functools.partial(column_view, here)
    up = functools.partial(column_view, tile)
    down = functools.partial(row_view, tile)
    parts = dict(
        pack=(r.pack, r.packs, lead_view, False),
        wm0=(r.own_wm, r.wm, columns(0, wide // 2)),
        wm1=(r.own_wm, r.wm, columns(wide // 2, wide // 2)),
        wq=(r.own_wqkv.at[0], r.wqkv.at[0], columns(0, width)),
        wk=(r.own_wqkv.at[1], r.wqkv.at[1], columns(0, width)),
        wv=(r.own_wqkv.at[2], r.wqkv.at[2], columns(0, width)),
        wp=(r.own_wp, r.wp, row_view(here, 0, here)),
        wu0=(r.own_wu, r.wu, up(0, width // 4)),
        wu1=(r.own_wu, r.wu, up(width // 4, width // 4)),
        wu2=(r.own_wu, r.wu, up(width // 2, width // 4)),
        wu3=(r.own_wu, r.wu, up(3 * width // 4, width // 4)),
        wd0=(r.own_wd, r.wd, down(0, tile // 2)),
        wd1=(r.own_wd, r.wd, down(tile // 2, tile // 2)),
    )
    made = [Gather(links, label, *part) for label, part in enumerate(parts.values())]
    return Refs(parts, made)


def reduces_of(links, r, boxes, first_label):
    grads = (r.gd, r.gd, r.gu, r.gu, r.gp, r.gqkv, r.gqkv, r.gqkv, r.gm, r.gm)
    results = (r.rd, r.rd, r.ru, r.ru, r.rp, r.rqkv, r.rqkv, r.rqkv, r.rm, r.rm)
    made = []
    for index, (first, size, across_first) in enumerate(UNITS.values()):
        at = pl.ds(first, size)
        group = boxes[index][3].shape[0] + 1
        made.append(
            Reduce(
                links, first_label + index, grads[index].at[:, at, :], *boxes[index],
                results[index].at[at, :], group, across_first,
            )
        )
    return Refs(UNITS, made)


def whole_kernel(names, group, *refs):
    boxes = refs[len(names) :]
    r = Refs(names, refs[: len(names)])
    links = Links(r.send_sems, r.recv_sems)
    arriving = [links.keep((-1, 0), r.h_x, r.x), links.keep((-1, 1), r.h_grad_out, r.grad_out)]
    fill_pack(r.pack, r.rel, r.qv, r.ub)
    links.greet([CORE, ACROSS, BESIDE] + [far(step) for step in range(1, group)])
    g = gathers_of(links, r)
    for gather in vars(g).values():
        gather.start()
    u = reduces_of(links, r, [boxes[4 * unit : 4 * unit + 4] for unit in range(len(UNITS))], 100)
    late, early = pl.ds(0, LATE_ROWS), pl.ds(LATE_ROWS, SUM_SIZE - LATE_ROWS)
    u.late = Total(links, 200, r.late_stages, r.late_in, r.late_seats, r.sums.at[late, :])
    u.early = Total(links, 201, r.early_stages, r.early_in, r.early_seats, r.sums.at[early, :])
    here = r.rel.shape[0]

    def table():
        parts = [r.packs[shard, 0:here, : 2 * LANES] for shard in range(SHARDS)]
        return jnp.concatenate(parts, axis=0)

    def qkv_bias(part):
        row = 4 if part == 0 else 5
        parts = [r.packs[shard, row : row + 1, :LANES] for shard in range(SHARDS)]
        return jnp.concatenate(parts, axis=1)

    def up_bias(index):
        return r.packs[index, 6:7, :]

    vectors = (
        r.merge_gain, r.merge_bias, r.attn_gain, r.attn_bias, r.mlp_gain, r.mlp_bias, r.proj_bias,
        r.down_bias,
    )
    fields = dict(
        vars(r), table=table, qkv_bias=qkv_bias, up_bias=up_bias, vectors=vectors,
        arriving=arriving, early=r.early_stages.at[0], late=r.late_stages.at[0],
    )
    local = Local(fields, links.tp * (r.x.shape[0] // TOK))
    leaving = []

    def put_d_in():
        leaving.append(links.keep((-1, 2), r.d_in, r.h_d_in))

    def put_out():
        leaving.append(links.keep((-1, 3), r.out, r.h_out))

    schedule(local, g, u, Refs(dict(d_in=0, out=0), (put_d_in, put_out)))
    for copy in leaving:
        copy.wait()
    links.drain()


def wide_rows(result, out):
    rows = out.shape[0]
    for block in range(out.shape[1] // LANES):
        lanes = slice(block * LANES, (block + 1) * LANES)
        out[:, lanes] = result[block * rows : (block + 1) * rows, :].astype(F32)


def finish_kernel(names, *refs):
    r = Refs(names, refs)
    tp = lax.axis_index("tp")
    pieces = []
    for source, target, held in ((r.h_d_in, r.o_d_in, r.v_d_in), (r.h_out, r.o_out, r.v_out)):
        size = held.shape[0] // PIECES
        for index in range(PIECES):
            at = pl.ds(index * size, size)
            number = 2 * len(pieces)
            pieces.append(
                (
                    pltpu.make_async_copy(source.at[at], held.at[at], r.sems.at[number]),
                    pltpu.make_async_copy(held.at[at], target.at[at], r.sems.at[number + 1]),
                )
            )
    for incoming, _ in pieces:
        incoming.start()
    vectors = (
        r.o_merge_gain, r.o_merge_bias, r.o_attn_gain, r.o_attn_bias, r.o_proj_bias, r.o_mlp_gain,
        r.o_mlp_bias, r.o_down_bias,
    )
    for row, out in enumerate(vectors):
        out[...] = r.sums[SUM_ROWS[row] : SUM_ROWS[row] + out.shape[0], :]
    for index in range(2):
        r.o_qv[index : index + 1, :] = r.sums[pl.ds(SUM_ROWS[8 + index] + tp, 1), :]
    blocks = r.o_ub.shape[0]
    for index in range(blocks):
        place = pl.ds(SUM_ROWS[10] + tp * blocks + index, 1)
        r.o_ub[index : index + 1, :] = r.sums[place, :]
    mine = r.o_rel.shape[0]
    for index in range(mine):
        first = SUM_ROWS[11] + tp * mine + index
        low, high = r.sums[pl.ds(first, 1), :], r.sums[pl.ds(first + SHARDS * mine, 1), :]
        r.o_rel[index : index + 1, :LANES] = low
        r.o_rel[index : index + 1, LANES:] = high[:, : REL - LANES]
    for incoming, outgoing in pieces:
        incoming.wait()
        outgoing.start()
    for result, out in ((r.rp, r.o_gp), (r.ru, r.o_gu), (r.rd, r.o_gd), (r.rm, r.o_gm)):
        wide_rows(result, out)
    rows = r.o_gqkv.shape[1]
    for part in range(r.o_gqkv.shape[0]):
        r.o_gqkv[part] = r.rqkv[part * rows : (part + 1) * rows, :].astype(F32)
    for _, outgoing in pieces:
        outgoing.wait()


VMEM_SPEC = pl.BlockSpec(memory_space=pltpu.VMEM)
SMEM_SPEC = pl.BlockSpec(memory_space=pltpu.SMEM)
HBM_SPEC = pl.BlockSpec(memory_space=pl.ANY)


def whole_call(group, small, large):
    rows, wide = large["h_x"].shape
    width, tile = large["own_wu"].shape
    units = SHARDS * tile
    scratch = local_scratch(rows, wide, width, units)
    block = lambda *shape: pltpu.VMEM(shape, BF16)
    exact = lambda *shape: pltpu.VMEM(shape, F32)
    early = SUM_SIZE - LATE_ROWS
    count = 13 * 6 + len(UNITS) * (6 + 2 * group) + 2 * (3 + group) + 4
    scratch.update(
        wm=block(wide, width), wqkv=block(3, width, width), wp=block(width, width),
        wu=block(width, units), wd=block(units, width), pack=exact(8, tile),
        packs=exact(SHARDS, 8, tile), x=block(rows, wide), grad_out=block(rows, width),
        out=block(rows, width), d_in=exact(rows, wide), gd=block(SHARDS, units, LANES),
        gu=block(SHARDS, units, LANES), gp=block(SHARDS, width, LANES),
        gqkv=block(SHARDS, 3 * width, LANES), gm=block(SHARDS, wide, LANES),
        late_stages=exact(3, LATE_ROWS, LANES), late_in=exact(3, LATE_ROWS, LANES),
        late_seats=exact(group, LATE_ROWS, LANES), early_stages=exact(3, early, LANES),
        early_in=exact(3, early, LANES), early_seats=exact(group, early, LANES),
        send_sems=pltpu.SemaphoreType.DMA((count,)), recv_sems=pltpu.SemaphoreType.DMA((count,)),
    )
    boxes = []
    for _, size, across_first in UNITS.values():
        half = size // 2
        boxes += [
            block(2, size, LANES),
            block(size, LANES) if across_first else block(2, half, LANES),
            block(half, LANES),
            block(group - 1, half // group, LANES),
        ]
    result = lambda size: jax.ShapeDtypeStruct((size, LANES), BF16)
    outs = dict(
        h_out=jax.ShapeDtypeStruct((rows, width), BF16),
        h_d_in=jax.ShapeDtypeStruct((rows, wide), F32),
        rd=result(units), ru=result(units), rp=result(width), rqkv=result(3 * width),
        rm=result(wide), sums=jax.ShapeDtypeStruct((SUM_SIZE, LANES), F32),
    )
    names = tuple(small) + tuple(large) + tuple(outs) + tuple(scratch)
    made = pl.pallas_call(
        functools.partial(whole_kernel, names, group),
        out_shape=list(outs.values()),
        in_specs=[SMEM_SPEC] * 2 + [VMEM_SPEC] * (len(small) - 2) + [HBM_SPEC] * len(large),
        out_specs=[HBM_SPEC] * 2 + [VMEM_SPEC] * (len(outs) - 2),
        scratch_shapes=list(scratch.values()) + boxes,
        compiler_params=pltpu.CompilerParams(
            vmem_limit_bytes=63 * MIB, collective_id=0, has_side_effects=True
        ),
    )(*small.values(), *large.values())
    return dict(zip(outs, made, strict=True))


def finish_call(results, shapes):
    (rows, width), (_, wide) = shapes["o_out"].shape, shapes["o_d_in"].shape
    scratch = dict(
        v_out=pltpu.VMEM((rows, width), BF16), v_d_in=pltpu.VMEM((rows, wide), F32),
        sems=pltpu.SemaphoreType.DMA((4 * PIECES,)),
    )
    names = tuple(results) + tuple(shapes) + tuple(scratch)
    made = pl.pallas_call(
        functools.partial(finish_kernel, names),
        out_shape=list(shapes.values()),
        in_specs=[HBM_SPEC] * 2 + [VMEM_SPEC] * (len(results) - 2),
        out_specs=[HBM_SPEC] * 2 + [VMEM_SPEC] * (len(shapes) - 2),
        scratch_shapes=list(scratch.values()),
        compiler_params=pltpu.CompilerParams(vmem_limit_bytes=63 * MIB),
    )(*results.values())
    return Refs(shapes, made)


def on_device(
    inputs, grad_out, window_valid, window_edge, merge_gain, merge_bias, merge_weight, attn_gain,
    attn_bias, query_key_value_weight, qv_bias, rel_table, proj_weight, proj_bias, mlp_gain,
    mlp_bias, up_weight, up_bias, down_weight, down_bias,
):
    lines = lambda vector: vector.reshape(-1, LANES)
    small = dict(
        valid=window_valid, edge=window_edge, rel=rel_table.T, qv=qv_bias, ub=lines(up_bias),
        merge_gain=lines(merge_gain), merge_bias=lines(merge_bias), attn_gain=lines(attn_gain),
        attn_bias=lines(attn_bias), mlp_gain=lines(mlp_gain), mlp_bias=lines(mlp_bias),
        proj_bias=lines(proj_bias), down_bias=lines(down_bias),
    )
    qkv = jnp.transpose(query_key_value_weight, (1, 0, 2))
    large = dict(
        h_x=inputs, h_grad_out=grad_out, own_wm=merge_weight, own_wqkv=qkv, own_wp=proj_weight,
        own_wu=up_weight, own_wd=down_weight,
    )
    results = whole_call(lax.axis_size("sp") // 2, small, large)
    like = lambda array: jax.ShapeDtypeStruct(array.shape, F32)
    shapes = dict(
        o_out=jax.ShapeDtypeStruct(grad_out.shape, BF16), o_d_in=like(inputs),
        o_gm=like(merge_weight), o_gqkv=like(qkv), o_gp=like(proj_weight), o_gu=like(up_weight),
        o_gd=like(down_weight), o_qv=like(qv_bias), o_rel=like(rel_table.T),
        o_ub=like(lines(up_bias)), o_merge_gain=like(lines(merge_gain)),
        o_merge_bias=like(lines(merge_bias)), o_attn_gain=like(lines(attn_gain)),
        o_attn_bias=like(lines(attn_bias)), o_proj_bias=like(lines(proj_bias)),
        o_mlp_gain=like(lines(mlp_gain)), o_mlp_bias=like(lines(mlp_bias)),
        o_down_bias=like(lines(down_bias)),
    )
    done = finish_call(results, shapes)
    flat = lambda block: block.reshape(-1)
    return (
        done.o_out, done.o_d_in, flat(done.o_merge_gain), flat(done.o_merge_bias), done.o_gm,
        flat(done.o_attn_gain), flat(done.o_attn_bias), jnp.transpose(done.o_gqkv, (1, 0, 2)),
        done.o_qv, done.o_rel.T, done.o_gp, flat(done.o_proj_bias), flat(done.o_mlp_gain),
        flat(done.o_mlp_bias), done.o_gu, flat(done.o_ub), done.o_gd, flat(done.o_down_bias),
    )


def solution(mesh):
    placed = (
        P(("sp", "tp"), None),
        P(("sp", "tp"), None),
        P("sp"),
        P("sp"),
        P(),
        P(),
        P(None, "tp"),
        P(),
        P(),
        P(None, None, "tp"),
        P(None, "tp"),
        P(None, "tp"),
        P("tp", None),
        P(),
        P(),
        P(),
        P(None, "tp"),
        P("tp"),
        P("tp", None),
        P(),
    )
    return jax.shard_map(
        on_device,
        mesh=mesh,
        in_specs=placed,
        out_specs=(
            P(("sp", "tp"), None),
            P(("sp", "tp"), None),
            P(),
            P(),
            P(None, "tp"),
            P(),
            P(),
            P(None, None, "tp"),
            P(None, "tp"),
            P(None, "tp"),
            P("tp", None),
            P(),
            P(),
            P(),
            P(None, "tp"),
            P("tp"),
            P("tp", None),
            P(),
        ),
        check_vma=False,
    )
```

```python
import functools
import math

import jax
import jax.numpy as jnp
from jax import lax
from jax.experimental import pallas as pl
from jax.experimental.pallas import tpu as pltpu
from jax.sharding import PartitionSpec as P

SIDE = 7
TOK = SIDE * SIDE
REL_SIDE = 2 * SIDE - 1
REL = REL_SIDE * REL_SIDE
SPAN = 64
GROUP = 4
HD = 32
LANES = 128
EPSILON = 1e-05
NEG_FILL = -1000000000.0
MIB = 1 << 20
F32 = jnp.float32
BF16 = jnp.bfloat16


def dot(left, right):
    return jnp.dot(left, right, preferred_element_type=F32)


def dot_cols(left, right):
    return lax.dot_general(left, right, (((1,), (1,)), ((), ())), preferred_element_type=F32)


def dot_rows(left, right):
    return lax.dot_general(left, right, (((0,), (0,)), ((), ())), preferred_element_type=F32)


def rows_at(index, size):
    return pl.ds(pl.multiple_of(index * size, size), size)


def each(count, body, unroll=1):
    def step(index, carry):
        body(index)
        return carry

    lax.fori_loop(0, count, step, 0, unroll=unroll)


def fold(values):
    total = values[0:8]
    for start in range(8, values.shape[0], 8):
        total = total + values[start : start + 8]
    return total


def iota(shape, dim):
    return lax.broadcasted_iota(jnp.int32, shape, dim)


def norm_rows(values):
    mean = jnp.mean(values, -1, keepdims=True)
    centred = values - mean
    inv = lax.rsqrt(jnp.mean(centred * centred, -1, keepdims=True) + EPSILON)
    return centred * inv, mean, inv


def norm_back(upstream, normed, inv, gain):
    scaled = upstream * gain
    return inv * (
        scaled
        - jnp.mean(scaled, -1, keepdims=True)
        - normed * jnp.mean(scaled * normed, -1, keepdims=True)
    )


def gelu_both(values):
    bell = jnp.exp2(values * values * -0.7213475204444817)
    span = 1.0 + 0.23164190 * jnp.abs(values)
    t = pltpu.reciprocal(span, approx=True)
    t = t * (2.0 - span * t)
    poly = t * (
        0.127414796
        + t * (-0.142248368 + t * (0.7107068705 + t * (-0.7265760135 + t * 0.5307027145)))
    )
    tail = poly * bell
    phi = jnp.where(values >= 0, 1.0 - tail, tail)
    return values * phi, phi + values * bell * 0.3989422804014327


def window_row_col(index):
    row = (index * 37) >> 8
    return row, index - SIDE * row


def region_ids(index, edge, outside):
    row, col = window_row_col(index)
    high = SIDE - SIDE // 2
    region = (edge & 1) * (col >= high).astype(jnp.int32) + 2 * (edge >> 1) * (
        row >= high
    ).astype(jnp.int32)
    return jnp.where((index >= 0) & (index < TOK), region, outside)


def head_masks():
    lane = iota((1, LANES), 1)
    return [((lane >> 5) == head).astype(F32).astype(BF16) for head in range(GROUP)]


def spread_heads(block, masks):
    return jnp.concatenate([block * mask for mask in masks], axis=0)


def pick_heads(product):
    lane = iota((SPAN, LANES), 1)
    result = product[3 * SPAN : 4 * SPAN]
    for head in (2, 1, 0):
        result = jnp.where(
            lane < (head + 1) * HD, product[head * SPAN : (head + 1) * SPAN], result
        )
    return result


def same_head(rows, columns):
    return (
        (iota((rows, columns), 0) // (rows // GROUP))
        == (iota((rows, columns), 1) // (columns // GROUP))
    ).astype(F32).astype(BF16)


def offset_select(half):
    place = iota((LANES, LANES), 0)
    lane = iota((LANES, LANES), 1)
    token = lane - half * SPAN
    row, col = window_row_col(token & (SPAN - 1))
    wanted = (SIDE - 1) * (REL_SIDE + 1) - (REL_SIDE * row + col)
    hit = (place == wanted) & (token >= 0) & (token < TOK)
    return hit.astype(F32).astype(BF16)


def build_bias(table, spread_ref, bias_ref):
    heads = table.shape[0]

    def one(index):
        row = index // SIDE
        shift = index + (SIDE - 1) * row
        rolled = pltpu.roll(table, (2 * LANES - shift) % (2 * LANES), 1)
        spread_ref[rows_at(index, heads), :] = rolled[:, :LANES]

    spread_ref[...] = jnp.zeros_like(spread_ref)
    for index in range(TOK):
        one(index)
    low, high = offset_select(0), offset_select(1)
    for pair in range(heads // 2):
        first = spread_ref[pl.ds(2 * pair, SPAN, stride=heads), :].astype(BF16)
        second = spread_ref[pl.ds(2 * pair + 1, SPAN, stride=heads), :].astype(BF16)
        bias_ref[:, pair * LANES : (pair + 1) * LANES] = dot(first, low) + dot(second, high)


def split_bf16(values):
    high = values.astype(BF16)
    return high, (values - high.astype(F32)).astype(BF16)


def reduce_bias(bias_ref, spread_ref, heads):
    low, high = offset_select(0), offset_select(1)
    for pair in range(heads // 2):
        parts = split_bf16(bias_ref[:, pair * LANES : (pair + 1) * LANES])
        spread_ref[pl.ds(2 * pair, SPAN, stride=heads), :] = sum(
            dot_cols(part, low) for part in parts
        )
        spread_ref[pl.ds(2 * pair + 1, SPAN, stride=heads), :] = sum(
            dot_cols(part, high) for part in parts
        )
    total = jnp.zeros((heads, 2 * LANES), F32)
    blank = jnp.zeros((heads, LANES), F32)
    for index in range(TOK):
        shift = index + (SIDE - 1) * (index // SIDE)
        row = jnp.concatenate([spread_ref[index * heads : (index + 1) * heads, :], blank], axis=1)
        total = total + (pltpu.roll(row, shift, 1) if shift else row)
    return total


def shift_both(ref, forward):
    rows, columns = ref.shape
    down, right = (1, 1) if forward else (rows - 1, columns - 1)
    ref[...] = pltpu.roll(pltpu.roll(ref[...], down, 0), right, 1)


def attention_forward(first, edges, qkv, bias_ref, probs_ref, att_ref):
    masks = head_masks()
    size = GROUP * SPAN
    ones = same_head(size, size)
    first_half = iota((SPAN, LANES), 1) < SPAN
    groups = range(att_ref.shape[1] // LANES)

    def part_of(array, group, width):
        return array[:, group * width : (group + 1) * width]

    def tops(values):
        found = []
        for half in range(size // LANES):
            piece = part_of(values, half, LANES)
            low = jnp.max(jnp.where(first_half, piece, 2 * NEG_FILL), -1, keepdims=True)
            high = jnp.max(jnp.where(first_half, 2 * NEG_FILL, piece), -1, keepdims=True)
            found.append(jnp.where(first_half, low, high))
        return jnp.concatenate(found, axis=1)

    bias = bias_ref[...]
    states = []
    for index, edge in enumerate(edges):
        window = first + index
        base = pl.ds(pl.multiple_of(window * (TOK - 1), 16), SPAN)
        row_index = iota((SPAN, 1), 0) - window
        row_in = (row_index >= 0) & (row_index < TOK)
        row_region = region_ids(row_index, edge, 8)
        lane_region = region_ids((iota((1, size), 1) & (SPAN - 1)) - window, edge, 16)
        query, key, value = (qkv[part, base, :] for part in range(3))
        states.append((window, base, row_in, row_region == lane_region, query, key, value, bias))
        bias = pltpu.roll(pltpu.roll(bias, 1, 0), 1, 1)
    bias_ref[...] = bias

    logits = [
        [
            jnp.where(
                allowed,
                dot_cols(
                    part_of(query, group, LANES), spread_heads(part_of(key, group, LANES), masks)
                )
                * (HD**-0.5)
                + part_of(shifted, group, size),
                NEG_FILL,
            )
            for group in groups
        ]
        for _, _, _, allowed, query, key, _, shifted in states
    ]
    terms = [[jnp.exp(values - tops(values)) for values in row] for row in logits]
    totals = [[dot(values.astype(BF16), ones) for values in row] for row in terms]
    probs = [
        [
            (terms[index][group] * (state[2].astype(F32) / totals[index][group])).astype(BF16)
            for group in groups
        ]
        for index, state in enumerate(states)
    ]
    attended = [
        jnp.concatenate(
            [
                dot(probs[index][group], spread_heads(part_of(state[6], group, LANES), masks))
                for group in groups
            ],
            axis=1,
        )
        for index, state in enumerate(states)
    ]
    for index, (window, base, row_in, *_) in enumerate(states):
        for group in groups:
            probs_ref[window, :, pl.ds(group * size, size)] = probs[index][group]
        before = att_ref[base, :].astype(F32)
        att_ref[base, :] = jnp.where(row_in, attended[index], before).astype(BF16)


def attention_backward(windows, qkv, d_att, probs_ref, d_bias_ref, d_qkv):
    masks = head_masks()
    size = GROUP * SPAN
    ones = same_head(size, size)
    groups = range(d_att.shape[1] // LANES)
    factor = HD**-0.5

    def part_of(array, group, width):
        return array[:, group * width : (group + 1) * width]

    states = []
    for window in windows:
        base = pl.ds(pl.multiple_of(window * (TOK - 1), 16), SPAN)
        query, key, value = (qkv[part, base, :] for part in range(3))
        states.append((base, query, key, value, d_att[base, :], probs_ref[window]))
    d_bias = d_bias_ref[...]

    weighted = [
        [
            dot_cols(
                part_of(upstream, group, LANES),
                spread_heads(part_of(value, group, LANES), masks),
            )
            * part_of(probs, group, size).astype(F32)
            for group in groups
        ]
        for _, _, _, value, upstream, probs in states
    ]
    deltas = [[dot(values.astype(BF16), ones) for values in row] for row in weighted]
    d_logits = [
        [
            (
                weighted[index][group]
                - part_of(state[5], group, size).astype(F32) * deltas[index][group]
            ).astype(BF16)
            for group in groups
        ]
        for index, state in enumerate(states)
    ]
    for row in d_logits:
        d_bias = pltpu.roll(pltpu.roll(d_bias, SPAN - 1, 0), d_bias.shape[1] - 1, 1)
        d_bias = d_bias + jnp.concatenate([values.astype(F32) for values in row], axis=1)
    d_bias_ref[...] = d_bias
    results = []
    for index, (base, query, key, value, upstream, probs) in enumerate(states):
        row = d_logits[index]
        d_query = [
            dot(row[group], spread_heads(part_of(key, group, LANES), masks)) * factor
            for group in groups
        ]
        d_key = [
            pick_heads(dot_rows(row[group], part_of(query, group, LANES))) * factor
            for group in groups
        ]
        d_value = [
            pick_heads(dot_rows(part_of(probs, group, size), part_of(upstream, group, LANES)))
            for group in groups
        ]
        results.append([jnp.concatenate(values, axis=1) for values in (d_query, d_key, d_value)])
    for index, window in enumerate(windows):
        base = states[index][0]
        row_index = iota((SPAN, 1), 0) - window
        row_in = (row_index >= 0) & (row_index < TOK)
        for part in range(3):
            old = d_qkv[part, base, :].astype(F32)
            d_qkv[part, base, :] = jnp.where(row_in, results[index][part], old).astype(BF16)


def sum_rows(values):
    return jnp.sum(values, 0, keepdims=True)


class Local:
    def __init__(self, refs, first_window):
        self.__dict__.update(refs)
        self.first_window = first_window
        self.rows, self.wide = self.x.shape
        self.width = self.section.shape[1]
        self.units = self.hidden.shape[1]
        self.windows = self.rows // TOK
        self.heads = self.width // HD
        self.chunk = self.rows
        self.steps = self.rows // self.chunk
        self.tile = self.units // self.gu.shape[0]

    def gain(self, row, lanes):
        return self.gains[row : row + 1, :lanes]

    def stat(self, at, index):
        return self.stats[at, index : index + 1]

    def keep_stats(self, at, index, mean, inv):
        self.stats[at, index : index + 1] = mean
        self.stats[at, index + 1 : index + 2] = inv

    def tiles(self):
        return [lax.axis_index("tp") ^ bits for bits in (3, 2, 1, 0)]

    def begin(self):
        for copy in self.arriving:
            copy.wait()
        self.early[...] = jnp.zeros_like(self.early)
        self.spread_vectors()

    def spread_vectors(self):
        for row, ref in enumerate(self.vectors):
            values = ref[...].astype(F32)
            for block in range(values.shape[0]):
                lanes = slice(block * LANES, (block + 1) * LANES)
                self.gains[row : row + 1, lanes] = values[block : block + 1]

    def prepare(self):
        def keep_rows(window):
            base = pl.ds(pl.multiple_of(window * (TOK - 1), 16), SPAN)
            index = iota((SPAN, 1), 0) - window
            inside = (index >= 0) & (index < TOK)
            valid = self.valid[self.first_window + window].astype(F32)
            self.stats[base, 6:7] = jnp.where(inside, valid, self.stats[base, 6:7])

        each(self.windows, keep_rows)

    def table_bias(self):
        build_bias(self.table(), self.spread, self.bias)

    def merge_norm(self):
        gain, shift = self.gain(0, self.wide), self.gain(1, self.wide)

        def step(index):
            at = rows_at(index, self.chunk)
            normed, mean, inv = norm_rows(self.x[at, :].astype(F32))
            self.merged[at, :] = (normed * gain + shift).astype(BF16)
            self.keep_stats(at, 0, mean, inv)

        each(self.steps, step)

    def merge(self):
        self.section[...] = dot(self.merged[...], self.wm[...]).astype(BF16)

    def attn_norm(self):
        gain, shift = self.gain(2, self.width), self.gain(3, self.width)

        def step(index):
            at = rows_at(index, self.chunk)
            normed, mean, inv = norm_rows(self.section[at, :].astype(F32))
            self.attn_in[at, :] = (normed * gain + shift).astype(BF16)
            self.keep_stats(at, 2, mean, inv)

        each(self.steps, step)

    def project(self, part):
        product = dot(self.attn_in[...], self.wqkv[part])
        if part != 1:
            product = product + self.qkv_bias(part)
        self.qkv[part] = product.astype(BF16)

    def attend(self, first, last, together=4):
        def step(index):
            window = first + index * together
            edges = [self.edge[self.first_window + window + more] for more in range(together)]
            attention_forward(window, edges, self.qkv, self.bias, self.probs, self.att)

        each((last - first) // together, step)

    def attn_out(self):
        self.pre[...] = dot(self.att[...], self.wp[...])

    def mlp_norm(self):
        gain, shift = self.gain(4, self.width), self.gain(5, self.width)
        proj_bias = self.gain(6, self.width)

        def step(index):
            at = rows_at(index, self.chunk)
            total = self.section[at, :].astype(F32) + self.pre[at, :] + proj_bias
            self.resid[at, :] = total
            normed, mean, inv = norm_rows(total)
            self.mlp_in[at, :] = (normed * gain + shift).astype(BF16)
            self.keep_stats(at, 4, mean, inv)

        each(self.steps, step)

    def up(self, index):
        columns = rows_at(index, self.tile)
        self.pre[...] = dot(self.mlp_in[...], self.wu[:, columns])
        shift = self.up_bias(index)

        def activate(step):
            at = rows_at(step, self.rows // 7)
            value, rate = gelu_both(self.pre[at, :] + shift)
            self.hidden[at, columns] = value.astype(BF16)
            self.slope[at, columns] = rate.astype(BF16)

        each(7, activate)
        put_blocks(self.gd, index, dot_rows(self.hidden[:, columns], self.d_mlp[...]))

    def down(self):
        self.pre[...] = dot(self.hidden[...], self.wd[...])

    def grad_rows(self):
        def step(index, total):
            at = rows_at(index, self.chunk)
            grad = self.grad_out[at, :].astype(F32) * self.stat(at, 6)
            self.d_mlp[at, :] = grad.astype(BF16)
            return total + fold(grad)

        total = lax.fori_loop(
            0, self.steps, step, jnp.zeros((8, self.width), F32)
        )
        self.put_sum(7, total)

    def finish(self):
        down_bias = self.gain(7, self.width)

        def step(index):
            at = rows_at(index, self.chunk)
            block = (self.resid[at, :] + self.pre[at, :] + down_bias) * self.stat(at, 6)
            self.out[at, :] = block.astype(BF16)

        each(self.steps, step)

    def hidden_back(self, index):
        columns = rows_at(index, self.tile)
        slope = self.slope[:, columns].astype(F32)
        grad = (dot_cols(self.d_mlp[...], self.wd[columns, :]) * slope).astype(BF16)
        self.d_pre[:, columns] = grad
        self.put_up_sum(index, fold(grad.astype(F32)))
        put_blocks(self.gu, index, dot_rows(self.mlp_in[...], grad))

    def hidden_back_pair(self):
        each(2, lambda index: self.hidden_back(lax.axis_index("tp") ^ (2 - index)))

    def up_back(self):
        self.pre[...] = dot_cols(self.d_pre[...], self.wu[...])

    def mlp_back(self):
        gain = self.gain(4, self.width)

        def step(index, totals):
            at = rows_at(index, self.chunk)
            inv = self.stat(at, 5)
            normed = (self.resid[at, :] - self.stat(at, 4)) * inv
            upstream = self.pre[at, :]
            d_resid = self.d_mlp[at, :].astype(F32) + norm_back(upstream, normed, inv, gain)
            self.d_resid[at, :] = d_resid
            self.d_attn[at, :] = d_resid.astype(BF16)
            return (
                totals[0] + fold(upstream * normed),
                totals[1] + fold(upstream),
                totals[2] + fold(d_resid),
            )

        blank = jnp.zeros((8, self.width), F32)
        totals = lax.fori_loop(0, self.steps, step, (blank, blank, blank))
        for row, total in zip((5, 6, 4), totals):
            self.put_sum(row, total)

    def proj_back(self):
        size = self.width // self.gp.shape[0]
        product = dot_rows(self.att[...], self.d_attn[...])
        for index in range(self.gp.shape[0]):
            put_blocks(self.gp, index, product[index * size : (index + 1) * size])
        self.att[...] = dot_cols(self.d_attn[...], self.wp[...]).astype(BF16)
        self.d_bias[...] = jnp.zeros_like(self.d_bias)

    def attend_back(self, first, last, together=2):
        def step(index):
            top = last - 1 - index * together
            windows = [top - less for less in range(together)]
            attention_backward(windows, self.qkv, self.att, self.probs, self.d_bias, self.qkv)

        each((last - first) // together, step)

    def bias_back(self):
        self.put_table(reduce_bias(self.d_bias, self.spread, self.heads))
        ones = jnp.full((8, self.rows), 1.0, BF16)
        self.put_sum(8, dot(ones, self.qkv[0]), True)
        self.put_sum(9, dot(ones, self.qkv[2]), True)

    def qkv_weight_back(self):
        for part in range(3):
            put_columns(self.gqkv, part, dot_rows(self.attn_in[...], self.qkv[part]))

    def qkv_back(self):
        self.pre[...] = (
            dot_cols(self.qkv[0], self.wqkv[0])
            + dot_cols(self.qkv[1], self.wqkv[1])
            + dot_cols(self.qkv[2], self.wqkv[2])
        )

    def attn_back(self):
        gain = self.gain(2, self.width)

        def step(index, totals):
            at = rows_at(index, self.chunk)
            inv = self.stat(at, 3)
            normed = (self.section[at, :].astype(F32) - self.stat(at, 2)) * inv
            upstream = self.pre[at, :]
            d_section = self.d_resid[at, :] + norm_back(upstream, normed, inv, gain)
            self.d_mlp[at, :] = d_section.astype(BF16)
            return totals[0] + fold(upstream * normed), totals[1] + fold(upstream)

        blank = jnp.zeros((8, self.width), F32)
        totals = lax.fori_loop(0, self.steps, step, (blank, blank))
        self.put_sum(2, totals[0])
        self.put_sum(3, totals[1])

    def merge_weight_back(self):
        put_columns(self.gm, 0, dot_rows(self.merged[...], self.d_mlp[...]))

    def merge_in_back(self):
        for half, ref in enumerate((self.pre, self.d_resid)):
            rows = slice(half * self.width, (half + 1) * self.width)
            ref[...] = dot_cols(self.d_mlp[...], self.wm[rows, :])

    def merge_back(self, first, last, totals=None):
        gain = self.gain(0, self.wide)

        def step(index, totals):
            at = pl.ds(first * 16, (last - first) * 16)
            inv = self.stat(at, 1)
            normed = (self.x[at, :].astype(F32) - self.stat(at, 0)) * inv
            upstream = jnp.concatenate([self.pre[at, :], self.d_resid[at, :]], axis=1)
            self.d_in[at, :] = norm_back(upstream, normed, inv, gain)
            return totals[0] + fold(upstream * normed), totals[1] + fold(upstream)

        blank = jnp.zeros((8, self.wide), F32)
        totals = step(0, totals or (blank, blank))
        if last == self.rows // 16:
            self.put_sum(0, totals[0])
            self.put_sum(1, totals[1])
        return totals

    def put_sum(self, row, values, summed=False):
        values = values[0:1] if summed else sum_rows(values)
        place, ref = SUM_ROWS[row], self.late
        if place >= LATE_ROWS:
            place, ref = place - LATE_ROWS, self.early
        for block in range(values.shape[1] // LANES):
            lanes = slice(block * LANES, (block + 1) * LANES)
            ref[place + block : place + block + 1, :] = values[:, lanes]

    def put_up_sum(self, index, total):
        values = sum_rows(total)
        blocks = self.tile // LANES
        for block in range(blocks):
            place = SUM_ROWS[10] - LATE_ROWS + index * blocks + block
            self.early[pl.ds(place, 1), :] = values[:, block * LANES : (block + 1) * LANES]

    def put_table(self, values):
        for half in range(2):
            place = SUM_ROWS[11] - LATE_ROWS + half * self.heads
            lanes = slice(half * LANES, (half + 1) * LANES)
            self.early[place : place + self.heads, :] = values[:, lanes]


SUM_ROWS = (0, 8, 16, 20, 24, 28, 32, 36, 40, 44, 48, 64)
LATE_ROWS = 16
SUM_SIZE = 96


def put_blocks(ref, shard, values):
    rows = values.shape[0]
    for block in range(values.shape[1] // LANES):
        at = pl.ds(block * rows, rows)
        ref[shard, at, :] = values[:, block * LANES : (block + 1) * LANES].astype(BF16)


def put_columns(ref, part, values):
    rows = values.shape[0]
    for shard in range(ref.shape[0]):
        piece = values[:, shard * LANES : (shard + 1) * LANES]
        ref[shard, part * rows : (part + 1) * rows, :] = piece.astype(BF16)


def local_scratch(rows, wide, width, units):
    heads = width // HD
    windows = rows // TOK
    return dict(
        merged=pltpu.VMEM((rows, wide), BF16),
        section=pltpu.VMEM((rows, width), BF16),
        attn_in=pltpu.VMEM((rows, width), BF16),
        qkv=pltpu.VMEM((3, rows, width), BF16),
        probs=pltpu.VMEM((windows, SPAN, heads * SPAN), BF16),
        att=pltpu.VMEM((rows, width), BF16),
        resid=pltpu.VMEM((rows, width), F32),
        mlp_in=pltpu.VMEM((rows, width), BF16),
        hidden=pltpu.VMEM((rows, units), BF16),
        slope=pltpu.VMEM((rows, units), BF16),
        pre=pltpu.VMEM((rows, width), F32),
        d_mlp=pltpu.VMEM((rows, width), BF16),
        d_pre=pltpu.VMEM((rows, units), BF16),
        d_attn=pltpu.VMEM((rows, width), BF16),
        d_resid=pltpu.VMEM((rows, width), F32),
        gains=pltpu.VMEM((8, wide), F32),
        stats=pltpu.VMEM((rows, 8), F32),
        bias=pltpu.VMEM((SPAN, heads * SPAN), F32),
        d_bias=pltpu.VMEM((SPAN, heads * SPAN), F32),
        spread=pltpu.VMEM((SPAN * heads, LANES), F32),
    )


MESH_ID = pl.DeviceIdType.MESH


class Links:
    def __init__(self, send_sems, recv_sems):
        self.send_sems, self.recv_sems = send_sems, recv_sems
        self.slots, self.sent = {}, []
        self.sp, self.tp = lax.axis_index("sp"), lax.axis_index("tp")

    def slot(self, label):
        return self.slots.setdefault(label, len(self.slots))

    def place(self, way):
        over_tp, distance = way
        if over_tp:
            return self.sp, self.tp ^ distance
        return self.sp ^ distance, self.tp

    def copy(self, label, way, source, target):
        slot = self.slot(label)
        return pltpu.make_async_remote_copy(
            src_ref=source,
            dst_ref=target,
            send_sem=self.send_sems.at[slot],
            recv_sem=self.recv_sems.at[slot],
            device_id=self.place(way),
            device_id_type=MESH_ID,
        )

    def send(self, label, way, source, target):
        copy = self.copy(label, way, source, target)
        copy.start()
        self.sent.append(copy)

    def receive(self, label, way, target):
        self.copy(label, way, target, target).wait_recv()

    def keep(self, label, source, target):
        copy = pltpu.make_async_copy(source, target, self.recv_sems.at[self.slot(label)])
        copy.start()
        return copy

    def greet(self, ways):
        barrier = pltpu.get_barrier_semaphore()
        for way in ways:
            pl.semaphore_signal(
                barrier, inc=1, device_id=self.place(way), device_id_type=MESH_ID
            )
        pl.semaphore_wait(barrier, len(ways))

    def drain(self):
        for copy in self.sent:
            copy.wait_send()


CORE, ACROSS, BESIDE = (True, 1), (True, 2), (False, 1)


def far(step):
    return False, 2 * step


class Gather:
    def __init__(self, links, label, own, whole, view, split=True):
        self.links, self.name, self.own, self.whole = links, label, own, whole
        self.view, self.split = view, split
        self.half = links.sp & 1 if split else None

    def part(self, shard, half=None):
        return self.view(self.whole, shard, half)

    def label(self, step):
        return self.name, step

    def start(self):
        links = self.links
        mine = links.tp
        source = self.view(self.own, None, None)
        self.local = links.keep(self.label(0), source, self.part(mine))
        links.send(
            self.label(1), ACROSS, self.view(self.own, None, self.half),
            self.part(mine, self.half),
        )
        links.send(self.label(2), CORE, source, self.part(mine))

    def forward(self):
        links = self.links
        block = self.part(links.tp ^ 2, self.half)
        links.receive(self.label(1), ACROSS, block)
        if self.split:
            links.send(self.label(3), BESIDE, block, block)
        links.send(self.label(4), CORE, block, block)

    def beside(self):
        links = self.links
        block = self.part(links.tp ^ 2, 1 - self.half)
        links.receive(self.label(3), BESIDE, block)
        links.send(self.label(5), CORE, block, block)

    def finish(self):
        links = self.links
        self.local.wait()
        links.receive(self.label(2), CORE, self.part(links.tp ^ 1))
        links.receive(self.label(4), CORE, self.part(links.tp ^ 3, self.half))
        if self.split:
            links.receive(self.label(5), CORE, self.part(links.tp ^ 3, 1 - self.half))


def column_view(size, first, rows):
    def view(ref, shard, half):
        start, count = (first, rows) if half is None else (first + half * (rows // 2), rows // 2)
        at = pl.ds(start if half is None else pl.multiple_of(start, 16), count)
        if shard is None:
            return ref.at[at, :]
        return ref.at[at, pl.ds(pl.multiple_of(shard * size, LANES), size)]

    return view


def row_view(size, first, rows):
    def view(ref, shard, half):
        start = first if shard is None else shard * size + first
        if half is None:
            return ref.at[pl.ds(start if shard is None else pl.multiple_of(start, 16), rows), :]
        return ref.at[pl.ds(pl.multiple_of(start + half * (rows // 2), 16), rows // 2), :]

    return view


def lead_view(ref, shard, half):
    return ref if shard is None else ref.at[shard]


def add_rows(target, start, rows, terms, chunk=512):
    chunk = math.gcd(rows, chunk)

    def step(index):
        offset = index * chunk

        def at(first):
            return pl.ds(pl.multiple_of(first + offset, 16), chunk)

        total = None
        for ref, first in terms:
            value = ref[at(first), :].astype(F32)
            total = value if total is None else total + value
        target[at(start), :] = total.astype(target.dtype)

    each(rows // chunk, step)


class Reduce:
    def __init__(self, links, label, grads, core_in, first_in, second_in, far_in, result, group,
                 across_first):
        self.links, self.name, self.grads = links, label, grads
        self.core_in, self.first_in, self.second_in = core_in, first_in, second_in
        self.far_in, self.result, self.group = far_in, result, group
        self.rows = grads.shape[1]
        self.half_rows = self.rows // 2
        self.piece = self.half_rows // group
        self.half = links.sp & 1
        self.seat = links.sp >> 1
        self.across = links.tp >> 1
        if across_first:
            self.add, self.first = self.core_add_across, self.across_beside
            self.second = self.beside_last
        else:
            self.add, self.first = self.core_add_beside, self.beside_across
            self.second = self.across_last

    def label(self, *step):
        return (self.name,) + step

    def rows_of(self, ref, half, piece=None):
        if piece is None:
            return ref.at[pl.ds(pl.multiple_of(half * self.half_rows, 16), self.half_rows), :]
        start = half * self.half_rows + piece * self.piece
        return ref.at[pl.ds(pl.multiple_of(start, 16), self.piece), :]

    def core_send(self, across, step):
        shard = (self.links.tp & 1) ^ 1 | 2 * across
        self.links.send(
            self.label(step), CORE, self.grads.at[shard], self.core_in.at[across]
        )

    def far(self):
        self.core_send(self.across ^ 1, 0)

    def near(self):
        self.core_send(self.across, 1)

    def receive_far(self):
        self.links.receive(self.label(0), CORE, self.core_in.at[self.across ^ 1])

    def receive_near(self):
        self.links.receive(self.label(1), CORE, self.core_in.at[self.across])

    def core_add_across(self):
        self.receive_far()
        other = self.links.tp ^ 2
        block = self.grads.at[other]
        add_rows(block, 0, self.rows, [(block, 0), (self.core_in.at[self.across ^ 1], 0)])
        self.links.send(self.label(2), ACROSS, block, self.first_in)

    def across_beside(self):
        links = self.links
        self.receive_near()
        links.receive(self.label(2), ACROSS, self.first_in)
        block = self.grads.at[links.tp]
        terms = [(block, 0), (self.core_in.at[self.across], 0), (self.first_in, 0)]
        add_rows(block, 0, self.rows, terms)
        links.send(
            self.label(3), BESIDE, self.rows_of(block, 1 - self.half), self.second_in
        )

    def beside_last(self):
        self.links.receive(self.label(3), BESIDE, self.second_in)
        self.add_and_spread([(self.second_in, 0)])

    def core_add_beside(self):
        links = self.links
        self.receive_far()
        self.receive_near()
        for across in range(2):
            block = self.grads.at[(links.tp & 1) | 2 * across]
            add_rows(block, 0, self.rows, [(block, 0), (self.core_in.at[across], 0)])
            links.send(
                self.label(3, across), BESIDE, self.rows_of(block, 1 - self.half),
                self.first_in.at[across],
            )

    def beside_across(self):
        links = self.links
        for across in range(2):
            links.receive(self.label(3, across), BESIDE, self.first_in.at[across])
        block = self.grads.at[links.tp ^ 2]
        mine = self.half * self.half_rows
        terms = [(block, mine), (self.first_in.at[self.across ^ 1], 0)]
        add_rows(block, mine, self.half_rows, terms)
        links.send(self.label(2), ACROSS, self.rows_of(block, self.half), self.second_in)

    def across_last(self):
        self.links.receive(self.label(2), ACROSS, self.second_in)
        self.add_and_spread([(self.first_in.at[self.across], 0), (self.second_in, 0)])

    def add_and_spread(self, terms):
        block = self.grads.at[self.links.tp]
        mine = self.half * self.half_rows
        add_rows(block, mine, self.half_rows, [(block, mine)] + terms)
        for step in range(1, self.group):
            self.links.send(
                self.label(4, step), far(step),
                self.rows_of(block, self.half, self.seat ^ step), self.far_in.at[step - 1],
            )

    def spread(self):
        links = self.links
        block = self.grads.at[links.tp]
        mine = self.half * self.half_rows + self.seat * self.piece
        terms = [(block, mine)]
        for step in range(1, self.group):
            links.receive(self.label(4, step), far(step), self.far_in.at[step - 1])
            terms.append((self.far_in.at[step - 1], 0))
        add_rows(self.result, mine, self.piece, terms)
        done = self.rows_of(self.result, self.half, self.seat)
        for step in range(1, self.group):
            links.send(self.label(5, step), far(step), done, done)

    def back(self):
        links = self.links
        for step in range(1, self.group):
            links.receive(
                self.label(5, step), far(step),
                self.rows_of(self.result, self.half, self.seat ^ step),
            )
        done = self.rows_of(self.result, self.half)
        links.send(self.label(6), BESIDE, done, done)

    def last(self):
        self.links.receive(
            self.label(6), BESIDE, self.rows_of(self.result, 1 - self.half)
        )


class Total:
    def __init__(self, links, label, stages, inboxes, seats, result):
        self.links, self.name, self.stages, self.inboxes = links, label, stages, inboxes
        self.seats, self.result = seats, result
        self.group = seats.shape[0]
        self.seat = links.sp >> 1

    def exchange(self, stage, way):
        self.links.send((self.name, stage), way, self.stages.at[stage], self.inboxes.at[stage])

    def take(self, stage, way):
        self.links.receive((self.name, stage), way, self.inboxes.at[stage])
        return self.stages[stage] + self.inboxes[stage]

    def send(self):
        self.exchange(0, CORE)

    def core(self):
        self.stages[1] = self.take(0, CORE)
        self.exchange(1, ACROSS)

    def across(self):
        self.stages[2] = self.take(1, ACROSS)
        self.exchange(2, BESIDE)

    def beside(self):
        mine = self.seats.at[self.seat]
        mine[...] = self.take(2, BESIDE)
        for step in range(1, self.group):
            self.links.send((self.name, 3, step), far(step), mine, mine)

    def last(self):
        for step in range(1, self.group):
            self.links.receive((self.name, 3, step), far(step), self.seats.at[self.seat ^ step])
        total = self.seats[0]
        for seat in range(1, self.group):
            total = total + self.seats[seat]
        self.result[...] = total


def schedule(local, g, u, done):
    windows = local.windows
    tiles = local.tiles()

    def attend_back(first, last):
        local.attend_back(windows - last * windows // 8, windows - first * windows // 8)

    local.begin()
    local.merge_norm()
    local.prepare()
    local.grad_rows()
    g.pack.forward()
    g.wm0.forward()
    g.wm1.forward()
    g.wq.forward()
    g.wm0.beside()
    g.wk.forward()
    g.wm0.finish()
    g.wm1.beside()
    g.wv.forward()
    g.wm1.finish()
    local.merge()
    g.wq.beside()
    g.wp.forward()
    g.pack.finish()
    local.table_bias()
    g.wk.beside()
    g.wu0.forward()
    local.attn_norm()
    g.wv.beside()
    g.wq.finish()
    local.project(0)
    g.wu1.forward()
    g.wk.finish()
    local.project(1)
    g.wv.finish()
    local.project(2)
    g.wp.beside()
    g.wu2.forward()
    local.attend(0, windows // 4)
    g.wu0.beside()
    g.wu3.forward()
    local.attend(windows // 4, windows // 2)
    g.wu1.beside()
    local.attend(windows // 2, 3 * windows // 4)
    g.wu2.beside()
    g.wd0.forward()
    local.attend(3 * windows // 4, windows)
    g.wu3.beside()
    g.wp.finish()
    local.attn_out()
    g.wd1.forward()
    local.mlp_norm()
    g.wu0.finish()
    g.wu1.finish()
    g.wu2.finish()
    g.wu3.finish()
    local.up(tiles[0])
    g.wd0.beside()
    u.gd0.far()
    u.gd1.far()
    local.up(tiles[1])
    g.wd1.beside()
    u.gd0.add()
    local.up(tiles[2])
    u.gd0.near()
    u.gd1.near()
    local.up(tiles[3])
    u.gd1.add()
    g.wd0.finish()
    g.wd1.finish()
    local.hidden_back(tiles[0])
    u.gu0.far()
    u.gu1.far()
    local.hidden_back_pair()
    u.gd0.first()
    u.gu0.add()
    u.gu1.add()
    u.gu0.near()
    u.gu1.near()
    local.hidden_back(tiles[3])
    local.up_back()
    u.gd1.first()
    local.mlp_back()
    local.proj_back()
    u.gd0.second()
    u.gu0.first()
    u.gp0.far()
    u.gp0.near()
    attend_back(0, 2)
    u.gp0.add()
    attend_back(2, 4)
    attend_back(4, 6)
    u.gu0.second()
    u.gu1.first()
    u.gd0.spread()
    attend_back(6, 8)
    u.gp0.first()
    u.gd1.second()
    local.qkv_weight_back()
    u.qkv0.far()
    u.qkv0.near()
    u.qkv1.far()
    u.qkv1.near()
    u.qkv2.far()
    u.qkv2.near()
    local.qkv_back()
    u.gp0.second()
    u.gu1.second()
    u.qkv0.add()
    u.qkv1.add()
    u.gu0.spread()
    u.qkv2.add()
    local.attn_back()
    local.merge_weight_back()
    u.gd0.back()
    u.gm0.far()
    u.gm0.near()
    u.gm1.far()
    u.gm1.near()
    local.down()
    u.gd1.spread()
    u.gm0.add()
    u.qkv1.first()
    u.qkv0.first()
    u.gp0.spread()
    u.gm1.add()
    local.finish()
    done.out()
    local.merge_in_back()
    u.qkv2.first()
    u.gu1.spread()
    part = local.rows // 16 // 7
    totals = local.merge_back(0, 2 * part)
    u.qkv0.second()
    totals = local.merge_back(2 * part, 5 * part, totals)
    local.merge_back(5 * part, 7 * part, totals)
    done.d_in()
    u.late.send()
    u.gm0.first()
    u.gu0.back()
    local.bias_back()
    u.early.send()
    u.qkv1.second()
    u.gm1.first()
    u.late.core()
    u.qkv2.second()
    u.gd1.back()
    u.early.core()
    u.gm0.second()
    u.gp0.back()
    u.gm1.second()
    u.gu1.back()
    u.late.across()
    u.early.across()
    u.qkv0.spread()
    u.qkv1.spread()
    u.qkv2.spread()
    u.gm0.spread()
    u.gm1.spread()
    u.late.beside()
    u.early.beside()
    u.qkv0.back()
    u.qkv1.back()
    u.qkv2.back()
    u.gm0.back()
    u.gm1.back()
    u.gd0.last()
    u.gu0.last()
    u.gd1.last()
    u.gp0.last()
    u.gu1.last()
    u.qkv0.last()
    u.qkv1.last()
    u.late.last()
    u.qkv2.last()
    u.gm0.last()
    u.gm1.last()
    u.early.last()


SHARDS = 4
PIECES = 7


class Refs:
    def __init__(self, names, refs):
        self.__dict__.update(zip(names, refs, strict=True))


UNITS = dict(
    gd0=(0, 1024, True),
    gd1=(1024, 1024, False),
    gu0=(0, 1024, True),
    gu1=(1024, 1024, True),
    gp0=(0, 512, False),
    qkv0=(0, 512, True),
    qkv1=(512, 512, False),
    qkv2=(1024, 512, True),
    gm0=(0, 512, True),
    gm1=(512, 512, False),
)


def fill_pack(pack, rel, qv, ub):
    pack[...] = jnp.zeros_like(pack)
    pack[0 : rel.shape[0], 0:REL] = rel[...].astype(F32)
    pack[4:6, 0:LANES] = qv[...].astype(F32)
    for block in range(ub.shape[0]):
        lanes = slice(block * LANES, (block + 1) * LANES)
        pack[6:7, lanes] = ub[block : block + 1, :].astype(F32)


def gathers_of(links, r):
    wide, here = r.own_wm.shape
    width, tile = r.own_wu.shape
    columns = functools.partial(column_view, here)
    up = functools.partial(column_view, tile)
    down = functools.partial(row_view, tile)
    parts = dict(
        pack=(r.pack, r.packs, lead_view, False),
        wm0=(r.own_wm, r.wm, columns(0, wide // 2)),
        wm1=(r.own_wm, r.wm, columns(wide // 2, wide // 2)),
        wq=(r.own_wqkv.at[0], r.wqkv.at[0], columns(0, width)),
        wk=(r.own_wqkv.at[1], r.wqkv.at[1], columns(0, width)),
        wv=(r.own_wqkv.at[2], r.wqkv.at[2], columns(0, width)),
        wp=(r.own_wp, r.wp, row_view(here, 0, here)),
        wu0=(r.own_wu, r.wu, up(0, width // 4)),
        wu1=(r.own_wu, r.wu, up(width // 4, width // 4)),
        wu2=(r.own_wu, r.wu, up(width // 2, width // 4)),
        wu3=(r.own_wu, r.wu, up(3 * width // 4, width // 4)),
        wd0=(r.own_wd, r.wd, down(0, tile // 2)),
        wd1=(r.own_wd, r.wd, down(tile // 2, tile // 2)),
    )
    made = [Gather(links, label, *part) for label, part in enumerate(parts.values())]
    return Refs(parts, made)


def reduces_of(links, r, boxes, first_label):
    grads = (r.gd, r.gd, r.gu, r.gu, r.gp, r.gqkv, r.gqkv, r.gqkv, r.gm, r.gm)
    results = (r.rd, r.rd, r.ru, r.ru, r.rp, r.rqkv, r.rqkv, r.rqkv, r.rm, r.rm)
    made = []
    for index, (first, size, across_first) in enumerate(UNITS.values()):
        at = pl.ds(first, size)
        group = boxes[index][3].shape[0] + 1
        made.append(
            Reduce(
                links, first_label + index, grads[index].at[:, at, :], *boxes[index],
                results[index].at[at, :], group, across_first,
            )
        )
    return Refs(UNITS, made)


def whole_kernel(names, group, *refs):
    boxes = refs[len(names) :]
    r = Refs(names, refs[: len(names)])
    links = Links(r.send_sems, r.recv_sems)
    arriving = [links.keep((-1, 0), r.h_x, r.x), links.keep((-1, 1), r.h_grad_out, r.grad_out)]
    fill_pack(r.pack, r.rel, r.qv, r.ub)
    links.greet([CORE, ACROSS, BESIDE] + [far(step) for step in range(1, group)])
    g = gathers_of(links, r)
    for gather in vars(g).values():
        gather.start()
    u = reduces_of(links, r, [boxes[4 * unit : 4 * unit + 4] for unit in range(len(UNITS))], 100)
    late, early = pl.ds(0, LATE_ROWS), pl.ds(LATE_ROWS, SUM_SIZE - LATE_ROWS)
    u.late = Total(links, 200, r.late_stages, r.late_in, r.late_seats, r.sums.at[late, :])
    u.early = Total(links, 201, r.early_stages, r.early_in, r.early_seats, r.sums.at[early, :])
    here = r.rel.shape[0]

    def table():
        parts = [r.packs[shard, 0:here, : 2 * LANES] for shard in range(SHARDS)]
        return jnp.concatenate(parts, axis=0)

    def qkv_bias(part):
        row = 4 if part == 0 else 5
        parts = [r.packs[shard, row : row + 1, :LANES] for shard in range(SHARDS)]
        return jnp.concatenate(parts, axis=1)

    def up_bias(index):
        return r.packs[index, 6:7, :]

    vectors = (
        r.merge_gain, r.merge_bias, r.attn_gain, r.attn_bias, r.mlp_gain, r.mlp_bias, r.proj_bias,
        r.down_bias,
    )
    fields = dict(
        vars(r), table=table, qkv_bias=qkv_bias, up_bias=up_bias, vectors=vectors,
        arriving=arriving, early=r.early_stages.at[0], late=r.late_stages.at[0],
    )
    local = Local(fields, links.tp * (r.x.shape[0] // TOK))
    leaving = []

    def put_d_in():
        leaving.append(links.keep((-1, 2), r.d_in, r.h_d_in))

    def put_out():
        leaving.append(links.keep((-1, 3), r.out, r.h_out))

    schedule(local, g, u, Refs(dict(d_in=0, out=0), (put_d_in, put_out)))
    for copy in leaving:
        copy.wait()
    links.drain()


def wide_rows(result, out):
    rows = out.shape[0]
    for block in range(out.shape[1] // LANES):
        lanes = slice(block * LANES, (block + 1) * LANES)
        out[:, lanes] = result[block * rows : (block + 1) * rows, :].astype(F32)


def finish_kernel(names, *refs):
    r = Refs(names, refs)
    tp = lax.axis_index("tp")
    pieces = []
    for source, target, held in ((r.h_d_in, r.o_d_in, r.v_d_in), (r.h_out, r.o_out, r.v_out)):
        size = held.shape[0] // PIECES
        for index in range(PIECES):
            at = pl.ds(index * size, size)
            number = 2 * len(pieces)
            pieces.append(
                (
                    pltpu.make_async_copy(source.at[at], held.at[at], r.sems.at[number]),
                    pltpu.make_async_copy(held.at[at], target.at[at], r.sems.at[number + 1]),
                )
            )
    for incoming, _ in pieces:
        incoming.start()
    vectors = (
        r.o_merge_gain, r.o_merge_bias, r.o_attn_gain, r.o_attn_bias, r.o_proj_bias, r.o_mlp_gain,
        r.o_mlp_bias, r.o_down_bias,
    )
    for row, out in enumerate(vectors):
        out[...] = r.sums[SUM_ROWS[row] : SUM_ROWS[row] + out.shape[0], :]
    for index in range(2):
        r.o_qv[index : index + 1, :] = r.sums[pl.ds(SUM_ROWS[8 + index] + tp, 1), :]
    blocks = r.o_ub.shape[0]
    for index in range(blocks):
        place = pl.ds(SUM_ROWS[10] + tp * blocks + index, 1)
        r.o_ub[index : index + 1, :] = r.sums[place, :]
    mine = r.o_rel.shape[0]
    for index in range(mine):
        first = SUM_ROWS[11] + tp * mine + index
        low, high = r.sums[pl.ds(first, 1), :], r.sums[pl.ds(first + SHARDS * mine, 1), :]
        r.o_rel[index : index + 1, :LANES] = low
        r.o_rel[index : index + 1, LANES:] = high[:, : REL - LANES]
    for incoming, outgoing in pieces:
        incoming.wait()
        outgoing.start()
    for result, out in ((r.rp, r.o_gp), (r.ru, r.o_gu), (r.rd, r.o_gd), (r.rm, r.o_gm)):
        wide_rows(result, out)
    rows = r.o_gqkv.shape[1]
    for part in range(r.o_gqkv.shape[0]):
        r.o_gqkv[part] = r.rqkv[part * rows : (part + 1) * rows, :].astype(F32)
    for _, outgoing in pieces:
        outgoing.wait()


VMEM_SPEC = pl.BlockSpec(memory_space=pltpu.VMEM)
SMEM_SPEC = pl.BlockSpec(memory_space=pltpu.SMEM)
HBM_SPEC = pl.BlockSpec(memory_space=pl.ANY)


def whole_call(group, small, large):
    rows, wide = large["h_x"].shape
    width, tile = large["own_wu"].shape
    units = SHARDS * tile
    scratch = local_scratch(rows, wide, width, units)
    block = lambda *shape: pltpu.VMEM(shape, BF16)
    exact = lambda *shape: pltpu.VMEM(shape, F32)
    early = SUM_SIZE - LATE_ROWS
    count = 13 * 6 + len(UNITS) * (6 + 2 * group) + 2 * (3 + group) + 4
    scratch.update(
        wm=block(wide, width), wqkv=block(3, width, width), wp=block(width, width),
        wu=block(width, units), wd=block(units, width), pack=exact(8, tile),
        packs=exact(SHARDS, 8, tile), x=block(rows, wide), grad_out=block(rows, width),
        out=block(rows, width), d_in=exact(rows, wide), gd=block(SHARDS, units, LANES),
        gu=block(SHARDS, units, LANES), gp=block(SHARDS, width, LANES),
        gqkv=block(SHARDS, 3 * width, LANES), gm=block(SHARDS, wide, LANES),
        late_stages=exact(3, LATE_ROWS, LANES), late_in=exact(3, LATE_ROWS, LANES),
        late_seats=exact(group, LATE_ROWS, LANES), early_stages=exact(3, early, LANES),
        early_in=exact(3, early, LANES), early_seats=exact(group, early, LANES),
        send_sems=pltpu.SemaphoreType.DMA((count,)), recv_sems=pltpu.SemaphoreType.DMA((count,)),
    )
    boxes = []
    for _, size, across_first in UNITS.values():
        half = size // 2
        boxes += [
            block(2, size, LANES),
            block(size, LANES) if across_first else block(2, half, LANES),
            block(half, LANES),
            block(group - 1, half // group, LANES),
        ]
    result = lambda size: jax.ShapeDtypeStruct((size, LANES), BF16)
    outs = dict(
        h_out=jax.ShapeDtypeStruct((rows, width), BF16),
        h_d_in=jax.ShapeDtypeStruct((rows, wide), F32),
        rd=result(units), ru=result(units), rp=result(width), rqkv=result(3 * width),
        rm=result(wide), sums=jax.ShapeDtypeStruct((SUM_SIZE, LANES), F32),
    )
    names = tuple(small) + tuple(large) + tuple(outs) + tuple(scratch)
    made = pl.pallas_call(
        functools.partial(whole_kernel, names, group),
        out_shape=list(outs.values()),
        in_specs=[SMEM_SPEC] * 2 + [VMEM_SPEC] * (len(small) - 2) + [HBM_SPEC] * len(large),
        out_specs=[HBM_SPEC] * 2 + [VMEM_SPEC] * (len(outs) - 2),
        scratch_shapes=list(scratch.values()) + boxes,
        compiler_params=pltpu.CompilerParams(
            vmem_limit_bytes=63 * MIB, collective_id=0, has_side_effects=True
        ),
    )(*small.values(), *large.values())
    return dict(zip(outs, made, strict=True))


def finish_call(results, shapes):
    (rows, width), (_, wide) = shapes["o_out"].shape, shapes["o_d_in"].shape
    scratch = dict(
        v_out=pltpu.VMEM((rows, width), BF16), v_d_in=pltpu.VMEM((rows, wide), F32),
        sems=pltpu.SemaphoreType.DMA((4 * PIECES,)),
    )
    names = tuple(results) + tuple(shapes) + tuple(scratch)
    made = pl.pallas_call(
        functools.partial(finish_kernel, names),
        out_shape=list(shapes.values()),
        in_specs=[HBM_SPEC] * 2 + [VMEM_SPEC] * (len(results) - 2),
        out_specs=[HBM_SPEC] * 2 + [VMEM_SPEC] * (len(shapes) - 2),
        scratch_shapes=list(scratch.values()),
        compiler_params=pltpu.CompilerParams(vmem_limit_bytes=63 * MIB),
    )(*results.values())
    return Refs(shapes, made)


def on_device(
    inputs, grad_out, window_valid, window_edge, merge_gain, merge_bias, merge_weight, attn_gain,
    attn_bias, query_key_value_weight, qv_bias, rel_table, proj_weight, proj_bias, mlp_gain,
    mlp_bias, up_weight, up_bias, down_weight, down_bias,
):
    lines = lambda vector: vector.reshape(-1, LANES)
    small = dict(
        valid=window_valid, edge=window_edge, rel=rel_table.T, qv=qv_bias, ub=lines(up_bias),
        merge_gain=lines(merge_gain), merge_bias=lines(merge_bias), attn_gain=lines(attn_gain),
        attn_bias=lines(attn_bias), mlp_gain=lines(mlp_gain), mlp_bias=lines(mlp_bias),
        proj_bias=lines(proj_bias), down_bias=lines(down_bias),
    )
    qkv = jnp.transpose(query_key_value_weight, (1, 0, 2))
    large = dict(
        h_x=inputs, h_grad_out=grad_out, own_wm=merge_weight, own_wqkv=qkv, own_wp=proj_weight,
        own_wu=up_weight, own_wd=down_weight,
    )
    results = whole_call(lax.axis_size("sp") // 2, small, large)
    like = lambda array: jax.ShapeDtypeStruct(array.shape, F32)
    shapes = dict(
        o_out=jax.ShapeDtypeStruct(grad_out.shape, BF16), o_d_in=like(inputs),
        o_gm=like(merge_weight), o_gqkv=like(qkv), o_gp=like(proj_weight), o_gu=like(up_weight),
        o_gd=like(down_weight), o_qv=like(qv_bias), o_rel=like(rel_table.T),
        o_ub=like(lines(up_bias)), o_merge_gain=like(lines(merge_gain)),
        o_merge_bias=like(lines(merge_bias)), o_attn_gain=like(lines(attn_gain)),
        o_attn_bias=like(lines(attn_bias)), o_proj_bias=like(lines(proj_bias)),
        o_mlp_gain=like(lines(mlp_gain)), o_mlp_bias=like(lines(mlp_bias)),
        o_down_bias=like(lines(down_bias)),
    )
    done = finish_call(results, shapes)
    flat = lambda block: block.reshape(-1)
    return (
        done.o_out, done.o_d_in, flat(done.o_merge_gain), flat(done.o_merge_bias), done.o_gm,
        flat(done.o_attn_gain), flat(done.o_attn_bias), jnp.transpose(done.o_gqkv, (1, 0, 2)),
        done.o_qv, done.o_rel.T, done.o_gp, flat(done.o_proj_bias), flat(done.o_mlp_gain),
        flat(done.o_mlp_bias), done.o_gu, flat(done.o_ub), done.o_gd, flat(done.o_down_bias),
    )


def solution(mesh):
    placed = (
        P(("sp", "tp"), None),
        P(("sp", "tp"), None),
        P("sp"),
        P("sp"),
        P(),
        P(),
        P(None, "tp"),
        P(),
        P(),
        P(None, None, "tp"),
        P(None, "tp"),
        P(None, "tp"),
        P("tp", None),
        P(),
        P(),
        P(),
        P(None, "tp"),
        P("tp"),
        P("tp", None),
        P(),
    )
    return jax.shard_map(
        on_device,
        mesh=mesh,
        in_specs=placed,
        out_specs=(
            P(("sp", "tp"), None),
            P(("sp", "tp"), None),
            P(),
            P(),
            P(None, "tp"),
            P(),
            P(),
            P(None, None, "tp"),
            P(None, "tp"),
            P(None, "tp"),
            P("tp", None),
            P(),
            P(),
            P(),
            P(None, "tp"),
            P("tp"),
            P("tp", None),
            P(),
        ),
        check_vma=False,
    )
```
